128 devices in a mesh: dp: 8 (over x, core), shard: 16 (over y, z).
Axes of the slice: x: 4, y: 4, z: 4, core: 2. Of those that a mesh axis runs over, the one named last changes fastest.
Arguments:
- source: bfloat16 [128, 384, 512], P(('dp', 'shard')), may hold values from -6 to 6
- target: bfloat16 [128, 384, 512], P(('dp', 'shard')), may hold values from -6 to 6
- source_lengths: int32 [128, 5], P(('dp', 'shard')), may hold values from 1 to 192, 384 in all within a row
- target_lengths: int32 [128, 5], P(('dp', 'shard')), may hold values from 1 to 192, 384 in all within a row
- lang_ids: int32 [128, 5], P(('dp', 'shard')), may hold values from 0 to 99
- out_cotangent: bfloat16 [128, 384, 512], P(('dp', 'shard')), may hold values from -6 to 6
- enc_attn: bfloat16 [4, 512, 512], P(None, ('dp', 'shard')), as said below
- enc_vectors: bfloat16 [8, 512], P(None, ('dp', 'shard'))
- enc_w_in: bfloat16 [512, 2048], P(('dp', 'shard')), may hold values from -0.25 to 0.25
- enc_b_in: bfloat16 [2048], P(('dp', 'shard')), may hold values from -4 to 4
- enc_w_out: bfloat16 [2048, 512], P(('dp', 'shard')), may hold values from -0.125 to 0.125
- dec_self: bfloat16 [4, 512, 512], P(None, ('dp', 'shard')), as said below
- dec_cross: bfloat16 [4, 512, 512], P(None, ('dp', 'shard')), as said below
- dec_vectors: bfloat16 [13, 512], P(None, ('dp', 'shard'))
- dec_w_in: bfloat16 [512, 2048], P(('dp', 'shard')), may hold values from -0.25 to 0.25
- dec_b_in: bfloat16 [2048], P(('dp', 'shard')), may hold values from -4 to 4
- dec_w_out: bfloat16 [2048, 512], P(('dp', 'shard')), may hold values from -0.125 to 0.125
- lang_table: bfloat16 [100, 512], P(None, ('dp', 'shard')), may hold values from -6 to 6
Outputs:
- dec_out: bfloat16 [128, 384, 512], P(('dp', 'shard'))
- grad_source: float32 [128, 384, 512], P(('dp', 'shard'))
- grad_target: float32 [128, 384, 512], P(('dp', 'shard'))
- grad_enc_attn: float32 [4, 512, 512], P(None, ('dp', 'shard'))
- grad_enc_vectors: float32 [8, 512], P(None, ('dp', 'shard'))
- grad_enc_w_in: float32 [512, 2048], P(('dp', 'shard'))
- grad_enc_b_in: float32 [2048], P(('dp', 'shard'))
- grad_enc_w_out: float32 [2048, 512], P(('dp', 'shard'))
- grad_dec_self: float32 [4, 512, 512], P(None, ('dp', 'shard'))
- grad_dec_cross: float32 [4, 512, 512], P(None, ('dp', 'shard'))
- grad_dec_vectors: float32 [13, 512], P(None, ('dp', 'shard'))
- grad_dec_w_in: float32 [512, 2048], P(('dp', 'shard'))
- grad_dec_b_in: float32 [2048], P(('dp', 'shard'))
- grad_dec_w_out: float32 [2048, 512], P(('dp', 'shard'))
- grad_lang_table: float32 [100, 512], P(None, ('dp', 'shard'))
The draws below stay inside these ranges and needn't reach their ends.
Inputs may be any that keep to these rules, and one draw needn't show every extreme that they name: `source_lengths`: each row's entries sum to 384; the first 4 are document lengths, the last is the row's padding; some entry equals 192. `target_lengths`: as for source_lengths, drawn independently. `enc_attn`: projection matrices stacked as query, key, value, output. `dec_self`: projection matrices stacked as query, key, value, output. `dec_cross`: projection matrices stacked as query, key, value, output.
All inputs are finite; a program needn't handle non-finite values.
Results may differ from the reference program's by a relative error of at most 0.022.
Values may be sent and summed in bfloat16 or wider, within the bound.
No kernel may reach another device: no remote copies, remote signals or barrier semaphores. Data moves between devices by JAX's collectives and lax.ppermute only.
A program may use at most 192 MiB of HBM per device.

```python
import math
import jax
import jax.numpy as jnp
import numpy as np
from jax import lax

D = 512
HEADS = 8
HEAD_DIM = 64
FF = 2048
LANGS = 100
SEQ = 384
DOCS = 5
ROWS = 128


def attn_stack(key):
    base = jax.random.normal(key, (4, D, D), jnp.float32)
    factor = jnp.array([1.0, 1.0, 1.0, 3.0], jnp.float32) * D ** (-0.5)
    return (base * factor[:, None, None]).astype(jnp.bfloat16)


def vector_rows(key, gain_rows):
    count = gain_rows.shape[0]
    key_gain, key_shift = jax.random.split(key)
    gains = 1.0 + 0.25 * jax.random.uniform(key_gain, (count, D), jnp.float32, -1.0, 1.0)
    shifts = 0.2 * jax.random.normal(key_shift, (count, D), jnp.float32)
    chosen = gain_rows[:, None]
    return (chosen * gains + (1.0 - chosen) * shifts).astype(jnp.bfloat16)


def draw_enc_attn(key, part):
    key = jax.random.fold_in(key, 11)
    return attn_stack(key)


def draw_dec_self(key, part):
    key = jax.random.fold_in(key, 12)
    return attn_stack(key)


def draw_dec_cross(key, part):
    key = jax.random.fold_in(key, 13)
    return attn_stack(key)


def draw_enc_vectors(key, part):
    key = jax.random.fold_in(key, 14)
    return vector_rows(key, jnp.array([1, 0, 0, 0, 0, 1, 0, 0], jnp.float32))


def draw_dec_vectors(key, part):
    key = jax.random.fold_in(key, 15)
    return vector_rows(key, jnp.array([1, 0, 0, 0, 0, 1, 0, 0, 0, 0, 1, 0, 0], jnp.float32))


def set_ends(result, rng, least, largest):
    longest = result.shape.index(max(result.shape))
    spots = []
    for shift in (0, 1):
        where = [jax.random.randint(jax.random.fold_in(rng, axis), (), 0, length) for axis, length in enumerate(result.shape)]
        where[longest] = (where[longest] + shift) % result.shape[longest]
        spots.append(tuple(where))
    return result.at[spots[0]].set(least).at[spots[1]].set(largest)


def shard_levels(own_key, dims, shards, low, largest):
    level, own = 1.0, jax.random.fold_in(own_key, 6)
    for axis_at, blocks in shards:
        steps = jnp.exp(jax.random.uniform(jax.random.fold_in(own, axis_at), (blocks,), jnp.float32, low / len(shards), largest / len(shards)))
        level = level * jnp.repeat(steps, dims[axis_at] // blocks).reshape([-1 if axis == axis_at else 1 for axis in range(len(dims))])
    return level


def rank_table(amount, slope):
    portions = [(1 << 20) // math.isqrt(grade ** slope) + 1 for grade in range(1, amount + 1)]
    scale = 1 + sum(portions) // (1 << 30)
    return np.cumsum(np.array([max(1, weight // scale) for weight in portions]))


def ranked_ids(stream_key, extent, amount, skew):
    grid = rank_table(amount, skew)
    lot = jax.random.randint(jax.random.fold_in(stream_key, 1), extent, 0, int(grid[amount - 1]))
    standing = jnp.searchsorted(jnp.asarray(grid, jnp.int32), lot, side="right")
    return jax.random.permutation(jax.random.fold_in(stream_key, 2), amount)[standing].astype(jnp.int32)


def profile(count, total, reach, slope):
    portions = [(1 << 20) // math.isqrt(grade ** slope) + 1 for grade in range(2, count + 1)]
    rest, holding = total - reach - (count - 1), [1] * (count - 1)
    while rest > 0:
        free = [i for i in range(count - 1) if holding[i] < reach]
        pool, remaining = sum([portions[i] for i in free]), rest
        for i in free:
            extra = min(reach - holding[i], max(1, remaining * portions[i] // pool), rest)
            holding[i] = holding[i] + extra
            rest = rest - extra
    return np.array([reach] + holding)


def ragged(key, count, total, bound, slope):
    if count == 2:
        one = jax.random.randint(key, (), max(1, total - bound), min(bound, total - 1) + 1)
        return jnp.stack([one, total - one])
    sizes = jnp.asarray(profile(count, total, bound, slope), jnp.int32)
    couples = (count - 1) // 2
    giver, receiver = sizes[1:1 + 2 * couples:2], sizes[2:2 + 2 * couples:2]
    slack = jnp.minimum(giver - 1, bound - receiver)
    passed = jax.random.randint(jax.random.fold_in(key, 1), (couples,), 0, 1 << 20) % (slack + 1)
    sizes = sizes.at[1:1 + 2 * couples:2].set(giver - passed).at[2:2 + 2 * couples:2].set(receiver + passed)
    return sizes[jax.random.permutation(jax.random.fold_in(key, 2), count)]


def normal_values(rng, extent, scale, bound, cuts=(), kind=jnp.bfloat16):
    result = jax.random.normal(rng, extent, jnp.float32) * scale
    if len(cuts) > 0:
        result = shard_levels(rng, extent, cuts, -0.22, 0.18) * result
    return jnp.clip(result, min=-bound, max=bound).astype(kind)


def setup_inputs(seed: int = 0) -> dict:
    streams_of = jax.random.split(jax.random.key(seed), 19)
    return {
        "source": normal_values(streams_of[0], (ROWS, SEQ, D), 1.0, 6.0, ((0, 128),)),
        "target": normal_values(streams_of[1], (ROWS, SEQ, D), 1.0, 6.0, ((0, 128),)),
        "source_lengths": jax.vmap(lambda own: ragged(own, DOCS, SEQ, SEQ // 2, 2))(jax.random.split(streams_of[2], ROWS)).reshape((ROWS, DOCS)).astype(jnp.int32),
        "target_lengths": jax.vmap(lambda own: ragged(own, DOCS, SEQ, SEQ // 2, 2))(jax.random.split(streams_of[3], ROWS)).reshape((ROWS, DOCS)).astype(jnp.int32),
        "lang_ids": set_ends(ranked_ids(streams_of[4], (ROWS, DOCS), LANGS, 2), jax.random.fold_in(streams_of[4], 3), 0, LANGS - 1).astype(jnp.int32),
        "out_cotangent": normal_values(streams_of[5], (ROWS, SEQ, D), 1.0, 6.0, ((0, 128),)),
        "enc_attn": draw_enc_attn(jax.random.fold_in(streams_of[18], 71), 0),
        "enc_vectors": draw_enc_vectors(jax.random.fold_in(streams_of[18], 71), 0),
        "enc_w_in": normal_values(streams_of[8], (D, FF), D ** -0.5, 0.25, ((0, 128),)),
        "enc_b_in": normal_values(streams_of[9], (FF,), 0.3, 4.0, ((0, 128),)),
        "enc_w_out": normal_values(streams_of[10], (FF, D), FF ** -0.5, 0.125, ((0, 128),)),
        "dec_self": draw_dec_self(jax.random.fold_in(streams_of[18], 71), 0),
        "dec_cross": draw_dec_cross(jax.random.fold_in(streams_of[18], 71), 0),
        "dec_vectors": draw_dec_vectors(jax.random.fold_in(streams_of[18], 71), 0),
        "dec_w_in": normal_values(streams_of[14], (D, FF), D ** -0.5, 0.25, ((0, 128),)),
        "dec_b_in": normal_values(streams_of[15], (FF,), 0.3, 4.0, ((0, 128),)),
        "dec_w_out": normal_values(streams_of[16], (FF, D), FF ** -0.5, 0.125, ((0, 128),)),
        "lang_table": normal_values(streams_of[17], (LANGS, D), 0.5, 6.0, ((1, 128),)),
    }


@jax.custom_vjp
def low(v):
    return lax.optimization_barrier(v.astype(jnp.bfloat16)).astype(jnp.float32)

@jax.custom_vjp
def low_back(v):
    return v

def low_keep(v):
    return (low(v), None)

def low_pass(kept, grad):
    return (grad,)

def back_keep(v):
    return (v, None)

def back_low(kept, grad):
    return (low(grad),)
low.defvjp(low_keep, low_pass)
low_back.defvjp(back_keep, back_low)
EPSILON = 1e-05
NEGATIVE = -1000000000.0
HIGHEST = lax.Precision.HIGHEST

def product(left, right):
    return jnp.dot(left, right, precision=HIGHEST, preferred_element_type=jnp.float32)

def layer_norm(values, gain, shift):
    center = values - lax.optimization_barrier(jnp.mean(values, axis=-1, keepdims=True))
    spread = lax.optimization_barrier(jnp.mean(center * center, axis=-1, keepdims=True))
    return center * lax.rsqrt(spread + EPSILON) * gain + shift

def doc_index(lengths):
    ends = jnp.cumsum(lengths)
    positions = jnp.arange(SEQ, dtype=jnp.int32)
    return lax.optimization_barrier(jnp.sum((positions[:, None] >= ends[None, :]).astype(jnp.int32), axis=1))

def attention(query_in, memory, weights, bias_q, bias_v, bias_o, mask):
    scale = HEAD_DIM ** (-0.5)
    query = low(low_back(scale * (product(query_in, weights[0]) + bias_q)))
    keys = low(low_back(product(memory, weights[1])))
    values = low(low_back(product(memory, weights[2]) + bias_v))
    query_heads = query.reshape(SEQ, HEADS, HEAD_DIM)
    key_heads = keys.reshape(SEQ, HEADS, HEAD_DIM)
    value_heads = values.reshape(SEQ, HEADS, HEAD_DIM)
    scores = low_back(jnp.einsum('qhd,khd->hqk', query_heads, key_heads, precision=HIGHEST))
    scores = jnp.where(mask[None], scores, NEGATIVE)
    row_max = lax.optimization_barrier(jnp.max(scores, axis=-1, keepdims=True))
    expd = jnp.exp(scores - row_max)
    attn_probs = low(expd / lax.optimization_barrier(jnp.sum(expd, axis=-1, keepdims=True)))
    context = jnp.einsum('hqk,khd->qhd', attn_probs, value_heads, precision=HIGHEST).reshape(SEQ, D)
    context = low(low_back(context))
    return low_back(product(context, weights[3]) + bias_o)

def feed(inputs, w_in, b_in, w_out, b_out):
    hidden = low_back(product(inputs, w_in) + b_in)
    active = low(jax.nn.silu(hidden))
    return low_back(product(active, w_out) + b_out)

def encode(source_row, params, mask):
    attn, vectors, w_in, b_in, w_out = params
    normed = low(layer_norm(source_row, vectors[0], vectors[1]))
    middle = source_row + attention(normed, normed, attn, vectors[2], vectors[3], vectors[4], mask)
    normed_two = low(layer_norm(middle, vectors[5], vectors[6]))
    return middle + feed(normed_two, w_in, b_in, w_out, vectors[7])

def decode(target_row, memory, params, lang_rows, self_mask, cross_mask):
    self_w, cross_w, vectors, w_in, b_in, w_out, table = params
    start = target_row + table[lang_rows]
    normed = low(layer_norm(start, vectors[0], vectors[1]))
    first = start + attention(normed, normed, self_w, vectors[2], vectors[3], vectors[4], self_mask)
    normed_two = low(layer_norm(first, vectors[5], vectors[6]))
    second = first + attention(normed_two, memory, cross_w, vectors[7], vectors[8], vectors[9], cross_mask)
    normed_three = low(layer_norm(second, vectors[10], vectors[11]))
    return second + feed(normed_three, w_in, b_in, w_out, vectors[12])

def one_row(params, row):
    source_row, target_row, source_len, target_len, langs = row
    source_doc = doc_index(source_len)
    target_doc = doc_index(target_len)
    positions = jnp.arange(SEQ, dtype=jnp.int32)
    enc_mask = source_doc[:, None] == source_doc[None, :]
    self_mask = (target_doc[:, None] == target_doc[None, :]) & (positions[None, :] <= positions[:, None])
    cross_mask = target_doc[:, None] == source_doc[None, :]
    lang_rows = langs[target_doc]
    encoded = encode(source_row, params[0], enc_mask)
    return decode(target_row, low(encoded), params[1], lang_rows, self_mask, cross_mask)

def reference(source, target, source_lengths, target_lengths, lang_ids, out_cotangent, enc_attn, enc_vectors, enc_w_in, enc_b_in, enc_w_out, dec_self, dec_cross, dec_vectors, dec_w_in, dec_b_in, dec_w_out, lang_table):

    def upcast(array):
        return array.astype(jnp.float32)
    params = ((upcast(enc_attn), upcast(enc_vectors), upcast(enc_w_in), upcast(enc_b_in), upcast(enc_w_out)), (upcast(dec_self), upcast(dec_cross), upcast(dec_vectors), upcast(dec_w_in), upcast(dec_b_in), upcast(dec_w_out), upcast(lang_table)))

    def forward(weights, source_all, target_all):
        step = jax.checkpoint(lambda row: one_row(weights, row))
        return lax.map(step, (source_all, target_all, source_lengths, target_lengths, lang_ids))
    outputs, pullback = jax.vjp(forward, params, upcast(source), upcast(target))
    grads, grad_src_all, grad_tgt_all = pullback(upcast(out_cotangent))
    enc_grads, dec_grads = grads
    return (outputs.astype(jnp.bfloat16), grad_src_all, grad_tgt_all, enc_grads[0], enc_grads[1], enc_grads[2], enc_grads[3], enc_grads[4], dec_grads[0], dec_grads[1], dec_grads[2], dec_grads[3], dec_grads[4], dec_grads[5], dec_grads[6])
```

```python
import functools
import itertools

import jax
import jax.numpy as jnp
from jax import lax
from jax.experimental import pallas as pl
from jax.experimental.pallas import tpu as pltpu
from jax.sharding import Mesh
from jax.sharding import PartitionSpec as P

D = 512
HEADS = 8
HEAD_DIM = 64
FF = 2048
LANGS = 100
SEQ = 384
DOCS = 5
EPSILON = 1e-05
NEGATIVE = -1000000000.0
OPEN = 3e38
SCALE = HEAD_DIM ** (-0.5)
AXES = ("x", "c", "y", "z")
SIZES = (4, 2, 4, 4)
BLOCKS = 32
ENC_VEC = 104
DEC_VEC = 112
CHUNK = 128
CHUNKS = SEQ // CHUNK
F32 = jnp.float32
BF16 = jnp.bfloat16


def dot(left, right):
    return lax.dot_general(left, right, (((1,), (0,)), ((), ())), preferred_element_type=F32)


def dot_nt(left, right):
    return lax.dot_general(left, right, (((1,), (1,)), ((), ())), preferred_element_type=F32)


def rows(index, size=CHUNK):
    return slice(index * size, (index + 1) * size)


def normed(values):
    mean = jnp.mean(values, axis=-1, keepdims=True)
    center = values - mean
    rstd = lax.rsqrt(jnp.mean(center * center, axis=-1, keepdims=True) + EPSILON)
    return center * rstd, rstd


def layer_norm(source, gain, shift, out):
    for i in range(CHUNKS):
        hat, _ = normed(source[rows(i), :])
        out[rows(i), :] = (hat * gain + shift).astype(BF16)


def norm_back(source, gain, grad, base, out):
    d_gain = jnp.zeros((1, D), F32)
    d_shift = jnp.zeros((1, D), F32)
    for i in range(CHUNKS):
        hat, rstd = normed(source[rows(i), :])
        dy = grad[rows(i), :]
        d_gain = d_gain + jnp.sum(dy * hat, axis=0, keepdims=True)
        d_shift = d_shift + jnp.sum(dy, axis=0, keepdims=True)
        dyg = dy * gain
        mean_one = jnp.mean(dyg, axis=-1, keepdims=True)
        mean_two = jnp.mean(dyg * hat, axis=-1, keepdims=True)
        out[rows(i), :] = base[rows(i), :].astype(F32) + rstd * (dyg - mean_one - hat * mean_two)
    return d_gain, d_shift


def low_lanes(count):
    return lax.broadcasted_iota(jnp.int32, (count, 128), 1) < HEAD_DIM


def head_mask():
    lane = lax.broadcasted_iota(jnp.int32, (1, D), 1)
    return ((lane // HEAD_DIM) % 2 == 0).astype(F32)


def doc_ids(lengths, shape, axis):
    position = lax.broadcasted_iota(jnp.int32, shape, axis)
    total = jnp.zeros(shape, jnp.int32)
    end = 0
    for i in range(DOCS):
        end = end + lengths[0, i]
        total = total + (position >= end).astype(jnp.int32)
    return total


def masks(s_len, t_len, bias_e, bias_s, bias_c):
    shape = (SEQ, SEQ)
    s_row = doc_ids(s_len, (1, SEQ), 1)
    t_row = doc_ids(t_len, (1, SEQ), 1)
    s_col = doc_ids(s_len, (SEQ, 1), 0)
    t_col = doc_ids(t_len, (SEQ, 1), 0)
    for i in range(CHUNKS):
        shape = (CHUNK, SEQ)
        sc = jnp.broadcast_to(s_col[rows(i), :], shape)
        tc = jnp.broadcast_to(t_col[rows(i), :], shape)
        key = lax.broadcasted_iota(jnp.int32, shape, 1)
        query = lax.broadcasted_iota(jnp.int32, shape, 0) + i * CHUNK
        bias_e[rows(i), :] = jnp.where(sc == s_row, OPEN, NEGATIVE)
        bias_s[rows(i), :] = jnp.where((tc == t_row) & (key <= query), OPEN, NEGATIVE)
        bias_c[rows(i), :] = jnp.where(tc == s_row, OPEN, NEGATIVE)


def lang_onehot(t_len, langs):
    doc = doc_ids(t_len, (SEQ, 128), 0)
    lang = jnp.zeros((SEQ, 128), jnp.int32)
    for i in range(DOCS):
        lang = jnp.where(doc == i, langs[0, i], lang)
    lane = lax.broadcasted_iota(jnp.int32, (SEQ, 128), 1)
    return jnp.where(lang == lane, 1.0, 0.0).astype(BF16)


def attn_project(query_in, memory, weights, bias_q, bias_v, q_even, q_odd, keys, values):
    even = head_mask()
    for i in range(CHUNKS):
        u = query_in[rows(i), :]
        m = memory[rows(i), :]
        q = SCALE * (dot(u, weights[0]) + bias_q)
        q_even[rows(i), :] = (q * even).astype(BF16)
        q_odd[rows(i), :] = (q * (1.0 - even)).astype(BF16)
        keys[rows(i), :] = dot(m, weights[1]).astype(BF16)
        values[rows(i), :] = (dot(m, weights[2]) + bias_v).astype(BF16)


def attn_core(q_even, q_odd, keys, values, bias, probs, context, causal):
    low = low_lanes(CHUNK)
    for pair in range(HEADS // 2):
        lanes = rows(pair, 128)
        for i in range(CHUNKS):
            limit = (i + 1) * CHUNK if causal else SEQ
            parts = []
            for half, query in enumerate((q_even, q_odd)):
                s = dot_nt(query[rows(i), lanes], keys[:limit, lanes])
                s = jnp.minimum(s, bias[rows(i), :limit])
                e = jnp.exp(s - jnp.max(s, axis=-1, keepdims=True))
                p = (e * (1.0 / jnp.sum(e, axis=-1, keepdims=True))).astype(BF16)
                probs[2 * pair + half, rows(i), :limit] = p
                parts.append(dot(p, values[:limit, lanes]))
            context[rows(i), lanes] = jnp.where(low, parts[0], parts[1]).astype(BF16)


def attn_output(context, weight, bias_o, residual, out):
    for i in range(CHUNKS):
        branch = dot(context[rows(i), :], weight[...]) + bias_o
        out[rows(i), :] = residual[rows(i), :].astype(F32) + branch


def put_rows(out, table, unit, first, value):
    for j in range(value.shape[0] // 16):
        out[table[first + j], unit] = value[rows(j, 16), :].astype(BF16)


def weight_grad(left_t, right, out, table, unit, scale=None):
    for i in range(D // CHUNK):
        value = dot(left_t[rows(i), :], right[...])
        if scale is not None:
            value = value * scale
        put_rows(out, table, unit, i * (CHUNK // 16), value)


def column_sum(ref):
    return jnp.sum(ref[...].astype(F32), axis=0, keepdims=True)


def attn_back(grad, query_in_t, memory_t, weights, kept, scratch, out, table, unit, causal):
    q_even, q_odd, keys, values, probs, context = kept
    d_even, d_odd, dc_t, q_t, c_t, ds, dq, dk_t, dv_t, dk, dv, du, dm = scratch
    even = head_mask()
    for i in range(CHUNKS):
        dc = dot_nt(grad[rows(i), :], weights[3])
        d_even[rows(i), :] = (dc * even).astype(BF16)
        d_odd[rows(i), :] = (dc * (1.0 - even)).astype(BF16)
    dc_t[...] = (d_even[...] + d_odd[...]).T
    q_t[...] = (q_even[...] + q_odd[...]).T
    c_t[...] = context[...].T
    low = low_lanes(CHUNK)
    for pair in range(HEADS // 2):
        lanes = rows(pair, 128)
        parts = []
        for half, d_ctx in enumerate((d_even, d_odd)):
            head = 2 * pair + half
            pieces = []
            for i in range(CHUNKS):
                limit = (i + 1) * CHUNK if causal else SEQ
                dch = d_ctx[rows(i), lanes]
                total = jnp.sum(
                    dch.astype(F32) * context[rows(i), lanes].astype(F32), axis=-1, keepdims=True
                )
                dp = dot_nt(dch, values[:limit, lanes])
                p = probs[head, rows(i), :limit].astype(F32)
                d_score = (p * (dp - total)).astype(BF16)
                ds[rows(i), :limit] = d_score
                pieces.append(dot(d_score, keys[:limit, lanes]))
            parts.append(pieces)
            span = rows(head, HEAD_DIM)
            if causal:
                for j in range(CHUNKS):
                    start = j * CHUNK
                    dk_t[span, rows(j)] = dot(q_t[span, start:], ds[start:, rows(j)]).astype(BF16)
                    dv_t[span, rows(j)] = dot(
                        dc_t[span, start:], probs[head, start:, rows(j)]
                    ).astype(BF16)
            else:
                dk_t[span, :] = dot(q_t[span, :], ds[...]).astype(BF16)
                dv_t[span, :] = dot(dc_t[span, :], probs[head]).astype(BF16)
        for i in range(CHUNKS):
            dq[rows(i), lanes] = jnp.where(low, parts[0][i], parts[1][i]).astype(BF16)
    dk[...] = dk_t[...].T
    dv[...] = dv_t[...].T
    weight_grad(query_in_t, dq, out, table, unit, SCALE)
    weight_grad(memory_t, dk, out, table, unit + 1)
    weight_grad(memory_t, dv, out, table, unit + 2)
    weight_grad(c_t, grad, out, table, unit + 3)
    for i in range(CHUNKS):
        du[rows(i), :] = SCALE * dot_nt(dq[rows(i), :], weights[0])
        dm[rows(i), :] = dot_nt(dk[rows(i), :], weights[1]) + dot_nt(dv[rows(i), :], weights[2])
    return SCALE * column_sum(dq), column_sum(dv), column_sum(grad)


def silu_parts(hidden):
    gate = 1.0 / (1.0 + jnp.exp(-hidden))
    return hidden * gate, gate


def feed_forward(inputs, w_in, b_in, w_out, bias, residual, out):
    for i in range(CHUNKS):
        u = inputs[rows(i), :]
        total = residual[rows(i), :] + bias
        for k in range(FF // D):
            hidden = dot(u, w_in[k]) + b_in[:, rows(k, D)]
            active, _ = silu_parts(hidden)
            total = total + dot(active.astype(BF16), w_out[k])
        out[rows(i), :] = total


def feed_both(
    inputs, inputs_t, w_in, b_in, w_out, grad, act, dh, total, d_in, out, table, unit_in, wout_out, b_grad
):
    for k in range(FF // D):
        for i in range(CHUNKS):
            hidden = dot(inputs[rows(i), :], w_in[k]) + b_in[:, rows(k, D)]
            active, gate = silu_parts(hidden)
            low = active.astype(BF16)
            act[rows(i), :] = low
            d_act = dot_nt(grad[rows(i), :], w_out[k])
            dh[rows(i), :] = (d_act * (gate + active * (1.0 - gate))).astype(BF16)
            if total is not None:
                total[rows(i), :] = total[rows(i), :] + dot(low, w_out[k])
            back = dot_nt(dh[rows(i), :], w_in[k])
            d_in[rows(i), :] = back if k == 0 else d_in[rows(i), :] + back
        b_grad[:, rows(k, D)] = column_sum(dh)
        weight_grad(inputs_t, dh, out, table, unit_in + k)
        act_t = act[...].T
        for i in range(D // CHUNK):
            value = dot(act_t[rows(i), :], grad[...])
            for j in range(CHUNK // 64):
                block = k * 8 + i * 2 + j
                for z in range(4):
                    start = j * 64 + z * 16
                    wout_out[table[block], z] = value[start : start + 16, :].astype(BF16)


def load(source, table, jobs, sem):
    def step(block, carry):
        slot = table[block]
        for k, (unit, target) in enumerate(jobs):
            if len(target.shape) == 3:
                place = target.at[:, pl.ds(pl.multiple_of(block * 16, 16), 16), :]
            else:
                place = target.at[block]
            pltpu.make_async_copy(source.at[slot, pl.ds(unit, 4)], place, sem.at[k]).start()
        return carry

    lax.fori_loop(0, BLOCKS, step, 0)


def arrived(target, sem):
    pltpu.make_async_copy(target, target, sem).wait()


class Wide:
    def __init__(self, ref):
        self.ref = ref

    def __getitem__(self, k):
        return self.ref[8 * k : 8 * k + 8].reshape(D, D)


def first_kernel(
    tab_a, tab_b, s_len, t_len, langs, source, target, cot, vecs, b_enc, b_dec, ga, gb,
    dec_out, d_ffn, g_second, g_rows, g_bias,
    e_n, e_qe, e_qo, e_k, e_v, e_p, e_c, e_mid, e_n2, memory,
    start, s_n, s_qe, s_qo, s_k, s_v, s_p, s_c, first, c_n, c_qe, c_qo, c_k, c_v, c_p, c_c,
    we, wi, wo, ws, wc, vi, vo, bias_e, bias_s, bias_c, buf, second, n3, n3_t, act, dh, d_in, sem_a, sem_b,
):
    load(ga, tab_a, ((0, we), (4, wi), (8, wo)), sem_a)
    load(gb, tab_b, ((0, ws), (4, wc), (8, vi), (12, vo)), sem_b)
    masks(s_len, t_len, bias_e, bias_s, bias_c)

    def vec(index):
        return vecs[index : index + 1, :]

    def enc(index):
        return vec(ENC_VEC + index)

    def dec(index):
        return vec(DEC_VEC + index)

    onehot = lang_onehot(t_len, langs)
    table = vecs[...].astype(BF16)
    for i in range(CHUNKS):
        buf[rows(i), :] = source[rows(i), :].astype(F32)
        start[rows(i), :] = target[rows(i), :].astype(F32) + dot(onehot[rows(i), :], table)
    layer_norm(buf, enc(0), enc(1), e_n)
    layer_norm(start, dec(0), dec(1), s_n)
    arrived(we, sem_a.at[0])
    attn_project(e_n, e_n, we, enc(2), enc(3), e_qe, e_qo, e_k, e_v)
    attn_core(e_qe, e_qo, e_k, e_v, bias_e, e_p, e_c, False)
    attn_output(e_c, we.at[3], enc(4), source, e_mid)
    layer_norm(e_mid, enc(5), enc(6), e_n2)
    arrived(wi, sem_a.at[1])
    arrived(wo, sem_a.at[2])
    feed_forward(e_n2, wi, b_enc, Wide(wo), enc(7), e_mid, buf)
    for i in range(CHUNKS):
        memory[rows(i), :] = buf[rows(i), :].astype(BF16)
    arrived(ws, sem_b.at[0])
    attn_project(s_n, s_n, ws, dec(2), dec(3), s_qe, s_qo, s_k, s_v)
    attn_core(s_qe, s_qo, s_k, s_v, bias_s, s_p, s_c, True)
    attn_output(s_c, ws.at[3], dec(4), start, first)
    layer_norm(first, dec(5), dec(6), c_n)
    arrived(wc, sem_b.at[1])
    attn_project(c_n, memory, wc, dec(7), dec(8), c_qe, c_qo, c_k, c_v)
    attn_core(c_qe, c_qo, c_k, c_v, bias_c, c_p, c_c, False)
    attn_output(c_c, wc.at[3], dec(9), first, second)
    layer_norm(second, dec(10), dec(11), n3)
    n3_t[...] = n3[...].T
    arrived(vi, sem_b.at[2])
    arrived(vo, sem_b.at[3])
    for i in range(CHUNKS):
        buf[rows(i), :] = second[rows(i), :] + dec(12)
    feed_both(
        n3, n3_t, vi, b_dec, Wide(vo), cot, act, dh, buf, d_in,
        d_ffn, tab_b, 0, d_ffn.at[:, 4:8], g_bias,
    )
    for i in range(CHUNKS):
        dec_out[rows(i), :] = buf[rows(i), :].astype(BF16)
    d_gain, d_shift = norm_back(second, dec(10), d_in, cot, g_second)
    g_rows[...] = jnp.zeros(g_rows.shape, F32)
    g_rows[0:1, :] = d_gain
    g_rows[1:2, :] = d_shift
    g_rows[2:3, :] = column_sum(cot)


def second_kernel(
    tab_b, t_len, langs, vecs, g_second, g_rows, memory,
    start, s_n, s_qe, s_qo, s_k, s_v, s_p, s_c, first, c_n, c_qe, c_qo, c_k, c_v, c_p, c_c, gb,
    d_attn, g_start, g_memory, g_vec,
    ws, wc, low, u_t, m_t, g_first, d_even, d_odd, dc_t, q_t, c_t, ds, dq, dk_t, dv_t, dk, dv, du, dm, sem,
):
    load(gb, tab_b, ((0, ws), (4, wc)), sem)
    scratch = (d_even, d_odd, dc_t, q_t, c_t, ds, dq, dk_t, dv_t, dk, dv, du, dm)

    def dec(index):
        return vecs[DEC_VEC + index : DEC_VEC + index + 1, :]

    u_t[...] = c_n[...].T
    m_t[...] = memory[...].T
    low[...] = g_second[...].astype(BF16)
    arrived(ws, sem.at[0])
    arrived(wc, sem.at[1])
    bias_two = attn_back(
        low, u_t, m_t, wc, (c_qe, c_qo, c_k, c_v, c_p, c_c), scratch, d_attn, tab_b, 4, False
    )
    g_memory[...] = dm[...]
    gain_two = norm_back(first, dec(5), du, g_second, g_first)
    low[...] = g_first[...].astype(BF16)
    u_t[...] = s_n[...].T
    bias_one = attn_back(
        low, u_t, u_t, ws, (s_qe, s_qo, s_k, s_v, s_p, s_c), scratch, d_attn, tab_b, 0, True
    )
    du[...] = du[...] + dm[...]
    gain_one = norm_back(start, dec(0), du, g_first, g_start)
    onehot = lang_onehot(t_len, langs)
    g_vec[...] = lax.dot_general(
        onehot, g_start[...].astype(BF16), (((0,), (0,)), ((), ())), preferred_element_type=F32
    )
    values = gain_one + bias_one + gain_two + bias_two
    for i, value in enumerate(values):
        g_vec[DEC_VEC + i : DEC_VEC + i + 1, :] = value
    g_vec[DEC_VEC + 10 : DEC_VEC + 13, :] = g_rows[0:3, :]


def third_kernel(
    tab_a, vecs, b_enc, source, g_memory, g_vec, g_bias,
    e_n, e_qe, e_qo, e_k, e_v, e_p, e_c, e_mid, e_n2, ga,
    d_enc, g_source,
    we, wi, wo, buf, low, u_t, act, dh, d_in, g_mid, b_grad, all_vec,
    d_even, d_odd, dc_t, q_t, c_t, ds, dq, dk_t, dv_t, dk, dv, du, dm, sem,
):
    load(ga, tab_a, ((0, we), (4, wi), (8, wo)), sem)
    scratch = (d_even, d_odd, dc_t, q_t, c_t, ds, dq, dk_t, dv_t, dk, dv, du, dm)

    def enc(index):
        return vecs[ENC_VEC + index : ENC_VEC + index + 1, :]

    u_t[...] = e_n2[...].T
    low[...] = g_memory[...].astype(BF16)
    arrived(wi, sem.at[1])
    arrived(wo, sem.at[2])
    feed_both(
        e_n2, u_t, wi, b_enc, Wide(wo), low, act, dh, None, d_in,
        d_enc, tab_a, 4, d_enc.at[:, 8:12], b_grad,
    )
    bias_out = column_sum(low)
    gain_two = norm_back(e_mid, enc(5), d_in, g_memory, g_mid)
    low[...] = g_mid[...].astype(BF16)
    u_t[...] = e_n[...].T
    arrived(we, sem.at[0])
    bias_one = attn_back(
        low, u_t, u_t, we, (e_qe, e_qo, e_k, e_v, e_p, e_c), scratch, d_enc, tab_a, 0, False
    )
    du[...] = du[...] + dm[...]
    for i in range(CHUNKS):
        buf[rows(i), :] = source[rows(i), :].astype(F32)
    gain_one = norm_back(buf, enc(0), du, g_mid, g_source)
    all_vec[...] = g_vec[...]
    for i, value in enumerate(gain_one + bias_one + gain_two + (bias_out,)):
        all_vec[ENC_VEC + i : ENC_VEC + i + 1, :] = value
    turned = all_vec[...].T.astype(BF16)
    zero = jnp.zeros((16, 128), BF16)
    for block in range(BLOCKS):
        slot = tab_a[block]
        tile = rows(block // 2, 128)
        d_enc[slot, 12, :, 0:128] = turned[rows(block, 16), :]
        d_enc[slot, 12, :, 128:256] = jnp.broadcast_to(b_grad[:, tile], (16, 128)).astype(BF16)
        d_enc[slot, 12, :, 256:384] = jnp.broadcast_to(g_bias[:, tile], (16, 128)).astype(BF16)
        d_enc[slot, 12, :, 384:512] = zero


VM = pl.BlockSpec(memory_space=pltpu.VMEM)
SM = pl.BlockSpec(memory_space=pltpu.SMEM)
HB = pl.BlockSpec(memory_space=pl.ANY)


def act_shape(dtype=BF16):
    return ((SEQ, D), dtype)


KEPT = [act_shape()] * 5 + [((HEADS, SEQ, SEQ), BF16), act_shape()]


def call(body, in_specs, outs, scratch, flops, args):
    return pl.pallas_call(
        body,
        in_specs=in_specs,
        out_specs=[VM] * len(outs),
        out_shape=[jax.ShapeDtypeStruct(s, t) for s, t in outs],
        scratch_shapes=[
            pltpu.VMEM(*s) if isinstance(s, tuple) else pltpu.SemaphoreType.DMA((s,))
            for s in scratch
        ],
        compiler_params=pltpu.CompilerParams(vmem_limit_bytes=63 * 1024 * 1024),
        cost_estimate=pl.CostEstimate(flops=flops, bytes_accessed=1 << 24, transcendentals=0),
    )(*args)


SQUARE = ((4, D, D), BF16)
TALL = ((BLOCKS, 4, 16, D), BF16)
TURN = ((D, SEQ), BF16)
BIAS = ((SEQ, SEQ), F32)
BACK = [act_shape()] * 2 + [TURN] * 3 + [((SEQ, SEQ), BF16), act_shape(), TURN, TURN, act_shape(), act_shape()]
BACK = BACK + [act_shape(F32)] * 2


def pairs(axis, step):
    k = AXES.index(axis)
    found = []

    def flat(place):
        index = 0
        for at, size in zip(place, SIZES):
            index = index * size + at
        return index

    for place in itertools.product(*[range(size) for size in SIZES]):
        if axis == "c":
            other = 1
        else:
            other = 1 if (step == 0) == (place[1] == 0) else 3
        target = list(place)
        target[k] = place[k] ^ other
        found.append((flat(place), flat(target)))
    return found


def swap(values, axis, step=0):
    return lax.ppermute(values, AXES, pairs(axis, step))


def slot_of(distance, core):
    zero = jnp.array([0, 1, 3, 2], jnp.int32)[distance]
    one = jnp.array([0, 2, 3, 1], jnp.int32)[distance]
    return jnp.where(core == 0, zero, one)


def slot_table(inner, outer):
    block = jnp.arange(BLOCKS, dtype=jnp.int32)
    at = {"x": block // 8, "c": (block // 4) % 2, "y": block % 4}
    me = {name: lax.axis_index(name) for name in AXES}
    core = at["c"]
    other = (core != me["c"]).astype(jnp.int32)
    return (
        16 * other
        + slot_of(at[inner] ^ me[inner], core)
        + 4 * slot_of(at[outer] ^ me[outer], core)
    )


def z_order(values, axis):
    me = lax.axis_index("z")
    core = lax.axis_index("c")
    picks = [lax.dynamic_index_in_dim(values, slot_of(q ^ me, core), axis) for q in range(4)]
    return jnp.concatenate(picks, axis)


def z_slots(values, axis):
    me = lax.axis_index("z")
    hop = jnp.where(lax.axis_index("c") == 0, 1, 3)
    picks = [lax.dynamic_index_in_dim(values, me ^ q, axis) for q in (0, hop, 4 - hop, 2)]
    return jnp.concatenate(picks, axis)


def grow(values, axis):
    for step in range(2):
        values = jnp.concatenate([values, swap(values, axis, step)], axis=0)
    return values


def shrink(values, axis, last=BF16):
    for step in (1, 0):
        half = values.shape[0] // 2
        received = swap(values[half:], axis, step)
        total = values[:half].astype(F32) + received.astype(F32)
        values = total.astype(BF16 if step else last)
    return values


def gather(units):
    around = z_order(grow(units[None], "z"), 0)

    def merge(first, last):
        part = around[:, first:last].reshape(4, last - first, 4, 4, D)
        return part.transpose(1, 2, 0, 3, 4).reshape((last - first) * 4, 16, D)

    enc = jnp.concatenate([merge(0, 2), around[:, 2]], axis=0)[None]
    dec = jnp.concatenate([merge(3, 6), around[:, 6]], axis=0)[None]
    enc = grow(grow(enc, "x"), "y")
    dec = grow(grow(dec, "y"), "x")
    return (
        jnp.concatenate([enc, swap(enc, "c")], axis=0),
        jnp.concatenate([dec, swap(dec, "c")], axis=0),
    )


def scatter(grads, inner, outer, wide):
    received = swap(grads[16:], "c")
    values = (grads[:16].astype(F32) + received.astype(F32)).astype(BF16)
    values = shrink(shrink(values, outer), inner)[0]
    narrow = values
    if wide is not None:
        narrow = jnp.concatenate([values[: wide[0]], values[wide[1] :]], axis=0)
    count = narrow.shape[0]
    parts = narrow.reshape(count, 4, 4, D).transpose(1, 0, 2, 3).reshape(4, count * 4, D)
    if wide is not None:
        parts = jnp.concatenate([parts, values[wide[0] : wide[1]]], axis=1)
    total = shrink(z_slots(parts, 0), "z", F32)[0]
    return total[: count * 4].reshape(count, 4, D), total[count * 4 :]


def turn_in(shard):
    return shard.reshape(4, 4, D).transpose(1, 0, 2).reshape(16, D)


def per_device(
    source, target, source_lengths, target_lengths, lang_ids, out_cotangent,
    enc_attn, enc_vectors, enc_w_in, enc_b_in, enc_w_out,
    dec_self, dec_cross, dec_vectors, dec_w_in, dec_b_in, dec_w_out, lang_table,
):
    small = jnp.concatenate(
        [
            lang_table.T,
            jnp.zeros((4, ENC_VEC - LANGS), BF16),
            enc_vectors.T,
            dec_vectors.T,
            jnp.zeros((4, 128 - DEC_VEC - 13), BF16),
            enc_b_in.reshape(4, 4),
            dec_b_in.reshape(4, 4),
            jnp.zeros((4, 120), BF16),
        ],
        axis=1,
    )
    small = lax.all_gather(small, AXES, axis=0, tiled=True)
    vecs = small[:, :128].T.astype(F32)
    b_enc = small[:, 128:132].reshape(1, FF).astype(F32)
    b_dec = small[:, 132:136].reshape(1, FF).astype(F32)
    units = jnp.stack(
        [
            enc_attn.reshape(16, D),
            turn_in(enc_w_in),
            enc_w_out,
            dec_self.reshape(16, D),
            dec_cross.reshape(16, D),
            turn_in(dec_w_in),
            dec_w_out,
        ]
    )
    ga, gb = gather(units)
    tab_a = slot_table("x", "y")
    tab_b = slot_table("y", "x")

    (
        dec_out, d_ffn, g_second, g_rows, g_bias,
        *rest,
    ) = call(
        first_kernel,
        [SM] * 5 + [VM] * 6 + [HB] * 2,
        [act_shape(), ((BLOCKS, 8, 16, D), BF16), act_shape(F32), ((8, D), F32), ((1, FF), F32)]
        + KEPT
        + [act_shape(F32), act_shape(), act_shape()]
        + [act_shape(F32)]
        + KEPT
        + [act_shape(F32)]
        + KEPT,
        [SQUARE, SQUARE, TALL, SQUARE, SQUARE, SQUARE, TALL, BIAS, BIAS, BIAS]
        + [act_shape(F32), act_shape(F32), act_shape(), TURN, act_shape(), act_shape(), act_shape(F32), 3, 4],
        12 * 10**9,
        (
            tab_a, tab_b, source_lengths, target_lengths, lang_ids,
            source[0], target[0], out_cotangent[0], vecs, b_enc, b_dec, ga, gb,
        ),
    )
    enc_kept, memory, dec_kept = rest[:9], rest[9], rest[10:]
    ffn_small, ffn_tall = scatter(d_ffn, "y", "x", (4, 8))
    d_attn, g_start, g_memory, g_vec = call(
        second_kernel,
        [SM] * 3 + [VM] * 20 + [HB],
        [((BLOCKS, 8, 16, D), BF16), act_shape(F32), act_shape(F32), ((128, D), F32)],
        [SQUARE, SQUARE, act_shape(), TURN, TURN, act_shape(F32)] + BACK + [2],
        6 * 10**9,
        (tab_b, target_lengths, lang_ids, vecs, g_second, g_rows, memory, *dec_kept, gb),
    )
    attn_small, _ = scatter(d_attn, "y", "x", None)
    d_enc, g_source = call(
        third_kernel,
        [SM] + [VM] * 15 + [HB],
        [((BLOCKS, 13, 16, D), BF16), act_shape(F32)],
        [SQUARE, SQUARE, TALL, act_shape(F32), act_shape(), TURN, act_shape(), act_shape()]
        + [act_shape(F32), act_shape(F32), ((1, FF), F32), ((128, D), F32)]
        + BACK
        + [3],
        8 * 10**9,
        (tab_a, vecs, b_enc, source[0], g_memory, g_vec, g_bias, *enc_kept, ga),
    )
    enc_small, enc_tall = scatter(d_enc, "x", "y", (8, 12))
    last = enc_small[8]
    offset = (lax.axis_index("y") % 2) * 64 + lax.axis_index("z") * 16
    bias_enc = lax.dynamic_slice(last, (0, 128 + offset), (1, 16)).reshape(16)
    bias_dec = lax.dynamic_slice(last, (0, 256 + offset), (1, 16)).reshape(16)
    vec_grads = last[:, :128].T

    def turn_out(part):
        return part.transpose(1, 0, 2).reshape(4, FF)

    return (
        dec_out[None],
        g_source[None],
        g_start[None],
        enc_small[0:4],
        vec_grads[ENC_VEC : ENC_VEC + 8],
        turn_out(enc_small[4:8]),
        bias_enc,
        enc_tall,
        attn_small[0:4],
        attn_small[4:8],
        vec_grads[DEC_VEC : DEC_VEC + 13],
        turn_out(ffn_small[0:4]),
        bias_dec,
        ffn_tall,
        vec_grads[:LANGS],
    )


def solution(mesh):
    fine = Mesh(mesh.devices.reshape(SIZES), AXES)
    flat = AXES
    in_specs = (
        P(flat, None, None),
        P(flat, None, None),
        P(flat, None),
        P(flat, None),
        P(flat, None),
        P(flat, None, None),
        P(None, flat, None),
        P(None, flat),
        P(flat, None),
        P(flat),
        P(flat, None),
        P(None, flat, None),
        P(None, flat, None),
        P(None, flat),
        P(flat, None),
        P(flat),
        P(flat, None),
        P(None, flat),
    )
    out_specs = (
        P(flat, None, None),
        P(flat, None, None),
        P(flat, None, None),
        P(None, flat, None),
        P(None, flat),
        P(flat, None),
        P(flat),
        P(flat, None),
        P(None, flat, None),
        P(None, flat, None),
        P(None, flat),
        P(flat, None),
        P(flat),
        P(flat, None),
        P(None, flat),
    )
    return jax.shard_map(
        per_device, mesh=fine, in_specs=in_specs, out_specs=out_specs, check_vma=False
    )
```

```python
import itertools

import jax
import jax.numpy as jnp
import numpy as np
from jax import lax
from jax.experimental import pallas as pl
from jax.experimental.pallas import tpu as pltpu
from jax.sharding import Mesh
from jax.sharding import PartitionSpec as P

D = 512
HEADS = 8
HEAD_DIM = 64
FF = 2048
LANGS = 100
SEQ = 384
DOCS = 5
EPSILON = 1e-05
NEGATIVE = -1000000000.0
OPEN = 3e38
SCALE = HEAD_DIM ** (-0.5)
AXES = ("x", "c", "y", "z")
SIZES = (4, 2, 4, 4)
BLOCKS = 32
ENC_VEC = 104
DEC_VEC = 112
CHUNK = 128
CHUNKS = SEQ // CHUNK
TAB_A, TAB_B, TALL_BLOCK, TALL_SLOT, CORE = 0, 32, 64, 192, 320
F32 = jnp.float32
BF16 = jnp.bfloat16


def dot(left, right):
    return lax.dot_general(left, right, (((1,), (0,)), ((), ())), preferred_element_type=F32)


def dot_nt(left, right):
    return lax.dot_general(left, right, (((1,), (1,)), ((), ())), preferred_element_type=F32)


def rows(index, size=CHUNK):
    return slice(index * size, (index + 1) * size)


def normed(values):
    mean = jnp.mean(values, axis=-1, keepdims=True)
    center = values - mean
    rstd = lax.rsqrt(jnp.mean(center * center, axis=-1, keepdims=True) + EPSILON)
    return center * rstd, rstd


def layer_norm(source, gain, shift, out):
    for i in range(CHUNKS):
        hat, _ = normed(source[rows(i), :])
        out[rows(i), :] = (hat * gain + shift).astype(BF16)


def norm_back(source, gain, grad, base, out):
    d_gain = jnp.zeros((1, D), F32)
    d_shift = jnp.zeros((1, D), F32)
    for i in range(CHUNKS):
        hat, rstd = normed(source[rows(i), :])
        dy = grad[rows(i), :]
        d_gain = d_gain + jnp.sum(dy * hat, axis=0, keepdims=True)
        d_shift = d_shift + jnp.sum(dy, axis=0, keepdims=True)
        dyg = dy * gain
        mean_one = jnp.mean(dyg, axis=-1, keepdims=True)
        mean_two = jnp.mean(dyg * hat, axis=-1, keepdims=True)
        out[rows(i), :] = base[rows(i), :].astype(F32) + rstd * (dyg - mean_one - hat * mean_two)
    return d_gain, d_shift


def low_lanes(count):
    return lax.broadcasted_iota(jnp.int32, (count, 128), 1) < HEAD_DIM


def head_mask():
    lane = lax.broadcasted_iota(jnp.int32, (1, D), 1)
    return ((lane // HEAD_DIM) % 2 == 0).astype(F32)


def doc_ids(lengths, shape, axis):
    position = lax.broadcasted_iota(jnp.int32, shape, axis)
    total = jnp.zeros(shape, jnp.int32)
    end = 0
    for i in range(DOCS):
        end = end + lengths[0, i]
        total = total + (position >= end).astype(jnp.int32)
    return total


def masks(s_len, t_len, bias_e, bias_s, bias_c):
    shape = (SEQ, SEQ)
    s_row = doc_ids(s_len, (1, SEQ), 1)
    t_row = doc_ids(t_len, (1, SEQ), 1)
    s_col = doc_ids(s_len, (SEQ, 1), 0)
    t_col = doc_ids(t_len, (SEQ, 1), 0)
    for i in range(CHUNKS):
        shape = (CHUNK, SEQ)
        sc = jnp.broadcast_to(s_col[rows(i), :], shape)
        tc = jnp.broadcast_to(t_col[rows(i), :], shape)
        key = lax.broadcasted_iota(jnp.int32, shape, 1)
        query = lax.broadcasted_iota(jnp.int32, shape, 0) + i * CHUNK
        bias_e[rows(i), :] = jnp.where(sc == s_row, OPEN, NEGATIVE)
        bias_s[rows(i), :] = jnp.where((tc == t_row) & (key <= query), OPEN, NEGATIVE)
        bias_c[rows(i), :] = jnp.where(tc == s_row, OPEN, NEGATIVE)


def lang_onehot(t_len, langs):
    doc = doc_ids(t_len, (SEQ, 128), 0)
    lang = jnp.zeros((SEQ, 128), jnp.int32)
    for i in range(DOCS):
        lang = jnp.where(doc == i, langs[0, i], lang)
    lane = lax.broadcasted_iota(jnp.int32, (SEQ, 128), 1)
    return jnp.where(lang == lane, 1.0, 0.0).astype(BF16)


def attn_project(query_in, memory, weights, bias_q, bias_v, q_even, q_odd, keys, values):
    even = head_mask()
    q = SCALE * (dot(query_in[...], weights[0]) + bias_q)
    q_even[...] = (q * even).astype(BF16)
    q_odd[...] = (q * (1.0 - even)).astype(BF16)
    keys[...] = dot(memory[...], weights[1]).astype(BF16)
    values[...] = (dot(memory[...], weights[2]) + bias_v).astype(BF16)


def attn_core(q_even, q_odd, keys, values, bias, probs, inverse, context):
    low = low_lanes(SEQ)
    queries = (q_even, q_odd)
    held = []

    def lanes(head):
        return rows(head // 2, 128)

    def scores(head):
        return dot_nt(queries[head % 2][:, lanes(head)], keys[:, lanes(head)])

    def finish(head, e, total):
        over = 1.0 / total
        held.append((dot(e, values[:, lanes(head)]) * over, over))
        if head % 2 == 1:
            (one, over_one), (two, over_two) = held
            held.clear()
            context[:, lanes(head)] = jnp.where(low, one, two).astype(BF16)
            inverse[:, lanes(head)] = jnp.where(low, over_one, over_two)

    s = scores(0)
    last = None
    for head in range(HEADS):
        s_next = scores(head + 1) if head + 1 < HEADS else None
        s = jnp.minimum(s, bias[...])
        e = jnp.exp(s - jnp.max(s, axis=-1, keepdims=True))
        total = jnp.sum(e, axis=-1, keepdims=True)
        e = e.astype(BF16)
        probs[head] = e
        if last is not None:
            finish(*last)
        last = (head, e, total)
        s = s_next
    finish(*last)


def attn_output(context, weight, bias_o, residual, out):
    branch = dot(context[...], weight[...]) + bias_o
    out[...] = residual[...].astype(F32) + branch


def put_blocks(acc, out, other, unit, table, first):
    for slot in range(16):
        for j, ref in enumerate((out, other)):
            start = pl.multiple_of(table[first + 16 * j + slot] * 16, 16)
            ref[slot, unit] = acc[pl.ds(start, 16), :].astype(BF16)


def weight_grad(left_t, right, acc, place, unit, scale=None):
    out, other, table, first = place
    value = dot(left_t[...], right[...])
    acc[...] = value if scale is None else value * scale
    put_blocks(acc, out, other, unit, table, first)


def tall_grad(left_t, right, acc, place, chunk):
    out, other, table = place
    acc[...] = dot(left_t, right[...])
    for j, ref in enumerate((out, other)):
        core = table[CORE] ^ j
        for block in range(16):
            slot = table[TALL_SLOT + chunk * 32 + core * 16 + block] - 64 * j
            start = pl.multiple_of(core * 256 + block * 16, 16)
            ref[slot] = acc[pl.ds(start, 16), :].astype(BF16)


def column_sum(ref):
    return jnp.sum(ref[...].astype(F32), axis=0, keepdims=True)


def attn_back(grad, query_in_t, memory_t, weights, kept, scratch, acc, place):
    q_even, q_odd, keys, values, probs, inverse, context = kept
    d_even, d_odd, dc_t, q_t, c_t, dq, dk_t, dv_t, dk, dv, du, dm = scratch
    even = head_mask()
    dc = dot_nt(grad[...], weights[3]) * inverse[...]
    d_even[...] = (dc * even).astype(BF16)
    d_odd[...] = (dc * (1.0 - even)).astype(BF16)
    dc_t[...] = (d_even[...] + d_odd[...]).T
    q_t[...] = (q_even[...] + q_odd[...]).T
    c_t[...] = context[...].T
    low = low_lanes(SEQ)
    d_ctx = (d_even, d_odd)
    held = []

    def lanes(head):
        return rows(head // 2, 128)

    def first(head):
        dch = d_ctx[head % 2][:, lanes(head)]
        total = jnp.sum(
            dch.astype(F32) * context[:, lanes(head)].astype(F32), axis=-1, keepdims=True
        )
        return dot_nt(dch, values[:, lanes(head)]), total

    def finish(head, ds):
        span = rows(head, HEAD_DIM)
        held.append(dot(ds, keys[:, lanes(head)]))
        dk_t[span, :] = dot(q_t[span, :], ds).astype(BF16)
        dv_t[span, :] = dot(dc_t[span, :], probs[head]).astype(BF16)
        if head % 2 == 1:
            dq[:, lanes(head)] = jnp.where(low, held[0], held[1]).astype(BF16)
            held.clear()

    now = first(0)
    last = None
    for head in range(HEADS):
        later = first(head + 1) if head + 1 < HEADS else None
        dp, total = now
        ds = (probs[head].astype(F32) * (dp - total)).astype(BF16)
        if last is not None:
            finish(*last)
        last = (head, ds)
        now = later
    finish(*last)
    dk[...] = dk_t[...].T
    dv[...] = dv_t[...].T
    weight_grad(query_in_t, dq, acc, place, 0, SCALE)
    weight_grad(memory_t, dk, acc, place, 1)
    weight_grad(memory_t, dv, acc, place, 2)
    weight_grad(c_t, grad, acc, place, 3)
    du[...] = SCALE * dot_nt(dq[...], weights[0])
    dm[...] = dot_nt(dk[...], weights[1]) + dot_nt(dv[...], weights[2])
    return SCALE * column_sum(dq), column_sum(dv), column_sum(grad)


def silu_parts(hidden):
    gate = 1.0 / (1.0 + jnp.exp(-hidden))
    return hidden * gate, gate


def feed_forward(inputs, w_in, b_in, w_out, bias, residual, out):
    total = residual[...] + bias
    for k in range(FF // D):
        active, _ = silu_parts(dot(inputs[...], w_in[k]) + b_in[:, rows(k, D)])
        total = total + dot(active.astype(BF16), w_out[k])
    out[...] = total


def feed_both(
    inputs, inputs_t, w_in, b_in, w_out, grad, act, dh, total, d_in, acc, place_in, place_out, b_grad
):
    hidden = dot(inputs[...], w_in[0]) + b_in[:, rows(0, D)]
    for k in range(FF // D):
        d_act = dot_nt(grad[...], w_out[k])
        active, gate = silu_parts(hidden)
        low = active.astype(BF16)
        act[...] = low
        d_hid = (d_act * (gate + active * (1.0 - gate))).astype(BF16)
        dh[...] = d_hid
        if k + 1 < FF // D:
            hidden = dot(inputs[...], w_in[k + 1]) + b_in[:, rows(k + 1, D)]
        if total is not None:
            total[...] = total[...] + dot(low, w_out[k])
        back = dot_nt(d_hid, w_in[k])
        d_in[...] = back if k == 0 else d_in[...] + back
        b_grad[:, rows(k, D)] = column_sum(dh)
        weight_grad(inputs_t, dh, acc, place_in, k)
        tall_grad(act[...].T, grad, acc, place_out, k)


def load(table, first, pieces, jobs):
    def step(slot, carry):
        for k, piece in enumerate(pieces):
            start = pl.multiple_of(table[first + 8 * k + slot] * 16, 16)
            for unit, count, target, row, sem in jobs:
                place = target.at[pl.ds(row, count), pl.ds(start, 16), :]
                pltpu.make_async_copy(piece.at[slot, pl.ds(unit, count)], place, sem).start()
        return carry

    lax.fori_loop(0, 8, step, 0)


def load_tall(table, pieces, jobs):
    def step(slot, carry):
        for k, piece in enumerate(pieces):
            block = table[TALL_BLOCK + 32 * k + slot]
            for unit, target, sem in jobs:
                pltpu.make_async_copy(piece.at[slot, unit], target.at[block], sem).start()
        return carry

    lax.fori_loop(0, 32, step, 0)


def arrived(target, sem):
    pltpu.make_async_copy(target, target, sem).wait()


class Wide:
    def __init__(self, ref):
        self.ref = ref

    def __getitem__(self, k):
        return self.ref[32 * k : 32 * k + 32].reshape(D, D)


def pack_kernel(
    spot, attn, w_in, w_out, self_w, cross, dec_in, dec_out, vec_e, vec_d, lang, b_e, b_d,
    narrow, tall, wide,
):
    narrow[0:4] = attn[...]
    narrow[9:11] = cross[0:2]
    narrow[11:15] = self_w[...]
    narrow[19:21] = cross[2:4]
    for k in range(4):
        narrow[4 + k] = w_in[:, rows(k, D)]
        narrow[15 + k] = dec_in[:, rows(k, D)]
    tall[0] = w_out[...]
    tall[1] = dec_out[...]
    wide[...] = jnp.zeros(wide.shape, F32)
    wide[0:LANGS, 0:4] = lang[...].astype(F32)
    wide[ENC_VEC : ENC_VEC + 8, 0:4] = vec_e[...].astype(F32)
    wide[DEC_VEC : DEC_VEC + 13, 0:4] = vec_d[...].astype(F32)
    turned = wide[...].T
    row = lax.broadcasted_iota(jnp.int32, (16, 128), 0)
    lane = lax.broadcasted_iota(jnp.int32, (16, 128), 1)
    place = jnp.where(lane == row + spot[0] * 16, 1.0, 0.0).astype(BF16)
    first = lax.broadcasted_iota(jnp.int32, (8, 128), 0) == 0
    wide[0:8, :] = turned[0:8, :]
    narrow[8, :, 0:128] = wide[0:4, :].astype(BF16)
    for k, ref in enumerate((b_e, b_d)):
        spread = dot(jnp.broadcast_to(ref[...].astype(F32), (8, 16)).astype(BF16), place)
        wide[0:8, :] = jnp.where(first, spread, 0.0)
        narrow[8, :, 128 + 128 * k : 256 + 128 * k] = wide[0:4, :].astype(BF16)
    narrow[8, :, 384:512] = jnp.zeros((4, 128), BF16)


def unpack_kernel(
    spot, p_low, p_got, q_low, q_got, r_low, r_got,
    attn, vec_e, w_in, b_e, w_out, self_w, cross, vec_d, dec_in, b_d, dec_out, lang,
    last,
):
    def total(low, got, index):
        return low[0, index].astype(F32) + got[0, index].astype(F32)

    for k in range(4):
        dec_in[:, rows(k, D)] = total(p_low, p_got, k)
        cross[k] = total(p_low, p_got, 4 + k)
        w_in[:, rows(k, D)] = total(p_low, p_got, 8 + k)
        self_w[k] = total(q_low, q_got, k)
        attn[k] = total(q_low, q_got, 4 + k)
    dec_out[...] = total(r_low, r_got, 0)
    w_out[...] = total(r_low, r_got, 1)
    last[...] = total(q_low, q_got, 8)
    lang[...] = last[:, 0:LANGS]
    vec_e[...] = last[:, ENC_VEC : ENC_VEC + 8]
    vec_d[...] = last[:, DEC_VEC : DEC_VEC + 13]
    for k, ref in enumerate((b_e, b_d)):
        tile = jnp.broadcast_to(last[0:1, 128 + 128 * k : 256 + 128 * k], (8, 128))
        ref[...] = pltpu.roll(tile, 128 - 16 * spot[0], 1)[0:1, 0:16]


class Copies:
    def __init__(self, incoming, outgoing, sem):
        self.sem = sem
        self.incoming = {}
        self.outgoing = {}
        for hbm, vmem in incoming:
            copy = pltpu.make_async_copy(hbm, vmem, sem.at[len(self.incoming)])
            copy.start()
            self.incoming[id(vmem)] = copy
        for hbm, vmem in outgoing:
            index = len(self.incoming) + len(self.outgoing)
            self.outgoing[id(vmem)] = pltpu.make_async_copy(vmem, hbm, sem.at[index])
        self.base = len(self.incoming)
        self.sent = []

    def need(self, *refs):
        for ref in refs:
            copy = self.incoming.pop(id(ref), None)
            if copy is not None:
                copy.wait()

    def send(self, *refs):
        for ref in refs:
            copy = self.outgoing.pop(id(ref))
            copy.start()
            self.sent.append(copy)

    def finish(self):
        for copy in list(self.outgoing.values()):
            copy.start()
            self.sent.append(copy)
        for copy in list(self.incoming.values()) + self.sent:
            copy.wait()


def first_kernel(
    io, table, s_len, t_len, langs, source, target, cot,
    a0, a1, a2, a3, b0, b1, b2, b3, t0, t1, t2, t3,
    dec_out, d_in_own, d_out_own, d_other_in, d_other_out, g_second, g_rows, g_bias, vecs, b_enc,
    e_n, e_qe, e_qo, e_k, e_v, e_p, e_i, e_c, e_mid, e_n2, memory,
    start, s_n, s_qe, s_qo, s_k, s_v, s_p, s_i, s_c, first, c_n, c_qe, c_qo, c_k, c_v, c_p, c_i, c_c,
    small, we, wi, wo, ws, wc, vi, vo, bias_e, bias_s, bias_c, buf, second, n3, n3_t, act, dh, d_in, acc,
    b_dec, sem,
):
    load(
        table, TAB_A, (a0, a1, a2, a3),
        ((8, 1, small, 0, sem.at[7]), (0, 4, we, 0, sem.at[0]), (4, 4, wi, 0, sem.at[1])),
    )
    load_tall(table, (t0, t1, t2, t3), ((0, wo, sem.at[2]), (1, vo, sem.at[6])))
    load(table, TAB_A, (a0, a1, a2, a3), ((9, 2, wc, 0, sem.at[4]),))
    load(
        table, TAB_B, (b0, b1, b2, b3),
        ((0, 4, ws, 0, sem.at[3]), (4, 4, vi, 0, sem.at[5]), (8, 2, wc, 2, sem.at[4])),
    )
    masks(s_len, t_len, bias_e, bias_s, bias_c)
    onehot = lang_onehot(t_len, langs)
    arrived(small, sem.at[7])
    vecs[...] = small[0, :, 0:128].astype(F32).T
    for k, ref in enumerate((b_enc, b_dec)):
        for tile in range(FF // 128):
            part = small[0, rows(tile, 32), 128 + 128 * k : 256 + 128 * k].astype(F32)
            ref[:, rows(tile, 128)] = jnp.sum(part, axis=0, keepdims=True)

    def enc(index):
        return vecs[ENC_VEC + index : ENC_VEC + index + 1, :]

    def dec(index):
        return vecs[DEC_VEC + index : DEC_VEC + index + 1, :]

    io.need(source)
    buf[...] = source[...].astype(F32)
    layer_norm(buf, enc(0), enc(1), e_n)
    arrived(we, sem.at[0])
    attn_project(e_n, e_n, we, enc(2), enc(3), e_qe, e_qo, e_k, e_v)
    attn_core(e_qe, e_qo, e_k, e_v, bias_e, e_p, e_i, e_c)
    io.send(vecs, b_enc, e_n, e_qe, e_qo, e_k, e_v, e_p, e_i, e_c)
    attn_output(e_c, we.at[3], enc(4), source, e_mid)
    layer_norm(e_mid, enc(5), enc(6), e_n2)
    io.send(e_mid, e_n2)
    arrived(wi, sem.at[1])
    arrived(wo, sem.at[2])
    feed_forward(e_n2, wi, b_enc, Wide(wo), enc(7), e_mid, buf)
    memory[...] = buf[...].astype(BF16)
    io.send(memory)
    io.need(target)
    start[...] = target[...].astype(F32) + dot(onehot, vecs[...].astype(BF16))
    layer_norm(start, dec(0), dec(1), s_n)
    arrived(ws, sem.at[3])
    attn_project(s_n, s_n, ws, dec(2), dec(3), s_qe, s_qo, s_k, s_v)
    attn_core(s_qe, s_qo, s_k, s_v, bias_s, s_p, s_i, s_c)
    io.send(start, s_n, s_qe, s_qo, s_k, s_v, s_p, s_i, s_c)
    attn_output(s_c, ws.at[3], dec(4), start, first)
    layer_norm(first, dec(5), dec(6), c_n)
    arrived(wc, sem.at[4])
    attn_project(c_n, memory, wc, dec(7), dec(8), c_qe, c_qo, c_k, c_v)
    attn_core(c_qe, c_qo, c_k, c_v, bias_c, c_p, c_i, c_c)
    io.send(first, c_n, c_qe, c_qo, c_k, c_v, c_p, c_i, c_c)
    attn_output(c_c, wc.at[3], dec(9), first, second)
    layer_norm(second, dec(10), dec(11), n3)
    n3_t[...] = n3[...].T
    buf[...] = second[...] + dec(12)
    arrived(vi, sem.at[5])
    arrived(vo, sem.at[6])
    io.need(cot)
    feed_both(
        n3, n3_t, vi, b_dec, Wide(vo), cot, act, dh, buf, d_in, acc,
        (d_in_own, d_other_in, table, TAB_A), (d_out_own, d_other_out, table), g_bias,
    )
    io.send(d_other_in, d_other_out, d_in_own, d_out_own)
    dec_out[...] = buf[...].astype(BF16)
    d_gain, d_shift = norm_back(second, dec(10), d_in, cot, g_second)
    g_rows[...] = jnp.zeros(g_rows.shape, F32)
    g_rows[0:1, :] = d_gain
    g_rows[1:2, :] = d_shift
    g_rows[2:3, :] = column_sum(cot)


def second_kernel(
    io, table, t_len, langs, vecs, g_second, g_rows, memory,
    c_n, c_qe, c_qo, c_k, c_v, c_p, c_i, c_c, first, s_n, s_qe, s_qo, s_k, s_v, s_p, s_i, s_c, start,
    a0, a1, a2, a3, b0, b1, b2, b3,
    d_cross, d_self, d_cross_other, d_self_other, g_start, g_memory, g_vec,
    ws, wc, low, acc, u_t, m_t, g_first, d_even, d_odd, dc_t, q_t, c_t, dq, dk_t, dv_t, dk, dv, du, dm, sem,
):
    load(table, TAB_A, (a0, a1, a2, a3), ((9, 2, wc, 0, sem.at[1]),))
    load(table, TAB_B, (b0, b1, b2, b3), ((8, 2, wc, 2, sem.at[1]), (0, 4, ws, 0, sem.at[0])))
    scratch = (d_even, d_odd, dc_t, q_t, c_t, dq, dk_t, dv_t, dk, dv, du, dm)

    def dec(index):
        return vecs[DEC_VEC + index : DEC_VEC + index + 1, :]

    io.need(vecs, g_second, g_rows, memory, c_n)
    u_t[...] = c_n[...].T
    m_t[...] = memory[...].T
    low[...] = g_second[...].astype(BF16)
    io.need(c_qe, c_qo, c_k, c_v, c_p, c_i, c_c)
    arrived(wc, sem.at[1])
    bias_two = attn_back(
        low, u_t, m_t, wc, (c_qe, c_qo, c_k, c_v, c_p, c_i, c_c), scratch, acc,
        (d_cross, d_cross_other, table, TAB_A),
    )
    g_memory[...] = dm[...]
    io.send(g_memory, d_cross, d_cross_other)
    io.need(first)
    gain_two = norm_back(first, dec(5), du, g_second, g_first)
    low[...] = g_first[...].astype(BF16)
    io.need(s_n, s_qe, s_qo, s_k, s_v, s_p, s_i, s_c)
    u_t[...] = s_n[...].T
    arrived(ws, sem.at[0])
    bias_one = attn_back(
        low, u_t, u_t, ws, (s_qe, s_qo, s_k, s_v, s_p, s_i, s_c), scratch, acc,
        (d_self, d_self_other, table, TAB_B),
    )
    io.send(d_self, d_self_other)
    io.need(start)
    du[...] = du[...] + dm[...]
    gain_one = norm_back(start, dec(0), du, g_first, g_start)
    io.send(g_start)
    onehot = lang_onehot(t_len, langs)
    g_vec[...] = lax.dot_general(
        onehot, g_start[...].astype(BF16), (((0,), (0,)), ((), ())), preferred_element_type=F32
    )
    values = gain_one + bias_one + gain_two + bias_two
    for i, value in enumerate(values):
        g_vec[DEC_VEC + i : DEC_VEC + i + 1, :] = value
    g_vec[DEC_VEC + 10 : DEC_VEC + 13, :] = g_rows[0:3, :]


def third_kernel(
    io, table, vecs, b_enc, g_memory, e_mid, e_n2, a0, a1, a2, a3, t0, t1, t2, t3,
    d_in_own, d_out_own, d_other_in, d_other_out, g_mid, g_rows, b_grad,
    wi, wo, low, acc, u_t, act, dh, d_in, sem,
):
    load(table, TAB_A, (a0, a1, a2, a3), ((4, 4, wi, 0, sem.at[0]),))
    load_tall(table, (t0, t1, t2, t3), ((0, wo, sem.at[1]),))
    io.need(g_memory, e_n2)
    u_t[...] = e_n2[...].T
    low[...] = g_memory[...].astype(BF16)
    io.need(b_enc)
    arrived(wi, sem.at[0])
    arrived(wo, sem.at[1])
    feed_both(
        e_n2, u_t, wi, b_enc, Wide(wo), low, act, dh, None, d_in, acc,
        (d_in_own, d_other_in, table, TAB_A), (d_out_own, d_other_out, table), b_grad,
    )
    io.send(d_other_in, d_other_out, d_in_own, d_out_own)
    io.need(vecs, e_mid)
    gain = vecs[ENC_VEC + 5 : ENC_VEC + 6, :]
    d_gain, d_shift = norm_back(e_mid, gain, d_in, g_memory, g_mid)
    g_rows[...] = jnp.zeros(g_rows.shape, F32)
    g_rows[0:1, :] = d_gain
    g_rows[1:2, :] = d_shift
    g_rows[2:3, :] = column_sum(low)


def fourth_kernel(
    io, table, g_mid, e_n, e_qe, e_qo, e_k, e_v, e_p, e_i, e_c,
    vecs, source, g_rows, g_vec, g_bias_enc, g_bias_dec, a0, a1, a2, a3,
    d_own, d_other, g_source,
    we, buf, low, acc, u_t, all_vec, turned,
    d_even, d_odd, dc_t, q_t, c_t, dq, dk_t, dv_t, dk, dv, du, dm, sem,
):
    load(table, TAB_A, (a0, a1, a2, a3), ((0, 4, we, 0, sem.at[0]),))
    scratch = (d_even, d_odd, dc_t, q_t, c_t, dq, dk_t, dv_t, dk, dv, du, dm)
    io.need(g_mid, e_n, e_qe, e_qo, e_k, e_v, e_p, e_i, e_c)
    low[...] = g_mid[...].astype(BF16)
    u_t[...] = e_n[...].T
    arrived(we, sem.at[0])
    bias_one = attn_back(
        low, u_t, u_t, we, (e_qe, e_qo, e_k, e_v, e_p, e_i, e_c), scratch, acc,
        (d_own, d_other, table, TAB_B),
    )
    du[...] = du[...] + dm[...]
    io.need(vecs, source, g_rows, g_vec, g_bias_enc, g_bias_dec)
    buf[...] = source[...].astype(F32)
    gain_one = norm_back(buf, vecs[ENC_VEC : ENC_VEC + 1, :], du, g_mid, g_source)
    io.send(g_source)
    all_vec[...] = g_vec[...]
    for i, value in enumerate(gain_one + bias_one):
        all_vec[ENC_VEC + i : ENC_VEC + i + 1, :] = value
    all_vec[ENC_VEC + 5 : ENC_VEC + 8, :] = g_rows[0:3, :]
    turned[:, 0:128] = all_vec[...].T
    for block in range(BLOCKS):
        tile = rows(block // 2, 128)
        turned[rows(block, 16), 128:256] = jnp.broadcast_to(g_bias_enc[:, tile], (16, 128))
        turned[rows(block, 16), 256:384] = jnp.broadcast_to(g_bias_dec[:, tile], (16, 128))
        turned[rows(block, 16), 384:512] = jnp.zeros((16, 128), F32)
    put_blocks(turned, d_own, d_other, 4, table, TAB_B)


VM = pl.BlockSpec(memory_space=pltpu.VMEM)
SM = pl.BlockSpec(memory_space=pltpu.SMEM)
HB = pl.BlockSpec(memory_space=pl.ANY)
IN = object()


def act_shape(dtype=BF16):
    return ((SEQ, D), dtype)


KEPT = [act_shape()] * 5 + [((HEADS, SEQ, SEQ), BF16), act_shape(F32), act_shape()]


def call(body, args, specs, outs, scratch, flops):
    brought = [k for k, spec in enumerate(specs) if spec is IN]

    def kernel(*refs):
        refs = list(refs)
        ins, refs = refs[: len(args)], refs[len(args) :]
        targets, refs = refs[: len(outs)], refs[len(outs) :]
        staged_in, refs = refs[: len(brought)], refs[len(brought) :]
        staged_out, refs = refs[: len(outs)], refs[len(outs) :]
        sem, refs = refs[0], refs[1:]
        pairs_in = []
        for k, ref in zip(brought, staged_in):
            pairs_in.append((ins[k], ref))
            ins[k] = ref
        copies = Copies(pairs_in, list(zip(targets, staged_out)), sem)
        body(copies, *ins, *staged_out, *refs)
        copies.finish()

    buffers = [pltpu.VMEM(args[k].shape, args[k].dtype) for k in brought]
    buffers += [pltpu.VMEM(*out) for out in outs]
    buffers += [pltpu.SemaphoreType.DMA((len(brought) + len(outs),))]
    buffers += [
        pltpu.VMEM(*s) if isinstance(s, tuple) else pltpu.SemaphoreType.DMA((s,)) for s in scratch
    ]
    return pl.pallas_call(
        kernel,
        in_specs=[HB if spec is IN else spec for spec in specs],
        out_specs=[HB] * len(outs),
        out_shape=[jax.ShapeDtypeStruct(s, t) for s, t in outs],
        scratch_shapes=buffers,
        compiler_params=pltpu.CompilerParams(vmem_limit_bytes=63 * 1024 * 1024),
        cost_estimate=pl.CostEstimate(flops=flops, bytes_accessed=1 << 24, transcendentals=0),
    )(*args)


def plain_call(body, args, outs, scratch):
    return pl.pallas_call(
        body,
        in_specs=[SM] + [VM] * (len(args) - 1),
        out_specs=[VM] * len(outs),
        out_shape=[jax.ShapeDtypeStruct(s, t) for s, t in outs],
        scratch_shapes=[pltpu.VMEM(*s) for s in scratch],
        cost_estimate=pl.CostEstimate(flops=1 << 20, bytes_accessed=1 << 18, transcendentals=0),
    )(*args)


SQUARE = ((4, D, D), BF16)
TALL = ((128, 16, D), BF16)
NARROW = ((16, 4, 16, D), BF16)
HIGH = ((64, 16, D), BF16)
ACC = ((D, D), F32)
TURN = ((D, SEQ), BF16)
BIAS = ((SEQ, SEQ), F32)
BACK = [act_shape()] * 2 + [TURN] * 3 + [act_shape(), TURN, TURN, act_shape(), act_shape()]
BACK = BACK + [act_shape(F32)] * 2


def pairs(axis, step):
    k = AXES.index(axis)
    found = []

    def flat(place):
        index = 0
        for at, size in zip(place, SIZES):
            index = index * size + at
        return index

    for place in itertools.product(*[range(size) for size in SIZES]):
        if axis == "c":
            other = 1
        else:
            other = 1 if (step == 0) == (place[1] == 0) else 3
        target = list(place)
        target[k] = place[k] ^ other
        found.append((flat(place), flat(target)))
    return found


def swap(values, axis, step=0):
    return lax.ppermute(values, AXES, pairs(axis, step))


def away(core, order):
    hop = 1 if core == 0 else 3
    return (0, hop, 4 - hop, 2)[order]


def tables():
    found = []
    for x, c, y, z in itertools.product(*[range(size) for size in SIZES]):
        row_a, row_b, row_t, slots = [], [], [], [0] * 128
        for j in range(2):
            core = c ^ j
            for slot in range(16):
                one, two = away(core, slot % 4), away(core, slot // 4)
                row_a.append((x ^ one) * 8 + core * 4 + (y ^ two))
                row_b.append((x ^ two) * 8 + core * 4 + (y ^ one))
            for slot in range(64):
                at_x = x ^ away(core, slot % 4)
                at_y = y ^ away(core, slot // 4 % 4)
                at_z = z ^ away(core, slot // 16)
                block = ((at_x * 2 + core) * 4 + at_y) * 4 + at_z
                row_t.append(block)
                slots[block] = 64 * j + slot
        found.append(row_a + row_b + row_t + slots + [c])
    return np.array(found, np.int32)


def step_all(parts):
    received = [swap(*part) for part in parts]
    return lax.optimization_barrier(tuple(received))


def join(values, received):
    return jnp.concatenate([values, received], axis=0)


def by_z(mine, one, two):
    me, core = lax.axis_index("z"), lax.axis_index("c")
    found = []
    for z in range(4):
        distance = me ^ z
        odd = jnp.where(core == 0, distance == 1, distance == 3)
        part = jnp.where(odd, one, jnp.where(distance == 2, two[1], two[0]))
        found.append(jnp.where(distance == 0, mine, part))
    return jnp.stack(found, axis=1).reshape(mine.shape[0] * 16, D)


def gather(narrow, tall):
    z_one, got = step_all([(narrow, "z", 0), (tall, "x", 0)])
    tall = join(tall, got)
    z_two, got = step_all([(jnp.stack([narrow, z_one]), "z", 1), (tall, "x", 1)])
    tall = join(tall, got)
    both = by_z(narrow, z_one, z_two)
    one, two = both[: 11 * 16], both[11 * 16 :]
    for step in range(2):
        got = step_all([(one, "x", step), (two, "y", step), (tall, "y", step)])
        one, two, tall = join(one, got[0]), join(two, got[1]), join(tall, got[2])
    got = step_all([(one, "y", 0), (two, "x", 0), (tall, "z", 0)])
    one, two, tall = join(one, got[0]), join(two, got[1]), join(tall, got[2])
    low = (one, two, tall)
    got = step_all(
        [(one, "y", 1), (two, "x", 1), (tall, "z", 1), (one, "c", 0), (two, "c", 0), (tall, "c", 0)]
    )
    high, other_low = got[:3], got[3:]
    other_high = [swap(part, "c") for part in high]
    found = []
    for k, units in enumerate((11, 10, 2)):
        pieces = (low[k], high[k], other_low[k], other_high[k])
        found.append([piece.reshape(-1, units, 16, D) for piece in pieces])
    return found


def add(left, right, dtype=BF16):
    return (left.astype(F32) + right.astype(F32)).astype(dtype)


def fold(values, received, dtype=BF16):
    half = values.shape[0] // 2
    return add(values[:half], received[:half], dtype), add(values[half:], received[half:], dtype)


def z_parts(values):
    me, core = lax.axis_index("z"), lax.axis_index("c")
    parts = values.reshape(-1, 4, 4, D)
    hop = jnp.where(core == 0, 1, 3)
    found = []
    for distance in (0, hop, 4 - hop, 2):
        want = me ^ distance
        picked = parts[:, 3]
        for z in range(3):
            picked = jnp.where(want == z, parts[:, z], picked)
        found.append(picked)
    return jnp.stack(found[:2]), jnp.stack(found[2:])


def per_device(
    source, target, source_lengths, target_lengths, lang_ids, out_cotangent,
    enc_attn, enc_vectors, enc_w_in, enc_b_in, enc_w_out,
    dec_self, dec_cross, dec_vectors, dec_w_in, dec_b_in, dec_w_out, lang_table,
):
    spot = (lax.axis_index("z") + 4 * (lax.axis_index("y") % 2)).reshape(1)
    narrow, tall = plain_call(
        pack_kernel,
        (
            spot, enc_attn, enc_w_in, enc_w_out, dec_self, dec_cross, dec_w_in, dec_w_out,
            enc_vectors, dec_vectors, lang_table, enc_b_in.reshape(1, 16), dec_b_in.reshape(1, 16),
        ),
        [((21, 4, D), BF16), ((2, 16, D), BF16)],
        [((128, 128), F32)],
    )
    ga, gb, gt = gather(narrow, tall.reshape(32, D))
    me = lax.axis_index(AXES)
    table = lax.dynamic_index_in_dim(jnp.asarray(tables()), me, 0, keepdims=False)
    results = call(
        first_kernel,
        (
            table, source_lengths, target_lengths, lang_ids,
            source[0], target[0], out_cotangent[0], *ga, *gb, *gt,
        ),
        [SM] * 4 + [IN] * 3 + [HB] * 12,
        [act_shape(), NARROW, HIGH, NARROW, HIGH, act_shape(F32), ((8, D), F32), ((1, FF), F32)]
        + [((128, D), F32), ((1, FF), F32)]
        + KEPT
        + [act_shape(F32), act_shape(), act_shape()]
        + [act_shape(F32)]
        + KEPT
        + [act_shape(F32)]
        + KEPT,
        [((1, D, D), BF16), SQUARE, SQUARE, TALL, SQUARE, SQUARE, SQUARE, TALL, BIAS, BIAS, BIAS]
        + [act_shape(F32), act_shape(F32), act_shape(), TURN, act_shape(), act_shape(), act_shape(F32)]
        + [ACC, ((1, FF), F32), 8],
        12 * 10**9,
    )
    dec_out, p_one, r_one, p_one_other, r_one_other, g_second, g_rows, g_bias_dec, vecs, b_enc = (
        results[:10]
    )
    rest = results[10:]
    enc_kept, e_mid, e_n2, memory = rest[:8], rest[8], rest[9], rest[10]
    start, self_kept, first, cross_kept = rest[11], rest[12:20], rest[20], rest[21:29]

    p_got, r_got = swap(p_one_other, "c"), swap(r_one_other, "c")
    (
        p_two, q_two, p_two_other, q_two_other, g_start, g_memory, g_vec,
    ) = call(
        second_kernel,
        (
            table, target_lengths, lang_ids, vecs, g_second, g_rows, memory,
            *cross_kept, first, *self_kept, start, *ga, *gb,
        ),
        [SM] * 3 + [IN] * 22 + [HB] * 8,
        [NARROW] * 4 + [act_shape(F32), act_shape(F32), ((128, D), F32)],
        [SQUARE, SQUARE, act_shape(), ACC, TURN, TURN, act_shape(F32)] + BACK + [2],
        6 * 10**9,
    )
    p_low, p_high = fold(p_one, p_got)
    r_low, r_high = fold(r_one, r_got)
    p_low, p_high, r_low, r_high, g_memory = lax.optimization_barrier(
        (p_low, p_high, r_low, r_high, g_memory)
    )
    p_got, r_got = swap(p_high, "y", 1), swap(r_high, "z", 1)
    two_got = swap(p_two_other, "c"), swap(q_two_other, "c")
    (
        p_three, r_three, p_three_other, r_three_other, g_mid, g_rows, g_bias_enc,
    ) = call(
        third_kernel,
        (table, vecs, b_enc, g_memory, e_mid, e_n2, *ga, *gt),
        [SM] + [IN] * 5 + [HB] * 8,
        [NARROW, HIGH, NARROW, HIGH, act_shape(F32), ((8, D), F32), ((1, FF), F32)],
        [SQUARE, TALL, act_shape(), ACC, TURN, act_shape(), act_shape(), act_shape(F32), 2],
        4 * 10**9,
    )
    p_low, p_high = fold(p_low, p_got)
    r_low, r_high = fold(r_low, r_got)
    p2_low, p2_high = fold(p_two, two_got[0])
    q2_low, q2_high = fold(q_two, two_got[1])
    p_low, p_high, r_low, r_high, p2_low, p2_high, q2_low, q2_high, g_mid = lax.optimization_barrier(
        (p_low, p_high, r_low, r_high, p2_low, p2_high, q2_low, q2_high, g_mid)
    )
    p_got, r_got = swap(p_high, "y", 0), swap(r_high, "z", 0)
    p2_got, q2_got = swap(p2_high, "y", 1), swap(q2_high, "x", 1)
    three_got = swap(p_three_other, "c"), swap(r_three_other, "c")
    q_four, q_four_other, g_source = call(
        fourth_kernel,
        (table, g_mid, *enc_kept, vecs, source[0], g_rows, g_vec, g_bias_enc, g_bias_dec, *ga),
        [SM] + [IN] * 15 + [HB] * 4,
        [((16, 5, 16, D), BF16)] * 2 + [act_shape(F32)],
        [SQUARE, act_shape(F32), act_shape(), ACC, TURN, ((128, D), F32), ACC] + BACK + [1],
        4 * 10**9,
    )
    p1 = add(p_low, p_got)
    r1 = add(r_low, r_got)
    p2_low, p2_high = fold(p2_low, p2_got)
    q2_low, q2_high = fold(q2_low, q2_got)
    p3_low, p3_high = fold(p_three, three_got[0])
    r3_low, r3_high = fold(r_three, three_got[1])
    q4_got, p2_got, q2_got, p3_got, r3_got = step_all(
        [
            (q_four_other, "c", 0), (p2_high, "y", 0), (q2_high, "x", 0),
            (p3_high, "y", 1), (r3_high, "z", 1),
        ]
    )
    p2 = add(p2_low, p2_got)
    q2 = add(q2_low, q2_got)
    p3_low, p3_high = fold(p3_low, p3_got)
    r3_low, r3_high = fold(r3_low, r3_got)
    q4_low, q4_high = fold(q_four, q4_got)
    q4_got, p3_got, r3_got = step_all([(q4_high, "x", 1), (p3_high, "y", 0), (r3_high, "z", 0)])
    q4_low, q4_high = fold(q4_low, q4_got)
    p = jnp.concatenate([p1, p2, add(p3_low, p3_got)], axis=1)
    r = jnp.stack([r1, add(r3_low, r3_got)], axis=1)
    q4_got, p_got, r_got = step_all([(q4_high, "x", 0), (p[2:], "x", 1), (r[8:], "y", 1)])
    q = jnp.concatenate([q2, add(q4_low, q4_got)], axis=1)
    p_low, p_high = fold(p[:2], p_got)
    r_low, r_high = fold(r[:8], r_got)
    q_got, p_got, r_got = step_all([(q[2:], "y", 1), (p_high, "x", 0), (r_high, "y", 0)])
    q_low, q_high = fold(q[:2], q_got)
    p = add(p_low, p_got)
    r = add(r_low, r_got)
    p_near, p_far = z_parts(p[0])
    q_got, p_got, r_got = step_all([(q_high, "y", 0), (p_far, "z", 1), (r[2:], "x", 1)])
    q_near, q_far = z_parts(add(q_low, q_got)[0])
    p_low, p_high = fold(p_near, p_got)
    r_low, r_high = fold(r[:2], r_got)
    q_got, p_got, r_got = step_all([(q_far, "z", 1), (p_high, "z", 0), (r_high, "x", 0)])
    q_low, q_high = fold(q_near, q_got)
    q_got = swap(q_high, "z", 0)
    quarter, four = ((4, FF), F32), ((4, 4, D), F32)
    (
        d_attn, d_vec_e, d_w_in, d_b_e, d_w_out, d_self, d_cross, d_vec_d, d_dec_in, d_b_d, d_dec_out, d_lang,
    ) = plain_call(
        unpack_kernel,
        (spot, p_low, p_got, q_low, q_got, r_low, r_got),
        [four, ((4, 8), F32), quarter, ((1, 16), F32), ((16, D), F32), four, four]
        + [((4, 13), F32), quarter, ((1, 16), F32), ((16, D), F32), ((4, LANGS), F32)],
        [((4, D), F32)],
    )
    return (
        dec_out[None],
        g_source[None],
        g_start[None],
        d_attn,
        d_vec_e.T,
        d_w_in,
        d_b_e.reshape(16),
        d_w_out,
        d_self,
        d_cross,
        d_vec_d.T,
        d_dec_in,
        d_b_d.reshape(16),
        d_dec_out,
        d_lang.T,
    )


def solution(mesh):
    fine = Mesh(mesh.devices.reshape(SIZES), AXES)
    flat = AXES
    in_specs = (
        P(flat, None, None),
        P(flat, None, None),
        P(flat, None),
        P(flat, None),
        P(flat, None),
        P(flat, None, None),
        P(None, flat, None),
        P(None, flat),
        P(flat, None),
        P(flat),
        P(flat, None),
        P(None, flat, None),
        P(None, flat, None),
        P(None, flat),
        P(flat, None),
        P(flat),
        P(flat, None),
        P(None, flat),
    )
    out_specs = (
        P(flat, None, None),
        P(flat, None, None),
        P(flat, None, None),
        P(None, flat, None),
        P(None, flat),
        P(flat, None),
        P(flat),
        P(flat, None),
        P(None, flat, None),
        P(None, flat, None),
        P(None, flat),
        P(flat, None),
        P(flat),
        P(flat, None),
        P(None, flat),
    )
    return jax.shard_map(
        per_device, mesh=fine, in_specs=in_specs, out_specs=out_specs, check_vma=False
    )
```

```python
import itertools

import jax
import jax.numpy as jnp
import numpy as np
from jax import lax
from jax.experimental import pallas as pl
from jax.experimental.pallas import tpu as pltpu
from jax.sharding import Mesh
from jax.sharding import PartitionSpec as P

D = 512
HEADS = 8
HEAD_DIM = 64
FF = 2048
LANGS = 100
SEQ = 384
DOCS = 5
EPSILON = 1e-05
NEGATIVE = -1000000000.0
OPEN = 3e38
SCALE = HEAD_DIM ** (-0.5)
AXES = ("x", "c", "y", "z")
SIZES = (4, 2, 4, 4)
BLOCKS = 32
ENC_VEC = 104
DEC_VEC = 112
CHUNK = 128
CHUNKS = SEQ // CHUNK
TAB_A, TAB_B, SLOT_A, SLOT_B, CORE = 0, 32, 64, 96, 128
F32 = jnp.float32
BF16 = jnp.bfloat16


def dot(left, right):
    return lax.dot_general(left, right, (((1,), (0,)), ((), ())), preferred_element_type=F32)


def dot_nt(left, right):
    return lax.dot_general(left, right, (((1,), (1,)), ((), ())), preferred_element_type=F32)


def rows(index, size=CHUNK):
    return slice(index * size, (index + 1) * size)


def normed(values):
    mean = jnp.mean(values, axis=-1, keepdims=True)
    center = values - mean
    rstd = lax.rsqrt(jnp.mean(center * center, axis=-1, keepdims=True) + EPSILON)
    return center * rstd, rstd


def layer_norm(source, gain, shift, out):
    for i in range(CHUNKS):
        hat, _ = normed(source[rows(i), :])
        out[rows(i), :] = (hat * gain + shift).astype(BF16)


def norm_back(source, gain, grad, base, out):
    d_gain = jnp.zeros((1, D), F32)
    d_shift = jnp.zeros((1, D), F32)
    for i in range(CHUNKS):
        hat, rstd = normed(source[rows(i), :])
        dy = grad[rows(i), :]
        d_gain = d_gain + jnp.sum(dy * hat, axis=0, keepdims=True)
        d_shift = d_shift + jnp.sum(dy, axis=0, keepdims=True)
        dyg = dy * gain
        mean_one = jnp.mean(dyg, axis=-1, keepdims=True)
        mean_two = jnp.mean(dyg * hat, axis=-1, keepdims=True)
        out[rows(i), :] = base[rows(i), :].astype(F32) + rstd * (dyg - mean_one - hat * mean_two)
    return d_gain, d_shift


def low_lanes(count):
    return lax.broadcasted_iota(jnp.int32, (count, 128), 1) < HEAD_DIM


def head_mask():
    lane = lax.broadcasted_iota(jnp.int32, (1, D), 1)
    return ((lane // HEAD_DIM) % 2 == 0).astype(F32)


def doc_ids(lengths, shape, axis):
    position = lax.broadcasted_iota(jnp.int32, shape, axis)
    total = jnp.zeros(shape, jnp.int32)
    end = 0
    for i in range(DOCS):
        end = end + lengths[0, i]
        total = total + (position >= end).astype(jnp.int32)
    return total


def masks(s_len, t_len, bias_s, bias_c):
    s_row = doc_ids(s_len, (1, SEQ), 1)
    t_row = doc_ids(t_len, (1, SEQ), 1)
    t_col = doc_ids(t_len, (SEQ, 1), 0)
    key = lax.broadcasted_iota(jnp.int32, (SEQ, SEQ), 1)
    query = lax.broadcasted_iota(jnp.int32, (SEQ, SEQ), 0)
    bias_s[...] = jnp.where((t_col == t_row) & (key <= query), OPEN, NEGATIVE)
    bias_c[...] = jnp.where(t_col == s_row, OPEN, NEGATIVE)


def lang_onehot(t_len, langs):
    doc = doc_ids(t_len, (SEQ, 128), 0)
    lang = jnp.zeros((SEQ, 128), jnp.int32)
    for i in range(DOCS):
        lang = jnp.where(doc == i, langs[0, i], lang)
    lane = lax.broadcasted_iota(jnp.int32, (SEQ, 128), 1)
    return jnp.where(lang == lane, 1.0, 0.0).astype(BF16)


def attn_project(query_in, memory, weights, bias_q, bias_v, q_even, q_odd, keys, values):
    even = head_mask()
    q = SCALE * (dot(query_in[...], weights[0]) + bias_q)
    q_even[...] = (q * even).astype(BF16)
    q_odd[...] = (q * (1.0 - even)).astype(BF16)
    keys[...] = dot(memory[...], weights[1]).astype(BF16)
    values[...] = (dot(memory[...], weights[2]) + bias_v).astype(BF16)


def attn_core(q_even, q_odd, keys, values, bias, probs, inverse, context):
    low = low_lanes(SEQ)
    queries = (q_even, q_odd)
    held = []

    def lanes(head):
        return rows(head // 2, 128)

    def scores(head):
        return dot_nt(queries[head % 2][:, lanes(head)], keys[:, lanes(head)])

    def finish(head, e, total):
        over = 1.0 / total
        held.append((dot(e, values[:, lanes(head)]) * over, over))
        if head % 2 == 1:
            (one, over_one), (two, over_two) = held
            held.clear()
            context[:, lanes(head)] = jnp.where(low, one, two).astype(BF16)
            inverse[:, lanes(head)] = jnp.where(low, over_one, over_two)

    s = scores(0)
    last = None
    for head in range(HEADS):
        s_next = scores(head + 1) if head + 1 < HEADS else None
        s = jnp.minimum(s, bias[...])
        e = jnp.exp(s - jnp.max(s, axis=-1, keepdims=True))
        total = jnp.sum(e, axis=-1, keepdims=True)
        e = e.astype(BF16)
        probs[head] = e
        if last is not None:
            finish(*last)
        last = (head, e, total)
        s = s_next
    finish(*last)


def attn_output(context, weight, bias_o, residual, out):
    branch = dot(context[...], weight[...]) + bias_o
    out[...] = residual[...].astype(F32) + branch


def put_blocks(acc, place):
    refs, units, table, first = place
    for slot in range(16):
        for j in range(2):
            start = pl.multiple_of(table[first + 16 * j + slot] * 16, 16)
            refs[j][slot, units[j]] = acc[pl.ds(start, 16), :].astype(BF16)


def place_of(own, other, unit, shift, table, first):
    return (own, other), (unit, unit + shift), table, first


def weight_grad(left_t, right, acc, place, scale=None):
    value = dot(left_t[...], right[...])
    acc[...] = value if scale is None else value * scale
    put_blocks(acc, place)


def tall_grad(left_t, right, acc, place, chunk):
    refs, units, table, slots = place
    acc[...] = dot(left_t, right[...])
    for j in range(2):
        core = table[CORE] ^ j
        for y in range(4):
            slot = table[slots + chunk * 8 + core * 4 + y] - 16 * j
            for z in range(4):
                start = pl.multiple_of(core * 256 + y * 64 + z * 16, 16)
                refs[j][slot, units[j] + z] = acc[pl.ds(start, 16), :].astype(BF16)


def column_sum(ref):
    return jnp.sum(ref[...].astype(F32), axis=0, keepdims=True)


def attn_back(grad, query_in_t, memory_t, weights, kept, scratch, acc, places):
    q_even, q_odd, keys, values, probs, inverse, context = kept
    d_even, d_odd, dc_t, q_t, c_t, dq, dk_t, dv_t, dk, dv, du, dm = scratch
    even = head_mask()
    dc = dot_nt(grad[...], weights[3]) * inverse[...]
    d_even[...] = (dc * even).astype(BF16)
    d_odd[...] = (dc * (1.0 - even)).astype(BF16)
    dc_t[...] = (d_even[...] + d_odd[...]).T
    q_t[...] = (q_even[...] + q_odd[...]).T
    c_t[...] = context[...].T
    low = low_lanes(SEQ)
    d_ctx = (d_even, d_odd)
    held = []

    def lanes(head):
        return rows(head // 2, 128)

    def first(head):
        dch = d_ctx[head % 2][:, lanes(head)]
        total = jnp.sum(
            dch.astype(F32) * context[:, lanes(head)].astype(F32), axis=-1, keepdims=True
        )
        return dot_nt(dch, values[:, lanes(head)]), total

    def finish(head, ds):
        span = rows(head, HEAD_DIM)
        held.append(dot(ds, keys[:, lanes(head)]))
        dk_t[span, :] = dot(q_t[span, :], ds).astype(BF16)
        dv_t[span, :] = dot(dc_t[span, :], probs[head]).astype(BF16)
        if head % 2 == 1:
            dq[:, lanes(head)] = jnp.where(low, held[0], held[1]).astype(BF16)
            held.clear()

    now = first(0)
    last = None
    for head in range(HEADS):
        later = first(head + 1) if head + 1 < HEADS else None
        dp, total = now
        ds = (probs[head].astype(F32) * (dp - total)).astype(BF16)
        if last is not None:
            finish(*last)
        last = (head, ds)
        now = later
    finish(*last)
    dk[...] = dk_t[...].T
    dv[...] = dv_t[...].T
    weight_grad(query_in_t, dq, acc, places[0], SCALE)
    weight_grad(memory_t, dk, acc, places[1])
    weight_grad(memory_t, dv, acc, places[2])
    weight_grad(c_t, grad, acc, places[3])
    du[...] = SCALE * dot_nt(dq[...], weights[0])
    dm[...] = dot_nt(dk[...], weights[1]) + dot_nt(dv[...], weights[2])
    return SCALE * column_sum(dq), column_sum(dv), column_sum(grad)


def silu_parts(hidden):
    gate = 1.0 / (1.0 + jnp.exp(-hidden))
    return hidden * gate, gate


def feed_forward(inputs, w_in, b_in, w_out, bias, residual, out):
    total = residual[...] + bias
    for k in range(FF // D):
        active, _ = silu_parts(dot(inputs[...], w_in[k]) + b_in[:, rows(k, D)])
        total = total + dot(active.astype(BF16), w_out[k])
    out[...] = total


def feed_both(
    inputs, inputs_t, w_in, b_in, w_out, grad, act, dh, total, d_in, acc, places_in, place_out, b_grad
):
    hidden = dot(inputs[...], w_in[0]) + b_in[:, rows(0, D)]
    for k in range(FF // D):
        d_act = dot_nt(grad[...], w_out[k])
        active, gate = silu_parts(hidden)
        low = active.astype(BF16)
        act[...] = low
        d_hid = (d_act * (gate + active * (1.0 - gate))).astype(BF16)
        dh[...] = d_hid
        if k + 1 < FF // D:
            hidden = dot(inputs[...], w_in[k + 1]) + b_in[:, rows(k + 1, D)]
        if total is not None:
            total[...] = total[...] + dot(low, w_out[k])
        back = dot_nt(d_hid, w_in[k])
        d_in[...] = back if k == 0 else d_in[...] + back
        b_grad[:, rows(k, D)] = column_sum(dh)
        weight_grad(inputs_t, dh, acc, places_in[k])
        tall_grad(act[...].T, grad, acc, place_out, k)


def load(table, first, pieces, jobs):
    def step(slot, carry):
        for k, piece in enumerate(pieces):
            block = table[first + 8 * k + slot]
            start = pl.multiple_of(block * 16, 16)
            for unit, count, target, row, sem in jobs:
                if len(target.shape) == 4:
                    place = target.at[block]
                else:
                    place = target.at[pl.ds(row, count), pl.ds(start, 16), :]
                pltpu.make_async_copy(piece.at[slot, pl.ds(unit, count)], place, sem).start()
        return carry

    lax.fori_loop(0, 8, step, 0)


def arrived(target, sem):
    pltpu.make_async_copy(target, target, sem).wait()


class Wide:
    def __init__(self, ref):
        self.ref = ref

    def __getitem__(self, k):
        return self.ref[8 * k : 8 * k + 8].reshape(D, D)


def pack_kernel(
    spot, attn, w_in, w_out, self_w, cross, dec_in, dec_out, vec_e, vec_d, lang, b_e, b_d,
    packed, wide, buf,
):
    for k in range(4):
        buf[rows(k, 4), :] = attn[k].astype(F32)
        buf[rows(4 + k if k < 2 else 5 + k, 4), :] = w_in[:, rows(k, D)].astype(F32)
        buf[rows(9 + k, 4), :] = self_w[k].astype(F32)
        buf[rows(13 + k, 4), :] = cross[k].astype(F32)
        buf[rows(17 + k, 4), :] = dec_in[:, rows(k, D)].astype(F32)
    buf[84:96, :] = jnp.zeros((12, D), F32)
    buf[96:112, :] = w_out[...].astype(F32)
    buf[112:128, :] = dec_out[...].astype(F32)
    wide[...] = jnp.zeros(wide.shape, F32)
    wide[0:4, 0:LANGS] = lang[...].astype(F32)
    wide[0:4, ENC_VEC : ENC_VEC + 8] = vec_e[...].astype(F32)
    wide[0:4, DEC_VEC : DEC_VEC + 13] = vec_d[...].astype(F32)
    row = lax.broadcasted_iota(jnp.int32, (16, 128), 0)
    lane = lax.broadcasted_iota(jnp.int32, (16, 128), 1)
    place = jnp.where(lane == row + spot[0] * 16, 1.0, 0.0).astype(BF16)
    first = lax.broadcasted_iota(jnp.int32, (8, 128), 0) == 0
    buf[24:28, 0:128] = wide[0:4, :]
    for k, ref in enumerate((b_e, b_d)):
        spread = dot(jnp.broadcast_to(ref[...].astype(F32), (8, 16)).astype(BF16), place)
        wide[0:8, :] = jnp.where(first, spread, 0.0)
        buf[24:28, 128 + 128 * k : 256 + 128 * k] = wide[0:4, :]
    buf[24:28, 384:512] = jnp.zeros((4, 128), F32)
    packed[...] = buf[...].astype(BF16)


def unpack_kernel(
    spot, low, got,
    attn, vec_e, w_in, b_e, w_out, self_w, cross, vec_d, dec_in, b_d, dec_out, lang,
    last,
):
    def total(one, two, index):
        return one[0, index].astype(F32) + two[0, index].astype(F32)

    for k in range(4):
        dec_in[:, rows(k, D)] = total(low, got, k)
        cross[k] = total(low, got, 4 + k if k < 2 else 16 + k)
        w_in[:, rows(k, D)] = total(low, got, 6 + k)
        w_out[rows(k, 4), :] = total(low, got, 10 + k)
        self_w[k] = total(low, got, 14 + k)
        dec_out[rows(k, 4), :] = total(low, got, 20 + k)
        attn[k] = total(low, got, 24 + k)
    last[...] = total(low, got, 28)
    lang[...] = last[:, 0:LANGS]
    vec_e[...] = last[:, ENC_VEC : ENC_VEC + 8]
    vec_d[...] = last[:, DEC_VEC : DEC_VEC + 13]
    for k, ref in enumerate((b_e, b_d)):
        tile = jnp.broadcast_to(last[0:1, 128 + 128 * k : 256 + 128 * k], (8, 128))
        ref[...] = pltpu.roll(tile, 128 - 16 * spot[0], 1)[0:1, 0:16]


class Copies:
    def __init__(self, incoming, outgoing, sem):
        self.waiting = {}
        self.flying = {}
        self.outgoing = {}
        self.sent = {}
        for index, (hbm, vmem) in enumerate(incoming):
            self.waiting[id(vmem)] = pltpu.make_async_copy(hbm, vmem, sem.at[index])
        for index, (hbm, vmem) in enumerate(outgoing):
            place = sem.at[len(incoming) + index]
            self.outgoing[id(vmem)] = pltpu.make_async_copy(vmem, hbm, place)

    def bring(self, *refs):
        for ref in refs:
            copy = self.waiting.pop(id(ref))
            copy.start()
            self.flying[id(ref)] = copy

    def need(self, *refs):
        for ref in refs:
            self.flying.pop(id(ref)).wait()

    def send(self, *refs):
        for ref in refs:
            copy = self.outgoing.pop(id(ref))
            copy.start()
            self.sent[id(ref)] = copy

    def free(self, *refs):
        for ref in refs:
            copy = self.sent.pop(id(ref))
            copy.wait()

    def finish(self):
        assert not self.waiting and not self.flying
        for copy in self.outgoing.values():
            copy.start()
        for copy in list(self.sent.values()) + list(self.outgoing.values()):
            copy.wait()


def encoder_kernel(
    io, table, s_len, source, a0, a1, a2, a3, b0, b1, b2, b3,
    vecs, b_enc, b_dec, e_n, e_qe, e_qo, e_k, e_v, e_p, e_i, e_c, e_mid, e_n2, memory,
    small, we, wi, wo, bias_e, buf, sem,
):
    io.bring(source)
    load(table, TAB_A, (a0, a1, a2, a3), ((6, 1, small, 0, sem.at[3]), (0, 4, we, 0, sem.at[0])))
    load(table, TAB_B, (b0, b1, b2, b3), ((0, 2, wi, 2, sem.at[1]), (2, 4, wo, 0, sem.at[2])))
    load(table, TAB_A, (a0, a1, a2, a3), ((4, 2, wi, 0, sem.at[1]),))
    s_row = doc_ids(s_len, (1, SEQ), 1)
    s_col = doc_ids(s_len, (SEQ, 1), 0)
    bias_e[...] = jnp.where(s_col == s_row, OPEN, NEGATIVE)
    arrived(small, sem.at[3])
    vecs[...] = small[0, :, 0:128].astype(F32).T
    for k, ref in enumerate((b_enc, b_dec)):
        for tile in range(FF // 128):
            part = small[0, rows(tile, 32), 128 + 128 * k : 256 + 128 * k].astype(F32)
            ref[:, rows(tile, 128)] = jnp.sum(part, axis=0, keepdims=True)

    def enc(index):
        return vecs[ENC_VEC + index : ENC_VEC + index + 1, :]

    io.need(source)
    buf[...] = source[...].astype(F32)
    layer_norm(buf, enc(0), enc(1), e_n)
    arrived(we, sem.at[0])
    attn_project(e_n, e_n, we, enc(2), enc(3), e_qe, e_qo, e_k, e_v)
    attn_core(e_qe, e_qo, e_k, e_v, bias_e, e_p, e_i, e_c)
    io.send(vecs, b_enc, b_dec, e_n, e_qe, e_qo, e_k, e_v, e_p, e_i, e_c)
    attn_output(e_c, we.at[3], enc(4), source, e_mid)
    layer_norm(e_mid, enc(5), enc(6), e_n2)
    io.send(e_mid, e_n2)
    arrived(wi, sem.at[1])
    arrived(wo, sem.at[2])
    feed_forward(e_n2, wi, b_enc, Wide(wo), enc(7), e_mid, buf)
    memory[...] = buf[...].astype(BF16)


def first_kernel(
    io, table, s_len, t_len, langs, vecs, target, memory, cot, b_dec,
    a0, a1, a2, a3, b0, b1, b2, b3,
    dec_out, d_p, d_q, d_other, g_start, g_memory, g_vec, g_bias,
    s_n, s_qe, s_qo, s_k, s_v, s_p, s_i, s_c, c_n, c_qe, c_qo, c_k, c_v, c_p, c_i, c_c,
    ws, wc, vi, vo, bias_s, bias_c, buf, start, first, second, n3,
    act, dh, d_in, g_first, acc, u_t, m_t, low,
    d_even, d_odd, dc_t, q_t, c_t, dq, dk_t, dv_t, dk, dv, du, dm, sem,
):
    io.bring(vecs, target)
    load(table, TAB_A, (a0, a1, a2, a3), ((0, 4, ws, 0, sem.at[0]),))
    masks(s_len, t_len, bias_s, bias_c)
    onehot = lang_onehot(t_len, langs)
    io.need(vecs, target)
    io.bring(memory, cot, b_dec)
    load(table, TAB_B, (b0, b1, b2, b3), ((0, 4, wc, 0, sem.at[1]), (4, 4, vi, 0, sem.at[2])))
    load(table, TAB_A, (a0, a1, a2, a3), ((4, 4, vo, 0, sem.at[3]),))

    def dec(index):
        return vecs[DEC_VEC + index : DEC_VEC + index + 1, :]

    start[...] = target[...].astype(F32) + dot(onehot, vecs[...].astype(BF16))
    layer_norm(start, dec(0), dec(1), s_n)
    arrived(ws, sem.at[0])
    attn_project(s_n, s_n, ws, dec(2), dec(3), s_qe, s_qo, s_k, s_v)
    attn_core(s_qe, s_qo, s_k, s_v, bias_s, s_p, s_i, s_c)
    attn_output(s_c, ws.at[3], dec(4), start, first)
    layer_norm(first, dec(5), dec(6), c_n)
    io.need(memory, cot, b_dec)
    arrived(wc, sem.at[1])
    attn_project(c_n, memory, wc, dec(7), dec(8), c_qe, c_qo, c_k, c_v)
    attn_core(c_qe, c_qo, c_k, c_v, bias_c, c_p, c_i, c_c)
    attn_output(c_c, wc.at[3], dec(9), first, second)
    layer_norm(second, dec(10), dec(11), n3)
    u_t[...] = n3[...].T
    buf[...] = second[...] + dec(12)
    arrived(vi, sem.at[2])
    arrived(vo, sem.at[3])

    def in_p(unit):
        return place_of(d_p, d_other, unit, 0, table, TAB_A)

    def in_q(unit):
        return place_of(d_q, d_other, unit, 6, table, TAB_B)

    feed_both(
        n3, u_t, vi, b_dec, Wide(vo), cot, act, dh, buf, d_in, acc,
        [in_p(k) for k in range(4)], place_of(d_q, d_other, 6, 6, table, SLOT_B), g_bias,
    )
    dec_out[...] = buf[...].astype(BF16)
    io.send(dec_out, g_bias)
    g_second = second
    gain_three = norm_back(second, dec(10), d_in, cot, g_second)
    scratch = (d_even, d_odd, dc_t, q_t, c_t, dq, dk_t, dv_t, dk, dv, du, dm)
    u_t[...] = c_n[...].T
    m_t[...] = memory[...].T
    low[...] = g_second[...].astype(BF16)
    bias_two = attn_back(
        low, u_t, m_t, wc, (c_qe, c_qo, c_k, c_v, c_p, c_i, c_c), scratch, acc,
        [in_p(4), in_p(5), in_q(4), in_q(5)],
    )
    io.send(d_p)
    g_memory[...] = dm[...]
    io.send(g_memory)
    gain_two = norm_back(first, dec(5), du, g_second, g_first)
    low[...] = g_first[...].astype(BF16)
    u_t[...] = s_n[...].T
    bias_one = attn_back(
        low, u_t, u_t, ws, (s_qe, s_qo, s_k, s_v, s_p, s_i, s_c), scratch, acc,
        [in_q(k) for k in range(4)],
    )
    io.send(d_other, d_q)
    du[...] = du[...] + dm[...]
    gain_one = norm_back(start, dec(0), du, g_first, g_start)
    io.send(g_start)
    g_vec[...] = lax.dot_general(
        onehot, g_start[...].astype(BF16), (((0,), (0,)), ((), ())), preferred_element_type=F32
    )
    values = gain_one + bias_one + gain_two + bias_two + gain_three + (column_sum(cot),)
    for i, value in enumerate(values):
        g_vec[DEC_VEC + i : DEC_VEC + i + 1, :] = value


def second_kernel(
    io, table, g_memory, e_n2, b_enc, vecs, e_mid, e_n, e_qe, e_qo, e_k, e_v, e_p, e_i, e_c,
    source, g_vec, g_bias_dec, a0, a1, a2, a3, b0, b1, b2, b3,
    d_p, d_q, d_other, g_source,
    we, wi, wo, buf, low, acc, u_t, act, dh, d_in, g_mid, b_grad, all_vec, turned,
    d_even, d_odd, dc_t, q_t, c_t, dq, dk_t, dv_t, dk, dv, du, dm, sem,
):
    io.bring(g_memory, e_n2, b_enc)
    load(table, TAB_A, (a0, a1, a2, a3), ((4, 2, wi, 0, sem.at[0]),))
    load(table, TAB_B, (b0, b1, b2, b3), ((0, 2, wi, 2, sem.at[0]), (2, 4, wo, 0, sem.at[1])))
    io.need(g_memory, e_n2, b_enc)
    u_t[...] = e_n2[...].T
    low[...] = g_memory[...].astype(BF16)
    bias_out = column_sum(low)
    arrived(wi, sem.at[0])
    arrived(wo, sem.at[1])
    io.bring(vecs, e_mid, e_n)
    load(table, TAB_A, (a0, a1, a2, a3), ((0, 4, we, 0, sem.at[2]),))
    io.bring(e_i, e_qe, e_qo, e_c, e_v, e_k, e_p, source, g_vec, g_bias_dec)

    def in_p(unit):
        return place_of(d_p, d_other, unit, 0, table, TAB_A)

    def in_q(unit):
        return place_of(d_q, d_other, unit, 8, table, TAB_B)

    feed_both(
        e_n2, u_t, wi, b_enc, Wide(wo), low, act, dh, None, d_in, acc,
        [in_p(k) for k in range(4)], place_of(d_p, d_other, 4, 0, table, SLOT_A), b_grad,
    )
    io.send(d_p)
    io.need(vecs, e_mid, e_n)
    gain_two = norm_back(e_mid, vecs[ENC_VEC + 5 : ENC_VEC + 6, :], d_in, g_memory, g_mid)
    low[...] = g_mid[...].astype(BF16)
    u_t[...] = e_n[...].T
    io.need(e_i, e_qe, e_qo, e_c, e_v, e_k, e_p)
    arrived(we, sem.at[2])
    scratch = (d_even, d_odd, dc_t, q_t, c_t, dq, dk_t, dv_t, dk, dv, du, dm)
    bias_one = attn_back(
        low, u_t, u_t, we, (e_qe, e_qo, e_k, e_v, e_p, e_i, e_c), scratch, acc,
        [in_q(k) for k in range(4)],
    )
    du[...] = du[...] + dm[...]
    io.need(source, g_vec, g_bias_dec)
    buf[...] = source[...].astype(F32)
    gain_one = norm_back(buf, vecs[ENC_VEC : ENC_VEC + 1, :], du, g_mid, g_source)
    io.send(g_source)
    all_vec[...] = g_vec[...]
    for i, value in enumerate(gain_one + bias_one + gain_two + (bias_out,)):
        all_vec[ENC_VEC + i : ENC_VEC + i + 1, :] = value
    turned[:, 0:128] = all_vec[...].T
    for block in range(BLOCKS):
        tile = rows(block // 2, 128)
        turned[rows(block, 16), 128:256] = jnp.broadcast_to(b_grad[:, tile], (16, 128))
        turned[rows(block, 16), 256:384] = jnp.broadcast_to(g_bias_dec[:, tile], (16, 128))
        turned[rows(block, 16), 384:512] = jnp.zeros((16, 128), F32)
    put_blocks(turned, in_q(4))


VM = pl.BlockSpec(memory_space=pltpu.VMEM)
SM = pl.BlockSpec(memory_space=pltpu.SMEM)
HB = pl.BlockSpec(memory_space=pl.ANY)
IN = object()


def units_of(count):
    return ((16, count, 16, D), BF16)


def act_shape(dtype=BF16):
    return ((SEQ, D), dtype)


KEPT = [act_shape()] * 5 + [((HEADS, SEQ, SEQ), BF16), act_shape(F32), act_shape()]


def call(body, args, specs, outs, scratch, flops):
    brought = [k for k, spec in enumerate(specs) if spec is IN]

    def kernel(*refs):
        refs = list(refs)
        ins, refs = refs[: len(args)], refs[len(args) :]
        targets, refs = refs[: len(outs)], refs[len(outs) :]
        staged_in, refs = refs[: len(brought)], refs[len(brought) :]
        staged_out, refs = refs[: len(outs)], refs[len(outs) :]
        sem, refs = refs[0], refs[1:]
        pairs_in = []
        for k, ref in zip(brought, staged_in):
            pairs_in.append((ins[k], ref))
            ins[k] = ref
        copies = Copies(pairs_in, list(zip(targets, staged_out)), sem)
        body(copies, *ins, *staged_out, *refs)
        copies.finish()

    buffers = [pltpu.VMEM(args[k].shape, args[k].dtype) for k in brought]
    buffers += [pltpu.VMEM(*out) for out in outs]
    buffers += [pltpu.SemaphoreType.DMA((len(brought) + len(outs),))]
    buffers += [
        pltpu.VMEM(*s) if isinstance(s, tuple) else pltpu.SemaphoreType.DMA((s,)) for s in scratch
    ]
    return pl.pallas_call(
        kernel,
        in_specs=[HB if spec is IN else spec for spec in specs],
        out_specs=[HB] * len(outs),
        out_shape=[jax.ShapeDtypeStruct(s, t) for s, t in outs],
        scratch_shapes=buffers,
        compiler_params=pltpu.CompilerParams(vmem_limit_bytes=63 * 1024 * 1024),
        cost_estimate=pl.CostEstimate(flops=flops, bytes_accessed=1 << 24, transcendentals=0),
    )(*args)


def plain_call(body, args, outs, scratch):
    return pl.pallas_call(
        body,
        in_specs=[SM] + [VM] * (len(args) - 1),
        out_specs=[VM] * len(outs),
        out_shape=[jax.ShapeDtypeStruct(s, t) for s, t in outs],
        scratch_shapes=[pltpu.VMEM(*s) for s in scratch],
        cost_estimate=pl.CostEstimate(flops=1 << 20, bytes_accessed=1 << 18, transcendentals=0),
    )(*args)


SQUARE = ((4, D, D), BF16)
TALL = ((BLOCKS, 4, 16, D), BF16)
ACC = ((D, D), F32)
TURN = ((D, SEQ), BF16)
BIAS = ((SEQ, SEQ), F32)
BACK = [act_shape()] * 2 + [TURN] * 3 + [act_shape(), TURN, TURN, act_shape(), act_shape()]
BACK = BACK + [act_shape(F32)] * 2


def pairs(axis, step):
    k = AXES.index(axis)
    found = []

    def flat(place):
        index = 0
        for at, size in zip(place, SIZES):
            index = index * size + at
        return index

    for place in itertools.product(*[range(size) for size in SIZES]):
        if axis == "c":
            other = 1
        else:
            other = 1 if (step == 0) == (place[1] == 0) else 3
        target = list(place)
        target[k] = place[k] ^ other
        found.append((flat(place), flat(target)))
    return found


def swap(values, axis, step=0):
    return lax.ppermute(values, AXES, pairs(axis, step))


def away(core, order):
    hop = 1 if core == 0 else 3
    return (0, hop, 4 - hop, 2)[order]


def tables():
    found = []
    for x, c, y, z in itertools.product(*[range(size) for size in SIZES]):
        row_a, row_b = [], []
        for j in range(2):
            core = c ^ j
            for slot in range(16):
                one, two = away(core, slot % 4), away(core, slot // 4)
                row_a.append((x ^ one) * 8 + core * 4 + (y ^ two))
                row_b.append((x ^ two) * 8 + core * 4 + (y ^ one))
        found.append(row_a + row_b + list(np.argsort(row_a)) + list(np.argsort(row_b)) + [c])
    return np.array(found, np.int32)


def step_all(parts):
    received = [swap(*part) for part in parts]
    return lax.optimization_barrier(tuple(received))


def join(values, received):
    return jnp.concatenate([values, received], axis=0)


def by_z(mine, one, two):
    me, core = lax.axis_index("z"), lax.axis_index("c")
    found = []
    for z in range(4):
        distance = me ^ z
        odd = jnp.where(core == 0, distance == 1, distance == 3)
        part = jnp.where(odd, one, jnp.where(distance == 2, two[1], two[0]))
        found.append(jnp.where(distance == 0, mine, part))
    narrow = jnp.stack([part[:84].reshape(21, 4, D) for part in found], axis=1).reshape(21 * 16, D)
    enc = [part[96:112] for part in found]
    dec = [part[112:] for part in found]
    return (
        jnp.concatenate([narrow[:112], narrow[144:208], *dec]),
        jnp.concatenate([narrow[112:144], *enc, narrow[208:]]),
    )


def parted(values, received, units, cut):
    values = values.reshape(4, units * 16, D)
    received = received.reshape(4, units * 16, D)
    return [
        jnp.concatenate([values[:, part], received[:, part]]).reshape(-1, D)
        for part in (slice(0, cut * 16), slice(cut * 16, None))
    ]


def gather(table, packed):
    z_one = swap(packed, "z", 0)
    table, z_one = lax.optimization_barrier((table, z_one))
    z_two = swap(jnp.stack([packed, z_one]), "z", 1)
    one, two = by_z(packed, z_one, z_two)
    for step in range(2):
        got = step_all([(one, "x", step), (two, "y", step)])
        one, two = join(one, got[0]), join(two, got[1])
    got = step_all([(one, "y", 0), (two, "x", 0)])
    one_enc, one_dec = parted(one, got[0], 15, 7)
    two_enc, two_dec = parted(two, got[1], 14, 6)
    enc = step_all([(one_enc, "y", 1), (two_enc, "x", 1), (one_enc, "c", 0), (two_enc, "c", 0)])
    dec = swap(one_dec, "y", 1), swap(two_dec, "x", 1), swap(one_dec, "c"), swap(two_dec, "c")
    return table, pieces_of((one_enc, two_enc), enc, (7, 6)), (one_dec, two_dec), dec


def pieces_of(low, got, units):
    found = []
    for k in range(2):
        for piece in (low[k], got[k], got[2 + k], swap(got[k], "c")):
            found.append(piece.reshape(8, units[k], 16, D))
    return found


def add(left, right):
    return left + right


def fold(values, received):
    half = values.shape[0] // 2
    return add(values[:half], received[:half]), add(values[half:], received[half:])


def beside(left, right):
    return jnp.concatenate([left, right], axis=1)


def z_parts(values, wide):
    me, core = lax.axis_index("z"), lax.axis_index("c")
    parts = values.reshape(-1, 4, 4, D)
    hop = jnp.where(core == 0, 1, 3)
    found = []
    for distance in (0, hop, 4 - hop, 2):
        want = me ^ distance
        picked, tall = parts[:, 3], parts[wide + 3]
        for z in range(3):
            picked = jnp.where(want == z, parts[:, z], picked)
            tall = jnp.where(want == z, parts[wide + z], tall)
        found.append(jnp.concatenate([picked[:wide], tall, picked[wide + 4 :]]))
    return jnp.stack(found[:2]), jnp.stack(found[2:])


def per_device(
    source, target, source_lengths, target_lengths, lang_ids, out_cotangent,
    enc_attn, enc_vectors, enc_w_in, enc_b_in, enc_w_out,
    dec_self, dec_cross, dec_vectors, dec_w_in, dec_b_in, dec_w_out, lang_table,
):
    spot = (lax.axis_index("z") + 4 * (lax.axis_index("y") % 2)).reshape(1)
    (packed,) = plain_call(
        pack_kernel,
        (
            spot, enc_attn, enc_w_in, enc_w_out, dec_self, dec_cross, dec_w_in, dec_w_out,
            enc_vectors.T, dec_vectors.T, lang_table.T, enc_b_in.reshape(1, 16), dec_b_in.reshape(1, 16),
        ),
        [((128, D), BF16)],
        [((8, 128), F32), ((128, D), F32)],
    )
    me = lax.axis_index(AXES)
    table = lax.dynamic_index_in_dim(jnp.asarray(tables()), me, 0, keepdims=False)
    table, g_enc, low_dec, got_dec = gather(table, packed)
    vecs, b_enc, b_dec, *kept, e_mid, e_n2, memory = call(
        encoder_kernel,
        (table, source_lengths, source[0], *g_enc),
        [SM] * 2 + [IN] + [HB] * 8,
        [((128, D), F32), ((1, FF), F32), ((1, FF), F32)]
        + KEPT
        + [act_shape(F32), act_shape(), act_shape()],
        [((1, D, D), BF16), SQUARE, SQUARE, TALL, BIAS, act_shape(F32), 4],
        5 * 10**9,
    )
    memory, *got_dec = lax.optimization_barrier((memory, *got_dec))
    g_dec = pieces_of(low_dec, got_dec, (8, 8))
    dec_out, p_dec, q_dec, other, g_start, g_memory, g_vec, g_bias_dec = call(
        first_kernel,
        (
            table, source_lengths, target_lengths, lang_ids, vecs,
            target[0], memory, out_cotangent[0], b_dec, *g_dec,
        ),
        [SM] * 4 + [IN] * 5 + [HB] * 8,
        [act_shape(), units_of(6), units_of(10), units_of(16)]
        + [act_shape(F32), act_shape(F32), ((128, D), F32), ((1, FF), F32)],
        KEPT
        + KEPT
        + [SQUARE, SQUARE, SQUARE, TALL, BIAS, BIAS]
        + [act_shape(F32)] * 4
        + [act_shape()] * 3
        + [act_shape(F32)] * 2
        + [ACC, TURN, TURN, act_shape()]
        + BACK
        + [4],
        15 * 10**9,
    )
    got = swap(other, "c")
    p_enc, q_enc, other, g_source = call(
        second_kernel,
        (
            table, g_memory, e_n2, b_enc, vecs, e_mid, *kept, source[0], g_vec, g_bias_dec, *g_enc,
        ),
        [SM] + [IN] * 16 + [HB] * 8,
        [units_of(8), units_of(5), units_of(13), act_shape(F32)],
        [SQUARE, SQUARE, TALL, act_shape(F32), act_shape(), ACC, TURN, act_shape(), act_shape()]
        + [act_shape(F32), act_shape(F32), ((1, FF), F32), ((128, D), F32), ACC]
        + BACK
        + [3],
        8 * 10**9,
    )
    other, got = lax.optimization_barrier((other, got))
    again = swap(other, "c")
    p_low, p_high = fold(p_dec, got[:, :6])
    q_low, q_high = fold(q_dec, got[:, 6:])
    p_got, q_got = swap(p_high, "y", 1), swap(q_high, "x", 1)
    one_low, one_high = fold(p_enc, again[:, :8])
    two_low, two_high = fold(q_enc, again[:, 8:])
    p_got, q_got, one_got, two_got = lax.optimization_barrier(
        (p_got, q_got, swap(one_high, "y", 1), swap(two_high, "x", 1))
    )
    p_low, p_high = map(beside, fold(p_low, p_got), fold(one_low, one_got))
    q_low, q_high = map(beside, fold(q_low, q_got), fold(two_low, two_got))
    for axes, step in ((("y", "x"), 0), (("x", "y"), 1)):
        p_got, q_got = step_all([(p_high, axes[0], step), (q_high, axes[1], step)])
        p_low, p_high = fold(p_low, p_got)
        q_low, q_high = fold(q_low, q_got)
    p_got, q_got = step_all([(p_high, "x", 0), (q_high, "y", 0)])
    p_near, p_far = z_parts(add(p_low, p_got)[0], 10)
    q_near, q_far = z_parts(add(q_low, q_got)[0], 6)
    got = swap(beside(p_far, q_far), "z", 1)
    low, high = fold(beside(p_near, q_near), got)
    got = swap(high, "z", 0)
    quarter, four = ((4, FF), F32), ((4, 4, D), F32)
    (
        d_attn, d_vec_e, d_w_in, d_b_e, d_w_out, d_self, d_cross, d_vec_d, d_dec_in, d_b_d, d_dec_out, d_lang,
    ) = plain_call(
        unpack_kernel,
        (spot, low, got),
        [four, ((4, 8), F32), quarter, ((1, 16), F32), ((16, D), F32), four, four]
        + [((4, 13), F32), quarter, ((1, 16), F32), ((16, D), F32), ((4, LANGS), F32)],
        [((4, D), F32)],
    )
    return (
        dec_out[None],
        g_source[None],
        g_start[None],
        d_attn,
        d_vec_e.T,
        d_w_in,
        d_b_e.reshape(16),
        d_w_out,
        d_self,
        d_cross,
        d_vec_d.T,
        d_dec_in,
        d_b_d.reshape(16),
        d_dec_out,
        d_lang.T,
    )


def solution(mesh):
    fine = Mesh(mesh.devices.reshape(SIZES), AXES)
    flat = AXES
    in_specs = (
        P(flat, None, None),
        P(flat, None, None),
        P(flat, None),
        P(flat, None),
        P(flat, None),
        P(flat, None, None),
        P(None, flat, None),
        P(None, flat),
        P(flat, None),
        P(flat),
        P(flat, None),
        P(None, flat, None),
        P(None, flat, None),
        P(None, flat),
        P(flat, None),
        P(flat),
        P(flat, None),
        P(None, flat),
    )
    out_specs = (
        P(flat, None, None),
        P(flat, None, None),
        P(flat, None, None),
        P(None, flat, None),
        P(None, flat),
        P(flat, None),
        P(flat),
        P(flat, None),
        P(None, flat, None),
        P(None, flat, None),
        P(None, flat),
        P(flat, None),
        P(flat),
        P(flat, None),
        P(None, flat),
    )
    return jax.shard_map(
        per_device, mesh=fine, in_specs=in_specs, out_specs=out_specs, check_vma=False
    )
```

```python
import itertools

import jax
import jax.numpy as jnp
import numpy as np
from jax import lax
from jax.experimental import pallas as pl
from jax.experimental.pallas import tpu as pltpu
from jax.sharding import Mesh
from jax.sharding import PartitionSpec as P

D = 512
HEADS = 8
HEAD_DIM = 64
FF = 2048
LANGS = 100
SEQ = 384
DOCS = 5
EPSILON = 1e-05
NEGATIVE = -1000000000.0
OPEN = 3e38
SCALE = HEAD_DIM ** (-0.5)
AXES = ("x", "c", "y", "z")
SIZES = (4, 2, 4, 4)
BLOCKS = 32
ENC_VEC = 104
DEC_VEC = 112
CHUNK = 128
CHUNKS = SEQ // CHUNK
TAB_A, TAB_B, SLOT_A, SLOT_B, CORE = 0, 32, 64, 96, 128
F32 = jnp.float32
BF16 = jnp.bfloat16


def dot(left, right):
    return lax.dot_general(left, right, (((1,), (0,)), ((), ())), preferred_element_type=F32)


def dot_nt(left, right):
    return lax.dot_general(left, right, (((1,), (1,)), ((), ())), preferred_element_type=F32)


def rows(index, size=CHUNK):
    return slice(index * size, (index + 1) * size)


def normed(values):
    mean = jnp.mean(values, axis=-1, keepdims=True)
    center = values - mean
    rstd = lax.rsqrt(jnp.mean(center * center, axis=-1, keepdims=True) + EPSILON)
    return center * rstd, rstd


def layer_norm(source, gain, shift, out):
    for i in range(CHUNKS):
        hat, _ = normed(source[rows(i), :])
        out[rows(i), :] = (hat * gain + shift).astype(BF16)


def norm_back(source, gain, grad, base, out):
    d_gain = jnp.zeros((1, D), F32)
    d_shift = jnp.zeros((1, D), F32)
    for i in range(CHUNKS):
        hat, rstd = normed(source[rows(i), :])
        dy = grad[rows(i), :]
        d_gain = d_gain + jnp.sum(dy * hat, axis=0, keepdims=True)
        d_shift = d_shift + jnp.sum(dy, axis=0, keepdims=True)
        dyg = dy * gain
        mean_one = jnp.mean(dyg, axis=-1, keepdims=True)
        mean_two = jnp.mean(dyg * hat, axis=-1, keepdims=True)
        out[rows(i), :] = base[rows(i), :].astype(F32) + rstd * (dyg - mean_one - hat * mean_two)
    return d_gain, d_shift


def low_lanes(count):
    return lax.broadcasted_iota(jnp.int32, (count, 128), 1) < HEAD_DIM


def head_mask():
    lane = lax.broadcasted_iota(jnp.int32, (1, D), 1)
    return ((lane // HEAD_DIM) % 2 == 0).astype(F32)


def doc_ids(lengths, shape, axis):
    position = lax.broadcasted_iota(jnp.int32, shape, axis)
    total = jnp.zeros(shape, jnp.int32)
    end = 0
    for i in range(DOCS):
        end = end + lengths[0, i]
        total = total + (position >= end).astype(jnp.int32)
    return total


def masks(s_len, t_len, bias_s, bias_c):
    s_row = doc_ids(s_len, (1, SEQ), 1)
    t_row = doc_ids(t_len, (1, SEQ), 1)
    t_col = doc_ids(t_len, (SEQ, 1), 0)
    key = lax.broadcasted_iota(jnp.int32, (SEQ, SEQ), 1)
    query = lax.broadcasted_iota(jnp.int32, (SEQ, SEQ), 0)
    bias_s[...] = jnp.where((t_col == t_row) & (key <= query), OPEN, NEGATIVE)
    bias_c[...] = jnp.where(t_col == s_row, OPEN, NEGATIVE)


def lang_onehot(t_len, langs):
    doc = doc_ids(t_len, (SEQ, 128), 0)
    lang = jnp.zeros((SEQ, 128), jnp.int32)
    for i in range(DOCS):
        lang = jnp.where(doc == i, langs[0, i], lang)
    lane = lax.broadcasted_iota(jnp.int32, (SEQ, 128), 1)
    return jnp.where(lang == lane, 1.0, 0.0).astype(BF16)


def attn_project(query_in, memory, weights, bias_q, bias_v, q_even, q_odd, keys, values):
    even = head_mask()
    q = SCALE * (dot(query_in[...], weights[0]) + bias_q)
    q_even[...] = (q * even).astype(BF16)
    q_odd[...] = (q * (1.0 - even)).astype(BF16)
    keys[...] = dot(memory[...], weights[1]).astype(BF16)
    values[...] = (dot(memory[...], weights[2]) + bias_v).astype(BF16)


def attn_core(q_even, q_odd, keys, values, bias, probs, inverse, context):
    low = low_lanes(SEQ)
    queries = (q_even, q_odd)
    held = []

    def lanes(head):
        return rows(head // 2, 128)

    def scores(head):
        return dot_nt(queries[head % 2][:, lanes(head)], keys[:, lanes(head)])

    def finish(head, e, total):
        over = 1.0 / total
        held.append((dot(e, values[:, lanes(head)]) * over, over))
        if head % 2 == 1:
            (one, over_one), (two, over_two) = held
            held.clear()
            context[:, lanes(head)] = jnp.where(low, one, two).astype(BF16)
            inverse[:, lanes(head)] = jnp.where(low, over_one, over_two)

    s = scores(0)
    last = None
    for head in range(HEADS):
        s_next = scores(head + 1) if head + 1 < HEADS else None
        s = jnp.minimum(s, bias[...])
        e = jnp.exp(s - jnp.max(s, axis=-1, keepdims=True))
        total = jnp.sum(e, axis=-1, keepdims=True)
        e = e.astype(BF16)
        probs[head] = e
        if last is not None:
            finish(*last)
        last = (head, e, total)
        s = s_next
    finish(*last)


def attn_output(context, weight, bias_o, residual, out):
    branch = dot(context[...], weight[...]) + bias_o
    out[...] = residual[...].astype(F32) + branch


def put_blocks(acc, place):
    refs, units, table, first = place
    for slot in range(16):
        for j in range(2):
            start = pl.multiple_of(table[first + 16 * j + slot] * 16, 16)
            refs[j][slot, units[j]] = acc[pl.ds(start, 16), :].astype(BF16)


def place_of(own, other, unit, shift, table, first):
    return (own, other), (unit, unit + shift), table, first


def weight_grad(left_t, right, acc, place, scale=None):
    value = dot(left_t[...], right[...])
    acc[...] = (value if scale is None else value * scale).astype(BF16)
    put_blocks(acc, place)


def tall_grad(left_t, right, acc, place, chunk):
    refs, units, table, slots = place
    acc[...] = dot(left_t, right[...]).astype(BF16)
    for j in range(2):
        core = table[CORE] ^ j
        for y in range(4):
            slot = table[slots + chunk * 8 + core * 4 + y] - 16 * j
            for z in range(4):
                start = pl.multiple_of(core * 256 + y * 64 + z * 16, 16)
                refs[j][slot, units[j] + z] = acc[pl.ds(start, 16), :].astype(BF16)


def column_sum(ref):
    return jnp.sum(ref[...].astype(F32), axis=0, keepdims=True)


def attn_back(grad, query_in_t, memory_t, weights, kept, scratch, acc, places):
    q_even, q_odd, keys, values, probs, inverse, context = kept
    d_even, d_odd, dc_t, q_t, c_t, dq, dk_t, dv_t, dk, dv, du, dm = scratch
    even = head_mask()
    dc = dot_nt(grad[...], weights[3]) * inverse[...]
    d_even[...] = (dc * even).astype(BF16)
    d_odd[...] = (dc * (1.0 - even)).astype(BF16)
    dc_t[...] = (d_even[...] + d_odd[...]).T
    q_t[...] = (q_even[...] + q_odd[...]).T
    c_t[...] = context[...].T
    low = low_lanes(SEQ)
    d_ctx = (d_even, d_odd)
    held = []

    def lanes(head):
        return rows(head // 2, 128)

    def first(head):
        dch = d_ctx[head % 2][:, lanes(head)]
        total = jnp.sum(
            dch.astype(F32) * context[:, lanes(head)].astype(F32), axis=-1, keepdims=True
        )
        return dot_nt(dch, values[:, lanes(head)]), total

    def finish(head, ds):
        span = rows(head, HEAD_DIM)
        held.append(dot(ds, keys[:, lanes(head)]))
        dk_t[span, :] = dot(q_t[span, :], ds).astype(BF16)
        dv_t[span, :] = dot(dc_t[span, :], probs[head]).astype(BF16)
        if head % 2 == 1:
            dq[:, lanes(head)] = jnp.where(low, held[0], held[1]).astype(BF16)
            held.clear()

    now = first(0)
    last = None
    for head in range(HEADS):
        later = first(head + 1) if head + 1 < HEADS else None
        dp, total = now
        ds = (probs[head].astype(F32) * (dp - total)).astype(BF16)
        if last is not None:
            finish(*last)
        last = (head, ds)
        now = later
    finish(*last)
    dk[...] = dk_t[...].T
    dv[...] = dv_t[...].T
    weight_grad(query_in_t, dq, acc, places[0], SCALE)
    weight_grad(memory_t, dk, acc, places[1])
    weight_grad(memory_t, dv, acc, places[2])
    weight_grad(c_t, grad, acc, places[3])
    du[...] = SCALE * dot_nt(dq[...], weights[0])
    dm[...] = dot_nt(dk[...], weights[1]) + dot_nt(dv[...], weights[2])
    return SCALE * column_sum(dq), column_sum(dv), column_sum(grad)


def silu_parts(hidden):
    gate = 1.0 / (1.0 + jnp.exp(-hidden))
    return hidden * gate, gate


def feed_forward(inputs, w_in, b_in, w_out, bias, residual, out):
    total = residual[...] + bias
    for k in range(FF // D):
        active, _ = silu_parts(dot(inputs[...], w_in[k]) + b_in[:, rows(k, D)])
        total = total + dot(active.astype(BF16), w_out[k])
    out[...] = total


def feed_both(
    inputs, inputs_t, w_in, b_in, w_out, grad, act, dh, total, d_in, acc, places_in, place_out, b_grad
):
    hidden = dot(inputs[...], w_in[0]) + b_in[:, rows(0, D)]
    for k in range(FF // D):
        d_act = dot_nt(grad[...], w_out[k])
        active, gate = silu_parts(hidden)
        low = active.astype(BF16)
        act[...] = low
        d_hid = (d_act * (gate + active * (1.0 - gate))).astype(BF16)
        dh[...] = d_hid
        if k + 1 < FF // D:
            hidden = dot(inputs[...], w_in[k + 1]) + b_in[:, rows(k + 1, D)]
        if total is not None:
            total[...] = total[...] + dot(low, w_out[k])
        back = dot_nt(d_hid, w_in[k])
        d_in[...] = back if k == 0 else d_in[...] + back
        b_grad[:, rows(k, D)] = column_sum(dh)
        weight_grad(inputs_t, dh, acc, places_in[k])
        tall_grad(act[...].T, grad, acc, place_out, k)


def load(table, first, pieces, jobs):
    def step(slot, carry):
        for k, piece in enumerate(pieces):
            block = table[first + 8 * k + slot]
            start = pl.multiple_of(block * 16, 16)
            for unit, count, target, row, sem in jobs:
                if len(target.shape) == 4:
                    place = target.at[block]
                else:
                    place = target.at[pl.ds(row, count), pl.ds(start, 16), :]
                pltpu.make_async_copy(piece.at[slot, pl.ds(unit, count)], place, sem).start()
        return carry

    lax.fori_loop(0, 8, step, 0)


def arrived(target, sem):
    pltpu.make_async_copy(target, target, sem).wait()


class Wide:
    def __init__(self, ref):
        self.ref = ref

    def __getitem__(self, k):
        return self.ref[8 * k : 8 * k + 8].reshape(D, D)


def pack_kernel(
    spot, attn, w_in, w_out, self_w, cross, dec_in, dec_out, vec_e, vec_d, lang, b_e, b_d,
    packed, wide, buf,
):
    for k in range(4):
        buf[rows(k, 4), :] = attn[k].astype(F32)
        buf[rows(4 + k if k < 2 else 5 + k, 4), :] = w_in[:, rows(k, D)].astype(F32)
        buf[rows(9 + k, 4), :] = self_w[k].astype(F32)
        buf[rows(13 + k, 4), :] = cross[k].astype(F32)
        buf[rows(17 + k, 4), :] = dec_in[:, rows(k, D)].astype(F32)
    buf[84:96, :] = jnp.zeros((12, D), F32)
    buf[96:112, :] = w_out[...].astype(F32)
    buf[112:128, :] = dec_out[...].astype(F32)
    wide[...] = jnp.zeros(wide.shape, F32)
    wide[0:4, 0:LANGS] = lang[...].astype(F32)
    wide[0:4, ENC_VEC : ENC_VEC + 8] = vec_e[...].astype(F32)
    wide[0:4, DEC_VEC : DEC_VEC + 13] = vec_d[...].astype(F32)
    row = lax.broadcasted_iota(jnp.int32, (16, 128), 0)
    lane = lax.broadcasted_iota(jnp.int32, (16, 128), 1)
    place = jnp.where(lane == row + spot[0] * 16, 1.0, 0.0).astype(BF16)
    first = lax.broadcasted_iota(jnp.int32, (8, 128), 0) == 0
    buf[24:28, 0:128] = wide[0:4, :]
    for k, ref in enumerate((b_e, b_d)):
        spread = dot(jnp.broadcast_to(ref[...].astype(F32), (8, 16)).astype(BF16), place)
        wide[0:8, :] = jnp.where(first, spread, 0.0)
        buf[24:28, 128 + 128 * k : 256 + 128 * k] = wide[0:4, :]
    buf[24:28, 384:512] = jnp.zeros((4, 128), F32)
    packed[...] = buf[...].astype(BF16)


def unpack_kernel(
    spot, mine, got_one, got_two, got_three,
    attn, vec_e, w_in, b_e, w_out, self_w, cross, vec_d, dec_in, b_d, dec_out, lang,
    last,
):
    def total(index):
        found = mine[index].astype(F32) + got_one[index].astype(F32)
        return found + (got_two[index].astype(F32) + got_three[index].astype(F32))

    for k in range(4):
        dec_in[:, rows(k, D)] = total(k)
        cross[k] = total(4 + k if k < 2 else 16 + k)
        w_in[:, rows(k, D)] = total(6 + k)
        w_out[rows(k, 4), :] = total(10 + k)
        self_w[k] = total(14 + k)
        dec_out[rows(k, 4), :] = total(20 + k)
        attn[k] = total(24 + k)
    last[...] = total(28)
    lang[...] = last[:, 0:LANGS]
    vec_e[...] = last[:, ENC_VEC : ENC_VEC + 8]
    vec_d[...] = last[:, DEC_VEC : DEC_VEC + 13]
    for k, ref in enumerate((b_e, b_d)):
        tile = jnp.broadcast_to(last[0:1, 128 + 128 * k : 256 + 128 * k], (8, 128))
        ref[...] = pltpu.roll(tile, 128 - 16 * spot[0], 1)[0:1, 0:16]


class Copies:
    def __init__(self, incoming, outgoing, sem):
        self.waiting = {}
        self.flying = {}
        self.outgoing = {}
        self.sent = {}
        for index, (hbm, vmem) in enumerate(incoming):
            self.waiting[id(vmem)] = pltpu.make_async_copy(hbm, vmem, sem.at[index])
        for index, (hbm, vmem) in enumerate(outgoing):
            self.outgoing[id(vmem)] = (vmem, hbm, sem.at[len(incoming) + index])
        self.targets = {id(vmem): hbm for hbm, vmem in outgoing}
        self.spare = [sem.at[len(incoming) + len(outgoing) + k] for k in range(SPARE)]

    def bring(self, *refs):
        for ref in refs:
            copy = self.waiting.pop(id(ref))
            copy.start()
            self.flying[id(ref)] = copy

    def need(self, *refs):
        for ref in refs:
            self.flying.pop(id(ref)).wait()

    def send(self, *refs):
        for ref in refs:
            copy = pltpu.make_async_copy(*self.outgoing.pop(id(ref)))
            copy.start()
            self.sent[id(ref)] = copy

    def send_units(self, ref, first, last):
        self.outgoing.pop(id(ref), None)
        hbm = self.targets[id(ref)]
        part = (slice(None), slice(first, last))
        copy = pltpu.make_async_copy(ref.at[part], hbm.at[part], self.spare.pop())
        copy.start()
        self.sent[(id(ref), first)] = copy

    def free(self, *refs):
        for ref in refs:
            copy = self.sent.pop(id(ref))
            copy.wait()

    def finish(self):
        assert not self.waiting and not self.flying
        for key, (vmem, hbm, sem) in self.outgoing.items():
            copy = pltpu.make_async_copy(vmem, hbm, sem)
            copy.start()
            self.sent[key] = copy
        for copy in self.sent.values():
            copy.wait()


def encoder_kernel(
    io, table, s_len, source, a0, a1, a2, a3, b0, b1, b2, b3,
    vecs, b_enc, b_dec, e_n, e_qe, e_qo, e_k, e_v, e_p, e_i, e_c, e_mid, e_n2, memory,
    small, we, wi, wo, bias_e, buf, sem,
):
    io.bring(source)
    load(table, TAB_A, (a0, a1, a2, a3), ((6, 1, small, 0, sem.at[3]), (0, 4, we, 0, sem.at[0])))
    load(table, TAB_B, (b0, b1, b2, b3), ((0, 2, wi, 2, sem.at[1]), (2, 4, wo, 0, sem.at[2])))
    load(table, TAB_A, (a0, a1, a2, a3), ((4, 2, wi, 0, sem.at[1]),))
    s_row = doc_ids(s_len, (1, SEQ), 1)
    s_col = doc_ids(s_len, (SEQ, 1), 0)
    bias_e[...] = jnp.where(s_col == s_row, OPEN, NEGATIVE)
    arrived(small, sem.at[3])
    vecs[...] = small[0, :, 0:128].astype(F32).T
    for k, ref in enumerate((b_enc, b_dec)):
        for tile in range(FF // 128):
            part = small[0, rows(tile, 32), 128 + 128 * k : 256 + 128 * k].astype(F32)
            ref[:, rows(tile, 128)] = jnp.sum(part, axis=0, keepdims=True)

    def enc(index):
        return vecs[ENC_VEC + index : ENC_VEC + index + 1, :]

    io.need(source)
    buf[...] = source[...].astype(F32)
    layer_norm(buf, enc(0), enc(1), e_n)
    arrived(we, sem.at[0])
    attn_project(e_n, e_n, we, enc(2), enc(3), e_qe, e_qo, e_k, e_v)
    attn_core(e_qe, e_qo, e_k, e_v, bias_e, e_p, e_i, e_c)
    io.send(vecs, b_enc, b_dec, e_n, e_qe, e_qo, e_k, e_v, e_p, e_i, e_c)
    attn_output(e_c, we.at[3], enc(4), source, e_mid)
    layer_norm(e_mid, enc(5), enc(6), e_n2)
    io.send(e_mid, e_n2)
    arrived(wi, sem.at[1])
    arrived(wo, sem.at[2])
    feed_forward(e_n2, wi, b_enc, Wide(wo), enc(7), e_mid, buf)
    memory[...] = buf[...].astype(BF16)


def first_kernel(
    io, table, s_len, t_len, langs, vecs, target, memory, cot, b_dec,
    a0, a1, a2, a3, b0, b1, b2, b3,
    dec_out, d_p, d_q, d_other, g_start, g_memory, g_vec, g_bias,
    s_n, s_qe, s_qo, s_k, s_v, s_p, s_i, s_c, c_n, c_qe, c_qo, c_k, c_v, c_p, c_i, c_c,
    ws, wc, vi, vo, bias_s, bias_c, buf, start, first, second, n3,
    act, dh, d_in, g_first, acc, u_t, m_t, low,
    d_even, d_odd, dc_t, q_t, c_t, dq, dk_t, dv_t, dk, dv, du, dm, sem,
):
    io.bring(vecs, target)
    load(table, TAB_A, (a0, a1, a2, a3), ((0, 4, ws, 0, sem.at[0]),))
    masks(s_len, t_len, bias_s, bias_c)
    onehot = lang_onehot(t_len, langs)
    io.need(vecs, target)
    io.bring(memory, cot, b_dec)
    load(table, TAB_B, (b0, b1, b2, b3), ((0, 4, wc, 0, sem.at[1]), (4, 4, vi, 0, sem.at[2])))
    load(table, TAB_A, (a0, a1, a2, a3), ((4, 4, vo, 0, sem.at[3]),))

    def dec(index):
        return vecs[DEC_VEC + index : DEC_VEC + index + 1, :]

    start[...] = target[...].astype(F32) + dot(onehot, vecs[...].astype(BF16))
    layer_norm(start, dec(0), dec(1), s_n)
    arrived(ws, sem.at[0])
    attn_project(s_n, s_n, ws, dec(2), dec(3), s_qe, s_qo, s_k, s_v)
    attn_core(s_qe, s_qo, s_k, s_v, bias_s, s_p, s_i, s_c)
    attn_output(s_c, ws.at[3], dec(4), start, first)
    layer_norm(first, dec(5), dec(6), c_n)
    io.need(memory, cot, b_dec)
    arrived(wc, sem.at[1])
    attn_project(c_n, memory, wc, dec(7), dec(8), c_qe, c_qo, c_k, c_v)
    attn_core(c_qe, c_qo, c_k, c_v, bias_c, c_p, c_i, c_c)
    attn_output(c_c, wc.at[3], dec(9), first, second)
    layer_norm(second, dec(10), dec(11), n3)
    u_t[...] = n3[...].T
    buf[...] = second[...] + dec(12)
    arrived(vi, sem.at[2])
    arrived(vo, sem.at[3])

    def in_p(unit):
        return place_of(d_p, d_other, unit, 0, table, TAB_A)

    def in_q(unit):
        return place_of(d_q, d_other, unit, 6, table, TAB_B)

    feed_both(
        n3, u_t, vi, b_dec, Wide(vo), cot, act, dh, buf, d_in, acc,
        [in_p(k) for k in range(4)], place_of(d_q, d_other, 6, 6, table, SLOT_B), g_bias,
    )
    dec_out[...] = buf[...].astype(BF16)
    io.send(dec_out, g_bias)
    io.send_units(d_other, 0, 4)
    io.send_units(d_other, 12, 16)
    io.send_units(d_q, 6, 10)
    g_second = second
    gain_three = norm_back(second, dec(10), d_in, cot, g_second)
    scratch = (d_even, d_odd, dc_t, q_t, c_t, dq, dk_t, dv_t, dk, dv, du, dm)
    u_t[...] = c_n[...].T
    m_t[...] = memory[...].T
    low[...] = g_second[...].astype(BF16)
    bias_two = attn_back(
        low, u_t, m_t, wc, (c_qe, c_qo, c_k, c_v, c_p, c_i, c_c), scratch, acc,
        [in_p(4), in_p(5), in_q(4), in_q(5)],
    )
    io.send(d_p)
    io.send_units(d_other, 4, 6)
    io.send_units(d_other, 10, 12)
    io.send_units(d_q, 4, 6)
    g_memory[...] = dm[...]
    io.send(g_memory)
    gain_two = norm_back(first, dec(5), du, g_second, g_first)
    low[...] = g_first[...].astype(BF16)
    u_t[...] = s_n[...].T
    bias_one = attn_back(
        low, u_t, u_t, ws, (s_qe, s_qo, s_k, s_v, s_p, s_i, s_c), scratch, acc,
        [in_q(k) for k in range(4)],
    )
    io.send_units(d_other, 6, 10)
    io.send_units(d_q, 0, 4)
    du[...] = du[...] + dm[...]
    gain_one = norm_back(start, dec(0), du, g_first, g_start)
    io.send(g_start)
    g_vec[...] = lax.dot_general(
        onehot, g_start[...].astype(BF16), (((0,), (0,)), ((), ())), preferred_element_type=F32
    )
    values = gain_one + bias_one + gain_two + bias_two + gain_three + (column_sum(cot),)
    for i, value in enumerate(values):
        g_vec[DEC_VEC + i : DEC_VEC + i + 1, :] = value


def second_kernel(
    io, table, g_memory, e_n2, b_enc, vecs, e_mid, e_n, e_qe, e_qo, e_k, e_v, e_p, e_i, e_c,
    source, g_vec, g_bias_dec, a0, a1, a2, a3, b0, b1, b2, b3,
    d_p, d_q, d_other, g_source,
    we, wi, wo, buf, low, acc, u_t, act, dh, d_in, g_mid, b_grad, all_vec, turned,
    d_even, d_odd, dc_t, q_t, c_t, dq, dk_t, dv_t, dk, dv, du, dm, sem,
):
    io.bring(g_memory, e_n2, b_enc)
    load(table, TAB_A, (a0, a1, a2, a3), ((4, 2, wi, 0, sem.at[0]),))
    load(table, TAB_B, (b0, b1, b2, b3), ((0, 2, wi, 2, sem.at[0]), (2, 4, wo, 0, sem.at[1])))
    io.need(g_memory, e_n2, b_enc)
    u_t[...] = e_n2[...].T
    low[...] = g_memory[...].astype(BF16)
    bias_out = column_sum(low)
    arrived(wi, sem.at[0])
    arrived(wo, sem.at[1])
    io.bring(vecs, e_mid, e_n)
    load(table, TAB_A, (a0, a1, a2, a3), ((0, 4, we, 0, sem.at[2]),))
    io.bring(e_i, e_qe, e_qo, e_c, e_v, e_k, e_p, source, g_vec, g_bias_dec)

    def in_p(unit):
        return place_of(d_p, d_other, unit, 0, table, TAB_A)

    def in_q(unit):
        return place_of(d_q, d_other, unit, 8, table, TAB_B)

    feed_both(
        e_n2, u_t, wi, b_enc, Wide(wo), low, act, dh, None, d_in, acc,
        [in_p(k) for k in range(4)], place_of(d_p, d_other, 4, 0, table, SLOT_A), b_grad,
    )
    io.send(d_p)
    io.send_units(d_other, 0, 8)
    io.need(vecs, e_mid, e_n)
    gain_two = norm_back(e_mid, vecs[ENC_VEC + 5 : ENC_VEC + 6, :], d_in, g_memory, g_mid)
    low[...] = g_mid[...].astype(BF16)
    u_t[...] = e_n[...].T
    io.need(e_i, e_qe, e_qo, e_c, e_v, e_k, e_p)
    arrived(we, sem.at[2])
    scratch = (d_even, d_odd, dc_t, q_t, c_t, dq, dk_t, dv_t, dk, dv, du, dm)
    bias_one = attn_back(
        low, u_t, u_t, we, (e_qe, e_qo, e_k, e_v, e_p, e_i, e_c), scratch, acc,
        [in_q(k) for k in range(4)],
    )
    io.send_units(d_other, 8, 12)
    io.send_units(d_q, 0, 4)
    du[...] = du[...] + dm[...]
    io.need(source, g_vec, g_bias_dec)
    buf[...] = source[...].astype(F32)
    gain_one = norm_back(buf, vecs[ENC_VEC : ENC_VEC + 1, :], du, g_mid, g_source)
    io.send(g_source)
    all_vec[...] = g_vec[...]
    for i, value in enumerate(gain_one + bias_one + gain_two + (bias_out,)):
        all_vec[ENC_VEC + i : ENC_VEC + i + 1, :] = value
    turned[:, 0:128] = all_vec[...].T
    for block in range(BLOCKS):
        tile = rows(block // 2, 128)
        turned[rows(block, 16), 128:256] = jnp.broadcast_to(b_grad[:, tile], (16, 128))
        turned[rows(block, 16), 256:384] = jnp.broadcast_to(g_bias_dec[:, tile], (16, 128))
        turned[rows(block, 16), 384:512] = jnp.zeros((16, 128), F32)
    put_blocks(turned, in_q(4))
    io.send_units(d_other, 12, 13)
    io.send_units(d_q, 4, 5)


VM = pl.BlockSpec(memory_space=pltpu.VMEM)
SM = pl.BlockSpec(memory_space=pltpu.SMEM)
HB = pl.BlockSpec(memory_space=pl.ANY)
IN = object()
SPARE = 8


def units_of(count):
    return ((16, count, 16, D), BF16)


def act_shape(dtype=BF16):
    return ((SEQ, D), dtype)


KEPT = [act_shape()] * 5 + [((HEADS, SEQ, SEQ), BF16), act_shape(F32), act_shape()]


def call(body, args, specs, outs, scratch, flops):
    brought = [k for k, spec in enumerate(specs) if spec is IN]

    def kernel(*refs):
        refs = list(refs)
        ins, refs = refs[: len(args)], refs[len(args) :]
        targets, refs = refs[: len(outs)], refs[len(outs) :]
        staged_in, refs = refs[: len(brought)], refs[len(brought) :]
        staged_out, refs = refs[: len(outs)], refs[len(outs) :]
        sem, refs = refs[0], refs[1:]
        pairs_in = []
        for k, ref in zip(brought, staged_in):
            pairs_in.append((ins[k], ref))
            ins[k] = ref
        copies = Copies(pairs_in, list(zip(targets, staged_out)), sem)
        body(copies, *ins, *staged_out, *refs)
        copies.finish()

    buffers = [pltpu.VMEM(args[k].shape, args[k].dtype) for k in brought]
    buffers += [pltpu.VMEM(*out) for out in outs]
    buffers += [pltpu.SemaphoreType.DMA((len(brought) + len(outs) + SPARE,))]
    buffers += [
        pltpu.VMEM(*s) if isinstance(s, tuple) else pltpu.SemaphoreType.DMA((s,)) for s in scratch
    ]
    return pl.pallas_call(
        kernel,
        in_specs=[HB if spec is IN else spec for spec in specs],
        out_specs=[HB] * len(outs),
        out_shape=[jax.ShapeDtypeStruct(s, t) for s, t in outs],
        scratch_shapes=buffers,
        compiler_params=pltpu.CompilerParams(vmem_limit_bytes=63 * 1024 * 1024),
        cost_estimate=pl.CostEstimate(flops=flops, bytes_accessed=flops >> 9, transcendentals=0),
    )(*args)


def plain_call(body, args, outs, scratch):
    return pl.pallas_call(
        body,
        in_specs=[SM] + [VM] * (len(args) - 1),
        out_specs=[VM] * len(outs),
        out_shape=[jax.ShapeDtypeStruct(s, t) for s, t in outs],
        scratch_shapes=[pltpu.VMEM(*s) for s in scratch],
        cost_estimate=pl.CostEstimate(flops=1 << 20, bytes_accessed=1 << 18, transcendentals=0),
    )(*args)


SQUARE = ((4, D, D), BF16)
TALL = ((BLOCKS, 4, 16, D), BF16)
ACC = ((D, D), BF16)
TURN = ((D, SEQ), BF16)
BIAS = ((SEQ, SEQ), F32)
BACK = [act_shape()] * 2 + [TURN] * 3 + [act_shape(), TURN, TURN, act_shape(), act_shape()]
BACK = BACK + [act_shape(F32)] * 2


def pairs(axis, step):
    k = AXES.index(axis)
    found = []

    def flat(place):
        index = 0
        for at, size in zip(place, SIZES):
            index = index * size + at
        return index

    for place in itertools.product(*[range(size) for size in SIZES]):
        if axis == "c":
            other = 1
        elif axis == "z":
            other = step
        else:
            other = 1 if (step == 0) == (place[1] == 0) else 3
        target = list(place)
        target[k] = place[k] ^ other
        found.append((flat(place), flat(target)))
    return found


def swap(values, axis, step=0):
    return lax.ppermute(values, AXES, pairs(axis, step))


def away(core, order):
    hop = 1 if core == 0 else 3
    return (0, hop, 4 - hop, 2)[order]


def tables():
    found = []
    for x, c, y, z in itertools.product(*[range(size) for size in SIZES]):
        row_a, row_b = [], []
        for j in range(2):
            core = c ^ j
            for slot in range(16):
                one, two = away(core, slot % 4), away(core, slot // 4)
                row_a.append((x ^ one) * 8 + core * 4 + (y ^ two))
                row_b.append((x ^ two) * 8 + core * 4 + (y ^ one))
        found.append(row_a + row_b + list(np.argsort(row_a)) + list(np.argsort(row_b)) + [c])
    return np.array(found, np.int32)


def step_all(parts):
    received = [swap(*part) for part in parts]
    return lax.optimization_barrier(tuple(received))


def join(values, received):
    return jnp.concatenate([values, received], axis=0)


def by_z(arrived):
    me = lax.axis_index("z")
    found = []
    for z in range(4):
        distance = me ^ z
        part = arrived[3]
        for k in range(3):
            part = jnp.where(distance == k, arrived[k], part)
        found.append(part)
    narrow = jnp.stack([part[:84].reshape(21, 4, D) for part in found], axis=1).reshape(21 * 16, D)
    enc = [part[96:112] for part in found]
    dec = [part[112:] for part in found]
    return (
        jnp.concatenate([narrow[:112], narrow[144:208], *dec]),
        jnp.concatenate([narrow[112:144], *enc, narrow[208:]]),
    )


def parted(values, received, units, cut):
    values = values.reshape(4, units * 16, D)
    received = received.reshape(4, units * 16, D)
    return [
        jnp.concatenate([values[:, part], received[:, part]]).reshape(-1, D)
        for part in (slice(0, cut * 16), slice(cut * 16, None))
    ]


def gather(table, packed):
    table, *others = lax.optimization_barrier(
        (table, *[swap(packed, "z", distance) for distance in (1, 2, 3)])
    )
    one, two = by_z([packed, *others])
    for step in range(2):
        got = step_all([(one, "x", step), (two, "y", step)])
        one, two = join(one, got[0]), join(two, got[1])
    got = step_all([(one, "y", 0), (two, "x", 0)])
    one_enc, one_dec = parted(one, got[0], 15, 7)
    two_enc, two_dec = parted(two, got[1], 14, 6)
    enc = [swap(one_enc, "y", 1), swap(two_enc, "x", 1), swap(one_enc, "c"), swap(two_enc, "c")]
    *enc, one_dec, two_dec = lax.optimization_barrier((*enc, one_dec, two_dec))
    dec = swap(one_dec, "y", 1), swap(two_dec, "x", 1), swap(one_dec, "c"), swap(two_dec, "c")
    return table, pieces_of((one_enc, two_enc), enc, (7, 6)), (one_dec, two_dec), dec


def pieces_of(low, got, units):
    found = []
    for k in range(2):
        for piece in (low[k], got[k], got[2 + k], swap(got[k], "c")):
            found.append(piece.reshape(8, units[k], 16, D))
    return found


def add(left, right):
    return left + right


def fold(values, received):
    half = values.shape[0] // 2
    return add(values[:half], received[:half]), add(values[half:], received[half:])


def beside(left, right):
    return jnp.concatenate([left, right], axis=1)


def z_parts(values, wide):
    me = lax.axis_index("z")
    parts = values.reshape(-1, 4, 4, D)
    found = []
    for distance in range(4):
        want = me ^ distance
        picked, tall = parts[:, 3], parts[wide + 3]
        for z in range(3):
            picked = jnp.where(want == z, parts[:, z], picked)
            tall = jnp.where(want == z, parts[wide + z], tall)
        found.append(jnp.concatenate([picked[:wide], tall, picked[wide + 4 :]]))
    return found


def per_device(
    source, target, source_lengths, target_lengths, lang_ids, out_cotangent,
    enc_attn, enc_vectors, enc_w_in, enc_b_in, enc_w_out,
    dec_self, dec_cross, dec_vectors, dec_w_in, dec_b_in, dec_w_out, lang_table,
):
    spot = (lax.axis_index("z") + 4 * (lax.axis_index("y") % 2)).reshape(1)
    (packed,) = plain_call(
        pack_kernel,
        (
            spot, enc_attn, enc_w_in, enc_w_out, dec_self, dec_cross, dec_w_in, dec_w_out,
            enc_vectors.T, dec_vectors.T, lang_table.T, enc_b_in.reshape(1, 16), dec_b_in.reshape(1, 16),
        ),
        [((128, D), BF16)],
        [((8, 128), F32), ((128, D), F32)],
    )
    me = lax.axis_index(AXES)
    table = lax.dynamic_index_in_dim(jnp.asarray(tables()), me, 0, keepdims=False)
    table, g_enc, low_dec, got_dec = gather(table, packed)
    vecs, b_enc, b_dec, *kept, e_mid, e_n2, memory = call(
        encoder_kernel,
        (table, source_lengths, source[0], *g_enc),
        [SM] * 2 + [IN] + [HB] * 8,
        [((128, D), F32), ((1, FF), F32), ((1, FF), F32)]
        + KEPT
        + [act_shape(F32), act_shape(), act_shape()],
        [((1, D, D), BF16), SQUARE, SQUARE, TALL, BIAS, act_shape(F32), 4],
        1 << 12,
    )
    memory, *got_dec = lax.optimization_barrier((memory, *got_dec))
    g_dec = pieces_of(low_dec, got_dec, (8, 8))
    dec_out, p_dec, q_dec, other, g_start, g_memory, g_vec, g_bias_dec = call(
        first_kernel,
        (
            table, source_lengths, target_lengths, lang_ids, vecs,
            target[0], memory, out_cotangent[0], b_dec, *g_dec,
        ),
        [SM] * 4 + [IN] * 5 + [HB] * 8,
        [act_shape(), units_of(6), units_of(10), units_of(16)]
        + [act_shape(F32), act_shape(F32), ((128, D), F32), ((1, FF), F32)],
        KEPT
        + KEPT
        + [SQUARE, SQUARE, SQUARE, TALL, BIAS, BIAS]
        + [act_shape(F32)] * 4
        + [act_shape()] * 3
        + [act_shape(F32)] * 2
        + [ACC, TURN, TURN, act_shape()]
        + BACK
        + [4],
        15 * 10**9,
    )
    got = swap(other, "c")
    p_enc, q_enc, other, g_source = call(
        second_kernel,
        (
            table, g_memory, e_n2, b_enc, vecs, e_mid, *kept, source[0], g_vec, g_bias_dec, *g_enc,
        ),
        [SM] + [IN] * 16 + [HB] * 8,
        [units_of(8), units_of(5), units_of(13), act_shape(F32)],
        [SQUARE, SQUARE, TALL, act_shape(F32), act_shape(), ACC, TURN, act_shape(), act_shape()]
        + [act_shape(F32), act_shape(F32), ((1, FF), F32), ((128, D), F32), ((D, D), F32)]
        + BACK
        + [3],
        8 * 10**9,
    )
    other, got = lax.optimization_barrier((other, got))
    again = swap(other, "c")
    p_low, p_high = fold(p_dec, got[:, :6])
    q_low, q_high = fold(q_dec, got[:, 6:])
    p_got, q_got = swap(p_high, "y", 1), swap(q_high, "x", 1)
    one_low, one_high = fold(p_enc, again[:, :8])
    two_low, two_high = fold(q_enc, again[:, 8:])
    p_got, q_got, one_got, two_got = lax.optimization_barrier(
        (p_got, q_got, swap(one_high, "y", 1), swap(two_high, "x", 1))
    )
    p_low, p_high = map(beside, fold(p_low, p_got), fold(one_low, one_got))
    q_low, q_high = map(beside, fold(q_low, q_got), fold(two_low, two_got))
    for axes, step in ((("y", "x"), 0), (("x", "y"), 1)):
        p_got, q_got = step_all([(p_high, axes[0], step), (q_high, axes[1], step)])
        p_low, p_high = fold(p_low, p_got)
        q_low, q_high = fold(q_low, q_got)
    p_got, q_got = step_all([(p_high, "x", 0), (q_high, "y", 0)])
    p_parts = z_parts(add(p_low, p_got)[0], 10)
    q_parts = z_parts(add(q_low, q_got)[0], 6)
    mine, *others = map(lambda *part: jnp.concatenate(part), p_parts, q_parts)
    got = [swap(part, "z", k + 1) for k, part in enumerate(others)]
    quarter, four = ((4, FF), F32), ((4, 4, D), F32)
    (
        d_attn, d_vec_e, d_w_in, d_b_e, d_w_out, d_self, d_cross, d_vec_d, d_dec_in, d_b_d, d_dec_out, d_lang,
    ) = plain_call(
        unpack_kernel,
        (spot, mine, *got),
        [four, ((4, 8), F32), quarter, ((1, 16), F32), ((16, D), F32), four, four]
        + [((4, 13), F32), quarter, ((1, 16), F32), ((16, D), F32), ((4, LANGS), F32)],
        [((4, D), F32)],
    )
    return (
        dec_out[None],
        g_source[None],
        g_start[None],
        d_attn,
        d_vec_e.T,
        d_w_in,
        d_b_e.reshape(16),
        d_w_out,
        d_self,
        d_cross,
        d_vec_d.T,
        d_dec_in,
        d_b_d.reshape(16),
        d_dec_out,
        d_lang.T,
    )


def solution(mesh):
    fine = Mesh(mesh.devices.reshape(SIZES), AXES)
    flat = AXES
    in_specs = (
        P(flat, None, None),
        P(flat, None, None),
        P(flat, None),
        P(flat, None),
        P(flat, None),
        P(flat, None, None),
        P(None, flat, None),
        P(None, flat),
        P(flat, None),
        P(flat),
        P(flat, None),
        P(None, flat, None),
        P(None, flat, None),
        P(None, flat),
        P(flat, None),
        P(flat),
        P(flat, None),
        P(None, flat),
    )
    out_specs = (
        P(flat, None, None),
        P(flat, None, None),
        P(flat, None, None),
        P(None, flat, None),
        P(None, flat),
        P(flat, None),
        P(flat),
        P(flat, None),
        P(None, flat, None),
        P(None, flat, None),
        P(None, flat),
        P(flat, None),
        P(flat),
        P(flat, None),
        P(None, flat),
    )
    return jax.shard_map(
        per_device, mesh=fine, in_specs=in_specs, out_specs=out_specs, check_vma=False
    )
```

```python
import itertools

import jax
import jax.numpy as jnp
import numpy as np
from jax import lax
from jax.experimental import pallas as pl
from jax.experimental.pallas import tpu as pltpu
from jax.sharding import Mesh
from jax.sharding import PartitionSpec as P

D = 512
HEADS = 8
HEAD_DIM = 64
FF = 2048
LANGS = 100
SEQ = 384
DOCS = 5
EPSILON = 1e-05
NEGATIVE = -1000000000.0
OPEN = 3e38
SCALE = HEAD_DIM ** (-0.5)
AXES = ("x", "c", "y", "z")
SIZES = (4, 2, 4, 4)
BLOCKS = 32
ENC_VEC = 104
DEC_VEC = 112
CHUNK = 128
CHUNKS = SEQ // CHUNK
TAB_A, TAB_B, SLOT_A, SLOT_B, CORE = 0, 32, 64, 96, 128
F32 = jnp.float32
BF16 = jnp.bfloat16


def dot(left, right):
    return lax.dot_general(left, right, (((1,), (0,)), ((), ())), preferred_element_type=F32)


def dot_nt(left, right):
    return lax.dot_general(left, right, (((1,), (1,)), ((), ())), preferred_element_type=F32)


def rows(index, size=CHUNK):
    return slice(index * size, (index + 1) * size)


def normed(values):
    mean = jnp.mean(values, axis=-1, keepdims=True)
    center = values - mean
    rstd = lax.rsqrt(jnp.mean(center * center, axis=-1, keepdims=True) + EPSILON)
    return center * rstd, rstd


def layer_norm(source, gain, shift, out):
    for i in range(CHUNKS):
        hat, _ = normed(source[rows(i), :])
        out[rows(i), :] = (hat * gain + shift).astype(BF16)


def norm_back(source, gain, grad, base, out):
    d_gain = jnp.zeros((1, D), F32)
    d_shift = jnp.zeros((1, D), F32)
    for i in range(CHUNKS):
        hat, rstd = normed(source[rows(i), :])
        dy = grad[rows(i), :]
        d_gain = d_gain + jnp.sum(dy * hat, axis=0, keepdims=True)
        d_shift = d_shift + jnp.sum(dy, axis=0, keepdims=True)
        dyg = dy * gain
        mean_one = jnp.mean(dyg, axis=-1, keepdims=True)
        mean_two = jnp.mean(dyg * hat, axis=-1, keepdims=True)
        out[rows(i), :] = base[rows(i), :].astype(F32) + rstd * (dyg - mean_one - hat * mean_two)
    return d_gain, d_shift


def low_lanes(count):
    return lax.broadcasted_iota(jnp.int32, (count, 128), 1) < HEAD_DIM


def head_mask():
    lane = lax.broadcasted_iota(jnp.int32, (1, D), 1)
    return ((lane // HEAD_DIM) % 2 == 0).astype(F32)


def doc_ids(lengths, shape, axis):
    position = lax.broadcasted_iota(jnp.int32, shape, axis)
    total = jnp.zeros(shape, jnp.int32)
    end = 0
    for i in range(DOCS):
        end = end + lengths[0, i]
        total = total + (position >= end).astype(jnp.int32)
    return total


def masks(s_len, t_len, bias_s, bias_c):
    s_row = doc_ids(s_len, (1, SEQ), 1)
    t_row = doc_ids(t_len, (1, SEQ), 1)
    t_col = doc_ids(t_len, (SEQ, 1), 0)
    key = lax.broadcasted_iota(jnp.int32, (SEQ, SEQ), 1)
    query = lax.broadcasted_iota(jnp.int32, (SEQ, SEQ), 0)
    bias_s[...] = jnp.where((t_col == t_row) & (key <= query), OPEN, NEGATIVE)
    bias_c[...] = jnp.where(t_col == s_row, OPEN, NEGATIVE)


def lang_onehot(t_len, langs):
    doc = doc_ids(t_len, (SEQ, 128), 0)
    lang = jnp.zeros((SEQ, 128), jnp.int32)
    for i in range(DOCS):
        lang = jnp.where(doc == i, langs[0, i], lang)
    lane = lax.broadcasted_iota(jnp.int32, (SEQ, 128), 1)
    return jnp.where(lang == lane, 1.0, 0.0).astype(BF16)


def attn_project(query_in, memory, weights, bias_q, bias_v, q_even, q_odd, keys, values):
    even = head_mask()
    q = SCALE * (dot(query_in[...], weights[0]) + bias_q)
    q_even[...] = (q * even).astype(BF16)
    q_odd[...] = (q * (1.0 - even)).astype(BF16)
    keys[...] = dot(memory[...], weights[1]).astype(BF16)
    values[...] = (dot(memory[...], weights[2]) + bias_v).astype(BF16)


def attn_core(q_even, q_odd, keys, values, bias, probs, inverse, context):
    low = low_lanes(SEQ)
    queries = (q_even, q_odd)
    held = []

    def lanes(head):
        return rows(head // 2, 128)

    def scores(head):
        return dot_nt(queries[head % 2][:, lanes(head)], keys[:, lanes(head)])

    def finish(head, e, total):
        over = 1.0 / total
        held.append((dot(e, values[:, lanes(head)]) * over, over))
        if head % 2 == 1:
            (one, over_one), (two, over_two) = held
            held.clear()
            context[:, lanes(head)] = jnp.where(low, one, two).astype(BF16)
            inverse[:, lanes(head)] = jnp.where(low, over_one, over_two)

    s = scores(0)
    last = None
    for head in range(HEADS):
        s_next = scores(head + 1) if head + 1 < HEADS else None
        s = jnp.minimum(s, bias[...])
        e = jnp.exp(s - jnp.max(s, axis=-1, keepdims=True))
        total = jnp.sum(e, axis=-1, keepdims=True)
        e = e.astype(BF16)
        probs[head] = e
        if last is not None:
            finish(*last)
        last = (head, e, total)
        s = s_next
    finish(*last)


def attn_output(context, weight, bias_o, residual, out):
    branch = dot(context[...], weight[...]) + bias_o
    out[...] = residual[...].astype(F32) + branch


def put_blocks(acc, place):
    refs, units, table, first = place
    for slot in range(16):
        for j in range(2):
            start = pl.multiple_of(table[first + 16 * j + slot] * 16, 16)
            refs[j][slot, units[j]] = acc[pl.ds(start, 16), :].astype(BF16)


def place_of(own, other, unit, shift, table, first):
    return (own, other), (unit, unit + shift), table, first


def weight_grad(left_t, right, acc, place, scale=None):
    value = dot(left_t[...], right[...])
    acc[...] = (value if scale is None else value * scale).astype(BF16)
    put_blocks(acc, place)


def tall_grad(left_t, right, acc, place, chunk):
    refs, units, table, slots = place
    acc[...] = dot(left_t, right[...]).astype(BF16)
    for j in range(2):
        core = table[CORE] ^ j
        for y in range(4):
            slot = table[slots + chunk * 8 + core * 4 + y] - 16 * j
            for z in range(4):
                start = pl.multiple_of(core * 256 + y * 64 + z * 16, 16)
                refs[j][slot, units[j] + z] = acc[pl.ds(start, 16), :].astype(BF16)


def column_sum(ref):
    return jnp.sum(ref[...].astype(F32), axis=0, keepdims=True)


def attn_back(grad, query_in_t, memory_t, weights, kept, scratch, acc, places):
    q_even, q_odd, keys, values, probs, inverse, context = kept
    d_even, d_odd, dc_t, q_t, c_t, dq, dk_t, dv_t, dk, dv, du, dm = scratch
    even = head_mask()
    dc = dot_nt(grad[...], weights[3]) * inverse[...]
    d_even[...] = (dc * even).astype(BF16)
    d_odd[...] = (dc * (1.0 - even)).astype(BF16)
    dc_t[...] = (d_even[...] + d_odd[...]).T
    q_t[...] = (q_even[...] + q_odd[...]).T
    c_t[...] = context[...].T
    low = low_lanes(SEQ)
    d_ctx = (d_even, d_odd)
    held = []

    def lanes(head):
        return rows(head // 2, 128)

    def first(head):
        dch = d_ctx[head % 2][:, lanes(head)]
        total = jnp.sum(
            dch.astype(F32) * context[:, lanes(head)].astype(F32), axis=-1, keepdims=True
        )
        return dot_nt(dch, values[:, lanes(head)]), total

    def finish(head, ds):
        span = rows(head, HEAD_DIM)
        held.append(dot(ds, keys[:, lanes(head)]))
        dk_t[span, :] = dot(q_t[span, :], ds).astype(BF16)
        dv_t[span, :] = dot(dc_t[span, :], probs[head]).astype(BF16)
        if head % 2 == 1:
            dq[:, lanes(head)] = jnp.where(low, held[0], held[1]).astype(BF16)
            held.clear()

    now = first(0)
    last = None
    for head in range(HEADS):
        later = first(head + 1) if head + 1 < HEADS else None
        dp, total = now
        ds = (probs[head].astype(F32) * (dp - total)).astype(BF16)
        if last is not None:
            finish(*last)
        last = (head, ds)
        now = later
    finish(*last)
    dk[...] = dk_t[...].T
    dv[...] = dv_t[...].T
    weight_grad(query_in_t, dq, acc, places[0], SCALE)
    weight_grad(memory_t, dk, acc, places[1])
    weight_grad(memory_t, dv, acc, places[2])
    weight_grad(c_t, grad, acc, places[3])
    du[...] = SCALE * dot_nt(dq[...], weights[0])
    dm[...] = dot_nt(dk[...], weights[1]) + dot_nt(dv[...], weights[2])
    return SCALE * column_sum(dq), column_sum(dv), column_sum(grad)


def silu_parts(hidden):
    gate = 1.0 / (1.0 + jnp.exp(-hidden))
    return hidden * gate, gate


def feed_forward(inputs, w_in, b_in, w_out, bias, residual, out):
    total = residual[...] + bias
    for k in range(FF // D):
        active, _ = silu_parts(dot(inputs[...], w_in[k]) + b_in[:, rows(k, D)])
        total = total + dot(active.astype(BF16), w_out[k])
    out[...] = total


def feed_both(
    inputs, inputs_t, w_in, b_in, w_out, grad, act, dh, total, d_in, acc, places_in, place_out, b_grad
):
    hidden = dot(inputs[...], w_in[0]) + b_in[:, rows(0, D)]
    for k in range(FF // D):
        d_act = dot_nt(grad[...], w_out[k])
        active, gate = silu_parts(hidden)
        low = active.astype(BF16)
        act[...] = low
        d_hid = (d_act * (gate + active * (1.0 - gate))).astype(BF16)
        dh[...] = d_hid
        if k + 1 < FF // D:
            hidden = dot(inputs[...], w_in[k + 1]) + b_in[:, rows(k + 1, D)]
        if total is not None:
            total[...] = total[...] + dot(low, w_out[k])
        back = dot_nt(d_hid, w_in[k])
        d_in[...] = back if k == 0 else d_in[...] + back
        b_grad[:, rows(k, D)] = column_sum(dh)
        weight_grad(inputs_t, dh, acc, places_in[k])
        tall_grad(act[...].T, grad, acc, place_out, k)


def load(table, first, pieces, jobs):
    def step(slot, carry):
        for k, piece in enumerate(pieces):
            block = table[first + 8 * k + slot]
            start = pl.multiple_of(block * 16, 16)
            for unit, count, target, row, sem in jobs:
                if len(target.shape) == 4:
                    place = target.at[block]
                else:
                    place = target.at[pl.ds(row, count), pl.ds(start, 16), :]
                pltpu.make_async_copy(piece.at[slot, pl.ds(unit, count)], place, sem).start()
        return carry

    lax.fori_loop(0, 8, step, 0)


def arrived(target, sem):
    pltpu.make_async_copy(target, target, sem).wait()


class Wide:
    def __init__(self, ref):
        self.ref = ref

    def __getitem__(self, k):
        return self.ref[8 * k : 8 * k + 8].reshape(D, D)


def pack_kernel(
    spot, attn, w_in, w_out, self_w, cross, dec_in, dec_out, vec_e, vec_d, lang, b_e, b_d,
    packed, wide, buf,
):
    for k in range(4):
        buf[rows(k, 4), :] = attn[k].astype(F32)
        buf[rows(4 + k if k < 2 else 5 + k, 4), :] = w_in[:, rows(k, D)].astype(F32)
        buf[rows(9 + k, 4), :] = self_w[k].astype(F32)
        buf[rows(13 + k, 4), :] = cross[k].astype(F32)
        buf[rows(17 + k, 4), :] = dec_in[:, rows(k, D)].astype(F32)
    buf[84:96, :] = jnp.zeros((12, D), F32)
    buf[96:112, :] = w_out[...].astype(F32)
    buf[112:128, :] = dec_out[...].astype(F32)
    wide[...] = jnp.zeros(wide.shape, F32)
    wide[0:4, 0:LANGS] = lang[...].astype(F32)
    wide[0:4, ENC_VEC : ENC_VEC + 8] = vec_e[...].astype(F32)
    wide[0:4, DEC_VEC : DEC_VEC + 13] = vec_d[...].astype(F32)
    row = lax.broadcasted_iota(jnp.int32, (16, 128), 0)
    lane = lax.broadcasted_iota(jnp.int32, (16, 128), 1)
    place = jnp.where(lane == row + spot[0] * 16, 1.0, 0.0).astype(BF16)
    first = lax.broadcasted_iota(jnp.int32, (8, 128), 0) == 0
    buf[24:28, 0:128] = wide[0:4, :]
    for k, ref in enumerate((b_e, b_d)):
        spread = dot(jnp.broadcast_to(ref[...].astype(F32), (8, 16)).astype(BF16), place)
        wide[0:8, :] = jnp.where(first, spread, 0.0)
        buf[24:28, 128 + 128 * k : 256 + 128 * k] = wide[0:4, :]
    buf[24:28, 384:512] = jnp.zeros((4, 128), F32)
    packed[...] = buf[...].astype(BF16)


def unpack_kernel(
    spot, mine, got_one, got_two, got_three,
    attn, vec_e, w_in, b_e, w_out, self_w, cross, vec_d, dec_in, b_d, dec_out, lang,
    last,
):
    def total(index):
        found = mine[index].astype(F32) + got_one[index].astype(F32)
        return found + (got_two[index].astype(F32) + got_three[index].astype(F32))

    for k in range(4):
        dec_in[:, rows(k, D)] = total(k)
        cross[k] = total(4 + k)
        w_in[:, rows(k, D)] = total(8 + k)
        attn[k] = total(12 + k if k < 2 else 25 + k)
        self_w[k] = total(15 + k)
        dec_out[rows(k, 4), :] = total(19 + k)
        w_out[rows(k, 4), :] = total(23 + k)
    last[...] = total(14)
    lang[...] = last[:, 0:LANGS]
    vec_e[...] = last[:, ENC_VEC : ENC_VEC + 8]
    vec_d[...] = last[:, DEC_VEC : DEC_VEC + 13]
    for k, ref in enumerate((b_e, b_d)):
        tile = jnp.broadcast_to(last[0:1, 128 + 128 * k : 256 + 128 * k], (8, 128))
        ref[...] = pltpu.roll(tile, 128 - 16 * spot[0], 1)[0:1, 0:16]


class Copies:
    def __init__(self, incoming, outgoing, sem):
        self.waiting = {}
        self.flying = {}
        self.outgoing = {}
        self.sent = {}
        for index, (hbm, vmem) in enumerate(incoming):
            self.waiting[id(vmem)] = pltpu.make_async_copy(hbm, vmem, sem.at[index])
        for index, (hbm, vmem) in enumerate(outgoing):
            self.outgoing[id(vmem)] = (vmem, hbm, sem.at[len(incoming) + index])
        self.targets = {id(vmem): hbm for hbm, vmem in outgoing}
        self.spare = [sem.at[len(incoming) + len(outgoing) + k] for k in range(SPARE)]

    def bring(self, *refs):
        for ref in refs:
            copy = self.waiting.pop(id(ref))
            copy.start()
            self.flying[id(ref)] = copy

    def need(self, *refs):
        for ref in refs:
            self.flying.pop(id(ref)).wait()

    def send(self, *refs):
        for ref in refs:
            copy = pltpu.make_async_copy(*self.outgoing.pop(id(ref)))
            copy.start()
            self.sent[id(ref)] = copy

    def send_units(self, ref, first, last):
        self.outgoing.pop(id(ref), None)
        hbm = self.targets[id(ref)]
        part = (slice(None), slice(first, last))
        copy = pltpu.make_async_copy(ref.at[part], hbm.at[part], self.spare.pop())
        copy.start()
        self.sent[(id(ref), first)] = copy

    def free(self, *refs):
        for ref in refs:
            copy = self.sent.pop(id(ref))
            copy.wait()

    def finish(self):
        assert not self.waiting and not self.flying
        for key, (vmem, hbm, sem) in self.outgoing.items():
            copy = pltpu.make_async_copy(vmem, hbm, sem)
            copy.start()
            self.sent[key] = copy
        for copy in self.sent.values():
            copy.wait()


def encoder_kernel(
    io, table, s_len, source, a0, a1, a2, a3, b0, b1, b2, b3,
    vecs, b_enc, b_dec, e_n, e_qe, e_qo, e_k, e_v, e_p, e_i, e_c, e_mid, e_n2, memory,
    small, we, wi, wo, bias_e, buf, sem,
):
    io.bring(source)
    load(table, TAB_A, (a0, a1, a2, a3), ((6, 1, small, 0, sem.at[3]), (0, 4, we, 0, sem.at[0])))
    load(table, TAB_B, (b0, b1, b2, b3), ((0, 2, wi, 2, sem.at[1]), (2, 4, wo, 0, sem.at[2])))
    load(table, TAB_A, (a0, a1, a2, a3), ((4, 2, wi, 0, sem.at[1]),))
    s_row = doc_ids(s_len, (1, SEQ), 1)
    s_col = doc_ids(s_len, (SEQ, 1), 0)
    bias_e[...] = jnp.where(s_col == s_row, OPEN, NEGATIVE)
    arrived(small, sem.at[3])
    vecs[...] = small[0, :, 0:128].astype(F32).T
    for k, ref in enumerate((b_enc, b_dec)):
        for tile in range(FF // 128):
            part = small[0, rows(tile, 32), 128 + 128 * k : 256 + 128 * k].astype(F32)
            ref[:, rows(tile, 128)] = jnp.sum(part, axis=0, keepdims=True)

    def enc(index):
        return vecs[ENC_VEC + index : ENC_VEC + index + 1, :]

    io.need(source)
    buf[...] = source[...].astype(F32)
    layer_norm(buf, enc(0), enc(1), e_n)
    arrived(we, sem.at[0])
    attn_project(e_n, e_n, we, enc(2), enc(3), e_qe, e_qo, e_k, e_v)
    attn_core(e_qe, e_qo, e_k, e_v, bias_e, e_p, e_i, e_c)
    io.send(vecs, b_enc, b_dec, e_n, e_qe, e_qo, e_k, e_v, e_p, e_i, e_c)
    attn_output(e_c, we.at[3], enc(4), source, e_mid)
    layer_norm(e_mid, enc(5), enc(6), e_n2)
    io.send(e_mid, e_n2)
    arrived(wi, sem.at[1])
    arrived(wo, sem.at[2])
    feed_forward(e_n2, wi, b_enc, Wide(wo), enc(7), e_mid, buf)
    memory[...] = buf[...].astype(BF16)


def first_kernel(
    io, table, s_len, t_len, langs, vecs, target, memory, cot, b_dec,
    a0, a1, a2, a3, b0, b1, b2, b3,
    dec_out, d_p, d_q, d_other, g_start, g_memory, g_vec, g_bias,
    s_n, s_qe, s_qo, s_k, s_v, s_p, s_i, s_c, c_n, c_qe, c_qo, c_k, c_v, c_p, c_i, c_c,
    ws, wc, vi, vo, bias_s, bias_c, buf, start, first, second, n3,
    act, dh, d_in, g_first, acc, u_t, m_t, low,
    d_even, d_odd, dc_t, q_t, c_t, dq, dk_t, dv_t, dk, dv, du, dm, sem,
):
    io.bring(vecs, target)
    load(table, TAB_A, (a0, a1, a2, a3), ((0, 4, ws, 0, sem.at[0]),))
    masks(s_len, t_len, bias_s, bias_c)
    onehot = lang_onehot(t_len, langs)
    io.need(vecs, target)
    io.bring(memory, cot, b_dec)
    load(table, TAB_B, (b0, b1, b2, b3), ((0, 4, wc, 0, sem.at[1]), (4, 4, vi, 0, sem.at[2])))
    load(table, TAB_A, (a0, a1, a2, a3), ((4, 4, vo, 0, sem.at[3]),))

    def dec(index):
        return vecs[DEC_VEC + index : DEC_VEC + index + 1, :]

    start[...] = target[...].astype(F32) + dot(onehot, vecs[...].astype(BF16))
    layer_norm(start, dec(0), dec(1), s_n)
    arrived(ws, sem.at[0])
    attn_project(s_n, s_n, ws, dec(2), dec(3), s_qe, s_qo, s_k, s_v)
    attn_core(s_qe, s_qo, s_k, s_v, bias_s, s_p, s_i, s_c)
    attn_output(s_c, ws.at[3], dec(4), start, first)
    layer_norm(first, dec(5), dec(6), c_n)
    io.need(memory, cot, b_dec)
    arrived(wc, sem.at[1])
    attn_project(c_n, memory, wc, dec(7), dec(8), c_qe, c_qo, c_k, c_v)
    attn_core(c_qe, c_qo, c_k, c_v, bias_c, c_p, c_i, c_c)
    attn_output(c_c, wc.at[3], dec(9), first, second)
    layer_norm(second, dec(10), dec(11), n3)
    u_t[...] = n3[...].T
    buf[...] = second[...] + dec(12)
    arrived(vi, sem.at[2])
    arrived(vo, sem.at[3])

    def in_p(unit):
        return place_of(d_p, d_other, unit, 0, table, TAB_A)

    def in_q(unit):
        return place_of(d_q, d_other, unit, 8, table, TAB_B)

    feed_both(
        n3, u_t, vi, b_dec, Wide(vo), cot, act, dh, buf, d_in, acc,
        [in_p(k) for k in range(4)], place_of(d_q, d_other, 4, 8, table, SLOT_B), g_bias,
    )
    dec_out[...] = buf[...].astype(BF16)
    io.send(dec_out, g_bias)
    io.send_units(d_other, 0, 4)
    io.send_units(d_other, 12, 16)
    io.send_units(d_q, 4, 8)
    g_second = second
    gain_three = norm_back(second, dec(10), d_in, cot, g_second)
    scratch = (d_even, d_odd, dc_t, q_t, c_t, dq, dk_t, dv_t, dk, dv, du, dm)
    u_t[...] = c_n[...].T
    m_t[...] = memory[...].T
    low[...] = g_second[...].astype(BF16)
    bias_two = attn_back(
        low, u_t, m_t, wc, (c_qe, c_qo, c_k, c_v, c_p, c_i, c_c), scratch, acc,
        [in_p(4 + k) for k in range(4)],
    )
    io.send(d_p)
    io.send_units(d_other, 4, 8)
    g_memory[...] = dm[...]
    io.send(g_memory)
    gain_two = norm_back(first, dec(5), du, g_second, g_first)
    low[...] = g_first[...].astype(BF16)
    u_t[...] = s_n[...].T
    bias_one = attn_back(
        low, u_t, u_t, ws, (s_qe, s_qo, s_k, s_v, s_p, s_i, s_c), scratch, acc,
        [in_q(k) for k in range(4)],
    )
    io.send_units(d_other, 8, 12)
    io.send_units(d_q, 0, 4)
    du[...] = du[...] + dm[...]
    gain_one = norm_back(start, dec(0), du, g_first, g_start)
    io.send(g_start)
    g_vec[...] = lax.dot_general(
        onehot, g_start[...].astype(BF16), (((0,), (0,)), ((), ())), preferred_element_type=F32
    )
    values = gain_one + bias_one + gain_two + bias_two + gain_three + (column_sum(cot),)
    for i, value in enumerate(values):
        g_vec[DEC_VEC + i : DEC_VEC + i + 1, :] = value


def second_kernel(
    io, table, g_memory, e_n2, b_enc, vecs, e_mid, e_n, e_qe, e_qo, e_k, e_v, e_p, e_i, e_c,
    source, g_vec, g_bias_dec, a0, a1, a2, a3, b0, b1, b2, b3,
    d_p, d_q, d_other, g_source,
    we, wi, wo, buf, low, acc, u_t, act, dh, d_in, g_mid, b_grad, all_vec, turned,
    d_even, d_odd, dc_t, q_t, c_t, dq, dk_t, dv_t, dk, dv, du, dm, sem,
):
    io.bring(g_memory, e_n2, b_enc)
    load(table, TAB_A, (a0, a1, a2, a3), ((4, 2, wi, 0, sem.at[0]),))
    load(table, TAB_B, (b0, b1, b2, b3), ((0, 2, wi, 2, sem.at[0]), (2, 4, wo, 0, sem.at[1])))
    io.need(g_memory, e_n2, b_enc)
    u_t[...] = e_n2[...].T
    low[...] = g_memory[...].astype(BF16)
    bias_out = column_sum(low)
    arrived(wi, sem.at[0])
    arrived(wo, sem.at[1])
    io.bring(vecs, e_mid, e_n)
    load(table, TAB_A, (a0, a1, a2, a3), ((0, 4, we, 0, sem.at[2]),))
    io.bring(e_i, e_qe, e_qo, e_c, e_v, e_k, e_p, source, g_vec, g_bias_dec)

    def in_p(unit):
        return place_of(d_p, d_other, unit, 0, table, TAB_A)

    def in_q(unit):
        return place_of(d_q, d_other, unit, 7, table, TAB_B)

    feed_both(
        e_n2, u_t, wi, b_enc, Wide(wo), low, act, dh, None, d_in, acc,
        [in_p(k) for k in range(4)], place_of(d_q, d_other, 0, 7, table, SLOT_B), b_grad,
    )
    io.send_units(d_p, 0, 4)
    io.send_units(d_other, 0, 4)
    io.send_units(d_other, 7, 11)
    io.need(vecs, e_mid, e_n)
    gain_two = norm_back(e_mid, vecs[ENC_VEC + 5 : ENC_VEC + 6, :], d_in, g_memory, g_mid)
    low[...] = g_mid[...].astype(BF16)
    u_t[...] = e_n[...].T
    io.need(e_i, e_qe, e_qo, e_c, e_v, e_k, e_p)
    arrived(we, sem.at[2])
    scratch = (d_even, d_odd, dc_t, q_t, c_t, dq, dk_t, dv_t, dk, dv, du, dm)
    bias_one = attn_back(
        low, u_t, u_t, we, (e_qe, e_qo, e_k, e_v, e_p, e_i, e_c), scratch, acc,
        [in_p(4), in_p(5), in_q(4), in_q(5)],
    )
    io.send(d_q)
    io.send_units(d_p, 4, 6)
    io.send_units(d_other, 4, 6)
    io.send_units(d_other, 11, 13)
    du[...] = du[...] + dm[...]
    io.need(source, g_vec, g_bias_dec)
    buf[...] = source[...].astype(F32)
    gain_one = norm_back(buf, vecs[ENC_VEC : ENC_VEC + 1, :], du, g_mid, g_source)
    io.send(g_source)
    all_vec[...] = g_vec[...]
    for i, value in enumerate(gain_one + bias_one + gain_two + (bias_out,)):
        all_vec[ENC_VEC + i : ENC_VEC + i + 1, :] = value
    turned[:, 0:128] = all_vec[...].T
    for block in range(BLOCKS):
        tile = rows(block // 2, 128)
        turned[rows(block, 16), 128:256] = jnp.broadcast_to(b_grad[:, tile], (16, 128))
        turned[rows(block, 16), 256:384] = jnp.broadcast_to(g_bias_dec[:, tile], (16, 128))
        turned[rows(block, 16), 384:512] = jnp.zeros((16, 128), F32)
    put_blocks(turned, in_p(6))
    io.send_units(d_p, 6, 7)
    io.send_units(d_other, 6, 7)


VM = pl.BlockSpec(memory_space=pltpu.VMEM)
SM = pl.BlockSpec(memory_space=pltpu.SMEM)
HB = pl.BlockSpec(memory_space=pl.ANY)
IN = object()
SPARE = 8


def units_of(count):
    return ((16, count, 16, D), BF16)


def act_shape(dtype=BF16):
    return ((SEQ, D), dtype)


KEPT = [act_shape()] * 5 + [((HEADS, SEQ, SEQ), BF16), act_shape(F32), act_shape()]


def call(body, args, specs, outs, scratch, flops):
    brought = [k for k, spec in enumerate(specs) if spec is IN]

    def kernel(*refs):
        refs = list(refs)
        ins, refs = refs[: len(args)], refs[len(args) :]
        targets, refs = refs[: len(outs)], refs[len(outs) :]
        staged_in, refs = refs[: len(brought)], refs[len(brought) :]
        staged_out, refs = refs[: len(outs)], refs[len(outs) :]
        sem, refs = refs[0], refs[1:]
        pairs_in = []
        for k, ref in zip(brought, staged_in):
            pairs_in.append((ins[k], ref))
            ins[k] = ref
        copies = Copies(pairs_in, list(zip(targets, staged_out)), sem)
        body(copies, *ins, *staged_out, *refs)
        copies.finish()

    buffers = [pltpu.VMEM(args[k].shape, args[k].dtype) for k in brought]
    buffers += [pltpu.VMEM(*out) for out in outs]
    buffers += [pltpu.SemaphoreType.DMA((len(brought) + len(outs) + SPARE,))]
    buffers += [
        pltpu.VMEM(*s) if isinstance(s, tuple) else pltpu.SemaphoreType.DMA((s,)) for s in scratch
    ]
    return pl.pallas_call(
        kernel,
        in_specs=[HB if spec is IN else spec for spec in specs],
        out_specs=[HB] * len(outs),
        out_shape=[jax.ShapeDtypeStruct(s, t) for s, t in outs],
        scratch_shapes=buffers,
        compiler_params=pltpu.CompilerParams(vmem_limit_bytes=63 << 20),
        cost_estimate=pl.CostEstimate(flops=flops, bytes_accessed=flops >> 9, transcendentals=0),
    )(*args)


def plain_call(body, args, outs, scratch):
    return pl.pallas_call(
        body,
        in_specs=[SM] + [VM] * (len(args) - 1),
        out_specs=[VM] * len(outs),
        out_shape=[jax.ShapeDtypeStruct(s, t) for s, t in outs],
        scratch_shapes=[pltpu.VMEM(*s) for s in scratch],
        cost_estimate=pl.CostEstimate(flops=1 << 20, bytes_accessed=1 << 18, transcendentals=0),
    )(*args)


SQUARE = ((4, D, D), BF16)
TALL = ((BLOCKS, 4, 16, D), BF16)
ACC = ((D, D), BF16)
TURN = ((D, SEQ), BF16)
BIAS = ((SEQ, SEQ), F32)
BACK = [act_shape()] * 2 + [TURN] * 3 + [act_shape(), TURN, TURN, act_shape(), act_shape()]
BACK = BACK + [act_shape(F32)] * 2


def pairs(axis, step):
    k = AXES.index(axis)
    found = []

    def flat(place):
        index = 0
        for at, size in zip(place, SIZES):
            index = index * size + at
        return index

    for place in itertools.product(*[range(size) for size in SIZES]):
        if axis == "c":
            other = 1
        elif axis == "z":
            other = step
        else:
            other = 1 if (step == 0) == (place[1] == 0) else 3
        target = list(place)
        target[k] = place[k] ^ other
        found.append((flat(place), flat(target)))
    return found


def swap(values, axis, step=0):
    return lax.ppermute(values, AXES, pairs(axis, step))


def away(core, order):
    hop = 1 if core == 0 else 3
    return (0, hop, 4 - hop, 2)[order]


def tables():
    found = []
    for x, c, y, z in itertools.product(*[range(size) for size in SIZES]):
        row_a, row_b = [], []
        for j in range(2):
            core = c ^ j
            for slot in range(16):
                one, two = away(core, slot % 4), away(core, slot // 4)
                row_a.append((x ^ one) * 8 + core * 4 + (y ^ two))
                row_b.append((x ^ two) * 8 + core * 4 + (y ^ one))
        found.append(row_a + row_b + list(np.argsort(row_a)) + list(np.argsort(row_b)) + [c])
    return np.array(found, np.int32)


def step_all(parts):
    received = [swap(*part) for part in parts]
    return lax.optimization_barrier(tuple(received))


def join(values, received):
    return jnp.concatenate([values, received], axis=0)


def by_z(arrived):
    me = lax.axis_index("z")
    found = []
    for z in range(4):
        distance = me ^ z
        part = arrived[3]
        for k in range(3):
            part = jnp.where(distance == k, arrived[k], part)
        found.append(part)
    narrow = jnp.stack([part[:84].reshape(21, 4, D) for part in found], axis=1).reshape(21 * 16, D)
    enc = [part[96:112] for part in found]
    dec = [part[112:] for part in found]
    return (
        jnp.concatenate([narrow[:112], narrow[144:208], *dec]),
        jnp.concatenate([narrow[112:144], *enc, narrow[208:]]),
    )


def parted(values, received, units, cut):
    values = values.reshape(4, units * 16, D)
    received = received.reshape(4, units * 16, D)
    return [
        jnp.concatenate([values[:, part], received[:, part]]).reshape(-1, D)
        for part in (slice(0, cut * 16), slice(cut * 16, None))
    ]


def gather(table, packed):
    table, *others = lax.optimization_barrier(
        (table, *[swap(packed, "z", distance) for distance in (1, 2, 3)])
    )
    one, two = by_z([packed, *others])
    for step in range(2):
        got = step_all([(one, "x", step), (two, "y", step)])
        one, two = join(one, got[0]), join(two, got[1])
    got = step_all([(one, "y", 0), (two, "x", 0)])
    one_enc, one_dec = parted(one, got[0], 15, 7)
    two_enc, two_dec = parted(two, got[1], 14, 6)
    enc = [swap(one_enc, "y", 1), swap(two_enc, "x", 1), swap(one_enc, "c"), swap(two_enc, "c")]
    *enc, one_dec, two_dec = lax.optimization_barrier((*enc, one_dec, two_dec))
    dec = swap(one_dec, "y", 1), swap(two_dec, "x", 1), swap(one_dec, "c"), swap(two_dec, "c")
    return table, pieces_of((one_enc, two_enc), enc, (7, 6)), (one_dec, two_dec), dec


def pieces_of(low, got, units):
    found = []
    for k in range(2):
        for piece in (low[k], got[k], got[2 + k], swap(got[k], "c")):
            found.append(piece.reshape(8, units[k], 16, D))
    return found


def add(left, right):
    return left + right


def fold(values, received):
    half = values.shape[0] // 2
    return add(values[:half], received[:half]), add(values[half:], received[half:])


def beside(left, right):
    return jnp.concatenate([left, right], axis=1)


def z_parts(values, wides):
    me = lax.axis_index("z")
    parts = values.reshape(-1, 4, 4, D)
    found = []
    for distance in range(4):
        want = me ^ distance
        picked = parts[:, 3]
        tall = [parts[wide + 3] for wide in wides]
        for z in range(3):
            picked = jnp.where(want == z, parts[:, z], picked)
            tall = [jnp.where(want == z, parts[w + z], t) for w, t in zip(wides, tall)]
        if wides:
            picked = jnp.concatenate([picked[: wides[0]], *tall, picked[wides[-1] + 4 :]])
        found.append(picked)
    return found


def per_device(
    source, target, source_lengths, target_lengths, lang_ids, out_cotangent,
    enc_attn, enc_vectors, enc_w_in, enc_b_in, enc_w_out,
    dec_self, dec_cross, dec_vectors, dec_w_in, dec_b_in, dec_w_out, lang_table,
):
    spot = (lax.axis_index("z") + 4 * (lax.axis_index("y") % 2)).reshape(1)
    (packed,) = plain_call(
        pack_kernel,
        (
            spot, enc_attn, enc_w_in, enc_w_out, dec_self, dec_cross, dec_w_in, dec_w_out,
            enc_vectors.T, dec_vectors.T, lang_table.T, enc_b_in.reshape(1, 16), dec_b_in.reshape(1, 16),
        ),
        [((128, D), BF16)],
        [((8, 128), F32), ((128, D), F32)],
    )
    me = lax.axis_index(AXES)
    table = lax.dynamic_index_in_dim(jnp.asarray(tables()), me, 0, keepdims=False)
    table, g_enc, low_dec, got_dec = gather(table, packed)
    vecs, b_enc, b_dec, *kept, e_mid, e_n2, memory = call(
        encoder_kernel,
        (table, source_lengths, source[0], *g_enc),
        [SM] * 2 + [IN] + [HB] * 8,
        [((128, D), F32), ((1, FF), F32), ((1, FF), F32)]
        + KEPT
        + [act_shape(F32), act_shape(), act_shape()],
        [((1, D, D), BF16), SQUARE, SQUARE, TALL, BIAS, act_shape(F32), 4],
        1 << 12,
    )
    memory, *got_dec = lax.optimization_barrier((memory, *got_dec))
    g_dec = pieces_of(low_dec, got_dec, (8, 8))
    dec_out, p_dec, q_dec, other, g_start, g_memory, g_vec, g_bias_dec = call(
        first_kernel,
        (
            table, source_lengths, target_lengths, lang_ids, vecs,
            target[0], memory, out_cotangent[0], b_dec, *g_dec,
        ),
        [SM] * 4 + [IN] * 5 + [HB] * 8,
        [act_shape(), units_of(8), units_of(8), units_of(16)]
        + [act_shape(F32), act_shape(F32), ((128, D), F32), ((1, FF), F32)],
        KEPT
        + KEPT
        + [SQUARE, SQUARE, SQUARE, TALL, BIAS, BIAS]
        + [act_shape(F32)] * 4
        + [act_shape()] * 3
        + [act_shape(F32)] * 2
        + [ACC, TURN, TURN, act_shape()]
        + BACK
        + [4],
        15 * 10**9,
    )
    got = swap(other, "c")
    p_enc, q_enc, other, g_source = call(
        second_kernel,
        (
            table, g_memory, e_n2, b_enc, vecs, e_mid, *kept, source[0], g_vec, g_bias_dec, *g_enc,
        ),
        [SM] + [IN] * 16 + [HB] * 8,
        [units_of(7), units_of(6), units_of(13), act_shape(F32)],
        [SQUARE, SQUARE, TALL, act_shape(F32), act_shape(), ACC, TURN, act_shape(), act_shape()]
        + [act_shape(F32), act_shape(F32), ((1, FF), F32), ((128, D), F32), ((D, D), F32)]
        + BACK
        + [3],
        8 * 10**9,
    )
    other, got = lax.optimization_barrier((other, got))
    again = swap(other, "c")
    p_low, p_high = fold(p_dec, got[:, :8])
    q_low, q_high = fold(q_dec, got[:, 8:])
    p_got, q_got = swap(p_high, "y", 1), swap(q_high, "x", 1)
    one_low, one_high = fold(p_enc, again[:, :7])
    two_low, two_high = fold(q_enc, again[:, 7:])
    p_got, q_got, one_got, two_got = lax.optimization_barrier(
        (p_got, q_got, swap(one_high, "y", 1), swap(two_high, "x", 1))
    )
    p_low, p_high = map(beside, fold(p_low, p_got), fold(one_low, one_got))
    q_low, q_high = map(beside, fold(q_low, q_got), fold(two_low, two_got))
    for axes, step in ((("y", "x"), 0), (("x", "y"), 1)):
        p_got, q_got = step_all([(p_high, axes[0], step), (q_high, axes[1], step)])
        p_low, p_high = fold(p_low, p_got)
        q_low, q_high = fold(q_low, q_got)
    p_got, q_got = step_all([(p_high, "x", 0), (q_high, "y", 0)])
    p_parts = z_parts(add(p_low, p_got)[0], ())
    q_parts = z_parts(add(q_low, q_got)[0], (4, 8))
    mine, *others = map(lambda *part: jnp.concatenate(part), p_parts, q_parts)
    got = [swap(part, "z", k + 1) for k, part in enumerate(others)]
    quarter, four = ((4, FF), F32), ((4, 4, D), F32)
    (
        d_attn, d_vec_e, d_w_in, d_b_e, d_w_out, d_self, d_cross, d_vec_d, d_dec_in, d_b_d, d_dec_out, d_lang,
    ) = plain_call(
        unpack_kernel,
        (spot, mine, *got),
        [four, ((4, 8), F32), quarter, ((1, 16), F32), ((16, D), F32), four, four]
        + [((4, 13), F32), quarter, ((1, 16), F32), ((16, D), F32), ((4, LANGS), F32)],
        [((4, D), F32)],
    )
    return (
        dec_out[None],
        g_source[None],
        g_start[None],
        d_attn,
        d_vec_e.T,
        d_w_in,
        d_b_e.reshape(16),
        d_w_out,
        d_self,
        d_cross,
        d_vec_d.T,
        d_dec_in,
        d_b_d.reshape(16),
        d_dec_out,
        d_lang.T,
    )


def solution(mesh):
    fine = Mesh(mesh.devices.reshape(SIZES), AXES)
    flat = AXES
    in_specs = (
        P(flat, None, None),
        P(flat, None, None),
        P(flat, None),
        P(flat, None),
        P(flat, None),
        P(flat, None, None),
        P(None, flat, None),
        P(None, flat),
        P(flat, None),
        P(flat),
        P(flat, None),
        P(None, flat, None),
        P(None, flat, None),
        P(None, flat),
        P(flat, None),
        P(flat),
        P(flat, None),
        P(None, flat),
    )
    out_specs = (
        P(flat, None, None),
        P(flat, None, None),
        P(flat, None, None),
        P(None, flat, None),
        P(None, flat),
        P(flat, None),
        P(flat),
        P(flat, None),
        P(None, flat, None),
        P(None, flat, None),
        P(None, flat),
        P(flat, None),
        P(flat),
        P(flat, None),
        P(None, flat),
    )
    return jax.shard_map(
        per_device, mesh=fine, in_specs=in_specs, out_specs=out_specs, check_vma=False
    )
```

```python
import itertools

import jax
import jax.numpy as jnp
import numpy as np
from jax import lax
from jax.experimental import pallas as pl
from jax.experimental.pallas import tpu as pltpu
from jax.sharding import Mesh
from jax.sharding import PartitionSpec as P

D = 512
HEADS = 8
HEAD_DIM = 64
FF = 2048
LANGS = 100
SEQ = 384
DOCS = 5
EPSILON = 1e-05
NEGATIVE = -1000000000.0
OPEN = 3e38
SCALE = HEAD_DIM ** (-0.5)
AXES = ("x", "c", "y", "z")
SIZES = (4, 2, 4, 4)
BLOCKS = 32
ENC_VEC = 104
DEC_VEC = 112
CHUNK = 128
CHUNKS = SEQ // CHUNK
TAB_A, TAB_B, SLOT_A, SLOT_B, CORE = 0, 32, 64, 96, 128
F32 = jnp.float32
BF16 = jnp.bfloat16


def dot(left, right):
    return lax.dot_general(left, right, (((1,), (0,)), ((), ())), preferred_element_type=F32)


def dot_nt(left, right):
    return lax.dot_general(left, right, (((1,), (1,)), ((), ())), preferred_element_type=F32)


def rows(index, size=CHUNK):
    return slice(index * size, (index + 1) * size)


def normed(values):
    mean = jnp.mean(values, axis=-1, keepdims=True)
    center = values - mean
    rstd = lax.rsqrt(jnp.mean(center * center, axis=-1, keepdims=True) + EPSILON)
    return center * rstd, rstd


def layer_norm(source, gain, shift, out):
    for i in range(CHUNKS):
        hat, _ = normed(source[rows(i), :])
        out[rows(i), :] = (hat * gain + shift).astype(BF16)


def norm_back(source, gain, grad, base, out):
    d_gain = jnp.zeros((1, D), F32)
    d_shift = jnp.zeros((1, D), F32)
    for i in range(CHUNKS):
        hat, rstd = normed(source[rows(i), :])
        dy = grad[rows(i), :]
        d_gain = d_gain + jnp.sum(dy * hat, axis=0, keepdims=True)
        d_shift = d_shift + jnp.sum(dy, axis=0, keepdims=True)
        dyg = dy * gain
        mean_one = jnp.mean(dyg, axis=-1, keepdims=True)
        mean_two = jnp.mean(dyg * hat, axis=-1, keepdims=True)
        out[rows(i), :] = base[rows(i), :].astype(F32) + rstd * (dyg - mean_one - hat * mean_two)
    return d_gain, d_shift


def low_lanes(count):
    return lax.broadcasted_iota(jnp.int32, (count, 128), 1) < HEAD_DIM


def head_mask():
    lane = lax.broadcasted_iota(jnp.int32, (1, D), 1)
    return ((lane // HEAD_DIM) % 2 == 0).astype(F32)


def doc_ids(lengths, shape, axis):
    position = lax.broadcasted_iota(jnp.int32, shape, axis)
    total = jnp.zeros(shape, jnp.int32)
    end = 0
    for i in range(DOCS):
        end = end + lengths[0, i]
        total = total + (position >= end).astype(jnp.int32)
    return total


def masks(s_len, t_len, bias_s, bias_c):
    s_row = doc_ids(s_len, (1, SEQ), 1)
    t_row = doc_ids(t_len, (1, SEQ), 1)
    t_col = doc_ids(t_len, (SEQ, 1), 0)
    key = lax.broadcasted_iota(jnp.int32, (SEQ, SEQ), 1)
    query = lax.broadcasted_iota(jnp.int32, (SEQ, SEQ), 0)
    bias_s[...] = jnp.where((t_col == t_row) & (key <= query), OPEN, NEGATIVE)
    bias_c[...] = jnp.where(t_col == s_row, OPEN, NEGATIVE)


def lang_onehot(t_len, langs):
    doc = doc_ids(t_len, (SEQ, 128), 0)
    lang = jnp.zeros((SEQ, 128), jnp.int32)
    for i in range(DOCS):
        lang = jnp.where(doc == i, langs[0, i], lang)
    lane = lax.broadcasted_iota(jnp.int32, (SEQ, 128), 1)
    return jnp.where(lang == lane, 1.0, 0.0).astype(BF16)


def attn_project(query_in, memory, weights, bias_q, bias_v, q_even, q_odd, keys, values):
    even = head_mask()
    q = SCALE * (dot(query_in[...], weights[0]) + bias_q)
    q_even[...] = (q * even).astype(BF16)
    q_odd[...] = (q * (1.0 - even)).astype(BF16)
    keys[...] = dot(memory[...], weights[1]).astype(BF16)
    values[...] = (dot(memory[...], weights[2]) + bias_v).astype(BF16)


def attn_core(q_even, q_odd, keys, values, bias, probs, inverse, context):
    low = low_lanes(SEQ)
    queries = (q_even, q_odd)
    held = []

    def lanes(head):
        return rows(head // 2, 128)

    def scores(head):
        return dot_nt(queries[head % 2][:, lanes(head)], keys[:, lanes(head)])

    def finish(head, e, total):
        over = 1.0 / total
        held.append((dot(e, values[:, lanes(head)]) * over, over))
        if head % 2 == 1:
            (one, over_one), (two, over_two) = held
            held.clear()
            context[:, lanes(head)] = jnp.where(low, one, two).astype(BF16)
            inverse[:, lanes(head)] = jnp.where(low, over_one, over_two)

    s = scores(0)
    last = None
    for head in range(HEADS):
        s_next = scores(head + 1) if head + 1 < HEADS else None
        s = jnp.minimum(s, bias[...])
        e = jnp.exp(s - jnp.max(s, axis=-1, keepdims=True))
        total = jnp.sum(e, axis=-1, keepdims=True)
        e = e.astype(BF16)
        probs[head] = e
        if last is not None:
            finish(*last)
        last = (head, e, total)
        s = s_next
    finish(*last)


def attn_output(context, weight, bias_o, residual, out):
    branch = dot(context[...], weight[...]) + bias_o
    out[...] = residual[...].astype(F32) + branch


def put_blocks(acc, place):
    refs, units, table, first = place
    for slot in range(16):
        for j in range(2):
            start = pl.multiple_of(table[first + 16 * j + slot] * 16, 16)
            refs[j][slot, units[j]] = acc[pl.ds(start, 16), :].astype(BF16)


def place_of(own, other, unit, shift, table, first):
    return (own, other), (unit, unit + shift), table, first


def weight_grad(left_t, right, acc, place, scale=None):
    value = dot(left_t[...], right[...])
    acc[...] = (value if scale is None else value * scale).astype(BF16)
    put_blocks(acc, place)


def tall_grad(left_t, right, acc, place, chunk):
    refs, units, table, slots = place
    acc[...] = dot(left_t, right[...]).astype(BF16)
    for j in range(2):
        core = table[CORE] ^ j
        for y in range(4):
            slot = table[slots + chunk * 8 + core * 4 + y] - 16 * j
            for z in range(4):
                start = pl.multiple_of(core * 256 + y * 64 + z * 16, 16)
                refs[j][slot, units[j] + z] = acc[pl.ds(start, 16), :].astype(BF16)


def column_sum(ref):
    return jnp.sum(ref[...].astype(F32), axis=0, keepdims=True)


def attn_back(grad, query_in_t, memory_t, weights, kept, scratch, acc, places):
    q_even, q_odd, keys, values, probs, inverse, context = kept
    d_even, d_odd, dc_t, q_t, c_t, dq, dk_t, dv_t, dk, dv, du, dm = scratch
    even = head_mask()
    dc = dot_nt(grad[...], weights[3]) * inverse[...]
    d_even[...] = (dc * even).astype(BF16)
    d_odd[...] = (dc * (1.0 - even)).astype(BF16)
    dc_t[...] = (d_even[...] + d_odd[...]).T
    q_t[...] = (q_even[...] + q_odd[...]).T
    c_t[...] = context[...].T
    low = low_lanes(SEQ)
    d_ctx = (d_even, d_odd)
    held = []

    def lanes(head):
        return rows(head // 2, 128)

    def first(head):
        dch = d_ctx[head % 2][:, lanes(head)]
        total = jnp.sum(
            dch.astype(F32) * context[:, lanes(head)].astype(F32), axis=-1, keepdims=True
        )
        return dot_nt(dch, values[:, lanes(head)]), total

    def finish(head, ds):
        span = rows(head, HEAD_DIM)
        held.append(dot(ds, keys[:, lanes(head)]))
        dk_t[span, :] = dot(q_t[span, :], ds).astype(BF16)
        dv_t[span, :] = dot(dc_t[span, :], probs[head]).astype(BF16)
        if head % 2 == 1:
            dq[:, lanes(head)] = jnp.where(low, held[0], held[1]).astype(BF16)
            held.clear()

    now = first(0)
    last = None
    for head in range(HEADS):
        later = first(head + 1) if head + 1 < HEADS else None
        dp, total = now
        ds = (probs[head].astype(F32) * (dp - total)).astype(BF16)
        if last is not None:
            finish(*last)
        last = (head, ds)
        now = later
    finish(*last)
    dk[...] = dk_t[...].T
    dv[...] = dv_t[...].T
    weight_grad(query_in_t, dq, acc, places[0], SCALE)
    weight_grad(memory_t, dk, acc, places[1])
    weight_grad(memory_t, dv, acc, places[2])
    weight_grad(c_t, grad, acc, places[3])
    du[...] = SCALE * dot_nt(dq[...], weights[0])
    dm[...] = dot_nt(dk[...], weights[1]) + dot_nt(dv[...], weights[2])
    return SCALE * column_sum(dq), column_sum(dv), column_sum(grad)


def silu_parts(hidden):
    gate = 1.0 / (1.0 + jnp.exp(-hidden))
    return hidden * gate, gate


def feed_forward(inputs, w_in, b_in, w_out, bias, residual, out):
    total = residual[...] + bias
    for k in range(FF // D):
        active, _ = silu_parts(dot(inputs[...], w_in[k]) + b_in[:, rows(k, D)])
        total = total + dot(active.astype(BF16), w_out[k])
    out[...] = total


def feed_both(
    inputs, inputs_t, w_in, b_in, w_out, grad, act, dh, total, d_in, acc, places_in, place_out, b_grad
):
    hidden = dot(inputs[...], w_in[0]) + b_in[:, rows(0, D)]
    for k in range(FF // D):
        d_act = dot_nt(grad[...], w_out[k])
        active, gate = silu_parts(hidden)
        low = active.astype(BF16)
        act[...] = low
        d_hid = (d_act * (gate + active * (1.0 - gate))).astype(BF16)
        dh[...] = d_hid
        if k + 1 < FF // D:
            hidden = dot(inputs[...], w_in[k + 1]) + b_in[:, rows(k + 1, D)]
        if total is not None:
            total[...] = total[...] + dot(low, w_out[k])
        back = dot_nt(d_hid, w_in[k])
        d_in[...] = back if k == 0 else d_in[...] + back
        b_grad[:, rows(k, D)] = column_sum(dh)
        weight_grad(inputs_t, dh, acc, places_in[k])
        tall_grad(act[...].T, grad, acc, place_out, k)


def load(table, first, pieces, jobs):
    def step(slot, carry):
        for k, piece in enumerate(pieces):
            block = table[first + 8 * k + slot]
            start = pl.multiple_of(block * 16, 16)
            for unit, count, target, row, sem in jobs:
                if len(target.shape) == 4:
                    place = target.at[block]
                else:
                    place = target.at[pl.ds(row, count), pl.ds(start, 16), :]
                pltpu.make_async_copy(piece.at[slot, pl.ds(unit, count)], place, sem).start()
        return carry

    lax.fori_loop(0, 8, step, 0)


def arrived(target, sem):
    pltpu.make_async_copy(target, target, sem).wait()


class Wide:
    def __init__(self, ref):
        self.ref = ref

    def __getitem__(self, k):
        return self.ref[8 * k : 8 * k + 8].reshape(D, D)


def pack_kernel(
    spot, attn, w_in, w_out, self_w, cross, dec_in, dec_out, vec_e, vec_d, lang, b_e, b_d,
    packed, wide, buf,
):
    for k in range(4):
        buf[rows(k, 4), :] = attn[k].astype(F32)
        buf[rows(4 + k if k < 2 else 5 + k, 4), :] = w_in[:, rows(k, D)].astype(F32)
        buf[rows(9 + k, 4), :] = self_w[k].astype(F32)
        buf[rows(13 + k, 4), :] = cross[k].astype(F32)
        buf[rows(17 + k, 4), :] = dec_in[:, rows(k, D)].astype(F32)
    buf[84:96, :] = jnp.zeros((12, D), F32)
    buf[96:112, :] = w_out[...].astype(F32)
    buf[112:128, :] = dec_out[...].astype(F32)
    wide[...] = jnp.zeros(wide.shape, F32)
    wide[0:4, 0:LANGS] = lang[...].astype(F32)
    wide[0:4, ENC_VEC : ENC_VEC + 8] = vec_e[...].astype(F32)
    wide[0:4, DEC_VEC : DEC_VEC + 13] = vec_d[...].astype(F32)
    row = lax.broadcasted_iota(jnp.int32, (16, 128), 0)
    lane = lax.broadcasted_iota(jnp.int32, (16, 128), 1)
    place = jnp.where(lane == row + spot[0] * 16, 1.0, 0.0).astype(BF16)
    first = lax.broadcasted_iota(jnp.int32, (8, 128), 0) == 0
    buf[24:28, 0:128] = wide[0:4, :]
    for k, ref in enumerate((b_e, b_d)):
        spread = dot(jnp.broadcast_to(ref[...].astype(F32), (8, 16)).astype(BF16), place)
        wide[0:8, :] = jnp.where(first, spread, 0.0)
        buf[24:28, 128 + 128 * k : 256 + 128 * k] = wide[0:4, :]
    buf[24:28, 384:512] = jnp.zeros((4, 128), F32)
    packed[...] = buf[...].astype(BF16)


def unpack_kernel(
    spot, mine, got_one, got_two, got_three,
    attn, vec_e, w_in, b_e, w_out, self_w, cross, vec_d, dec_in, b_d, dec_out, lang,
    last,
):
    def total(index):
        found = mine[index].astype(F32) + got_one[index].astype(F32)
        return found + (got_two[index].astype(F32) + got_three[index].astype(F32))

    for k in range(4):
        dec_in[:, rows(k, D)] = total(k)
        cross[k] = total(4 + k)
        w_in[:, rows(k, D)] = total(8 + k)
        attn[k] = total(12 + k if k < 2 else 25 + k)
        self_w[k] = total(15 + k)
        dec_out[rows(k, 4), :] = total(19 + k)
        w_out[rows(k, 4), :] = total(23 + k)
    last[...] = total(14)
    lang[...] = last[:, 0:LANGS]
    vec_e[...] = last[:, ENC_VEC : ENC_VEC + 8]
    vec_d[...] = last[:, DEC_VEC : DEC_VEC + 13]
    for k, ref in enumerate((b_e, b_d)):
        tile = jnp.broadcast_to(last[0:1, 128 + 128 * k : 256 + 128 * k], (8, 128))
        ref[...] = pltpu.roll(tile, 128 - 16 * spot[0], 1)[0:1, 0:16]


class Copies:
    def __init__(self, incoming, outgoing, sem):
        self.waiting = {}
        self.flying = {}
        self.outgoing = {}
        self.sent = {}
        for index, (hbm, vmem) in enumerate(incoming):
            self.waiting[id(vmem)] = pltpu.make_async_copy(hbm, vmem, sem.at[index])
        for index, (hbm, vmem) in enumerate(outgoing):
            self.outgoing[id(vmem)] = (vmem, hbm, sem.at[len(incoming) + index])
        self.targets = {id(vmem): hbm for hbm, vmem in outgoing}
        self.spare = [sem.at[len(incoming) + len(outgoing) + k] for k in range(SPARE)]

    def bring(self, *refs):
        for ref in refs:
            copy = self.waiting.pop(id(ref))
            copy.start()
            self.flying[id(ref)] = copy

    def need(self, *refs):
        for ref in refs:
            self.flying.pop(id(ref)).wait()

    def send(self, *refs):
        for ref in refs:
            copy = pltpu.make_async_copy(*self.outgoing.pop(id(ref)))
            copy.start()
            self.sent[id(ref)] = copy

    def send_units(self, ref, first, last):
        self.outgoing.pop(id(ref), None)
        hbm = self.targets[id(ref)]
        part = (slice(None), slice(first, last))
        copy = pltpu.make_async_copy(ref.at[part], hbm.at[part], self.spare.pop())
        copy.start()
        self.sent[(id(ref), first)] = copy

    def free(self, *refs):
        for ref in refs:
            copy = self.sent.pop(id(ref))
            copy.wait()

    def finish(self):
        assert not self.waiting and not self.flying
        for key, (vmem, hbm, sem) in self.outgoing.items():
            copy = pltpu.make_async_copy(vmem, hbm, sem)
            copy.start()
            self.sent[key] = copy
        for copy in self.sent.values():
            copy.wait()


def encoder_kernel(
    io, table, s_len, source, a0, a1, a2, a3, b0, b1, b2, b3,
    vecs, b_enc, b_dec, e_n, e_qe, e_qo, e_k, e_v, e_p, e_i, e_c, e_mid, e_n2, memory,
    small, we, wi, wo, bias_e, buf, sem,
):
    io.bring(source)
    load(table, TAB_A, (a0, a1, a2, a3), ((6, 1, small, 0, sem.at[3]), (0, 4, we, 0, sem.at[0])))
    load(table, TAB_B, (b0, b1, b2, b3), ((0, 2, wi, 2, sem.at[1]), (2, 4, wo, 0, sem.at[2])))
    load(table, TAB_A, (a0, a1, a2, a3), ((4, 2, wi, 0, sem.at[1]),))
    s_row = doc_ids(s_len, (1, SEQ), 1)
    s_col = doc_ids(s_len, (SEQ, 1), 0)
    bias_e[...] = jnp.where(s_col == s_row, OPEN, NEGATIVE)
    arrived(small, sem.at[3])
    vecs[...] = small[0, :, 0:128].astype(F32).T
    for k, ref in enumerate((b_enc, b_dec)):
        for tile in range(FF // 128):
            part = small[0, rows(tile, 32), 128 + 128 * k : 256 + 128 * k].astype(F32)
            ref[:, rows(tile, 128)] = jnp.sum(part, axis=0, keepdims=True)

    def enc(index):
        return vecs[ENC_VEC + index : ENC_VEC + index + 1, :]

    io.need(source)
    buf[...] = source[...].astype(F32)
    layer_norm(buf, enc(0), enc(1), e_n)
    arrived(we, sem.at[0])
    attn_project(e_n, e_n, we, enc(2), enc(3), e_qe, e_qo, e_k, e_v)
    attn_core(e_qe, e_qo, e_k, e_v, bias_e, e_p, e_i, e_c)
    io.send(vecs, b_enc, b_dec, e_n, e_qe, e_qo, e_k, e_v, e_p, e_i, e_c)
    attn_output(e_c, we.at[3], enc(4), source, e_mid)
    layer_norm(e_mid, enc(5), enc(6), e_n2)
    io.send(e_mid, e_n2)
    arrived(wi, sem.at[1])
    arrived(wo, sem.at[2])
    feed_forward(e_n2, wi, b_enc, Wide(wo), enc(7), e_mid, buf)
    memory[...] = buf[...].astype(BF16)


def first_kernel(
    io, table, s_len, t_len, langs, vecs, target, memory, cot, b_dec,
    a0, a1, a2, a3, b0, b1, b2, b3,
    dec_out, d_p, d_q, d_other, g_start, g_memory, g_vec, g_bias,
    s_n, s_qe, s_qo, s_k, s_v, s_p, s_i, s_c, c_n, c_qe, c_qo, c_k, c_v, c_p, c_i, c_c,
    ws, wc, vi, vo, bias_s, bias_c, buf, start, first, second, n3,
    act, dh, d_in, g_first, acc, u_t, m_t, low,
    d_even, d_odd, dc_t, q_t, c_t, dq, dk_t, dv_t, dk, dv, du, dm, sem,
):
    io.bring(vecs, target)
    load(table, TAB_A, (a0, a1, a2, a3), ((0, 4, ws, 0, sem.at[0]),))
    masks(s_len, t_len, bias_s, bias_c)
    onehot = lang_onehot(t_len, langs)
    io.need(vecs, target)
    io.bring(memory, cot, b_dec)
    load(table, TAB_B, (b0, b1, b2, b3), ((0, 4, wc, 0, sem.at[1]), (4, 4, vi, 0, sem.at[2])))
    load(table, TAB_A, (a0, a1, a2, a3), ((4, 4, vo, 0, sem.at[3]),))

    def dec(index):
        return vecs[DEC_VEC + index : DEC_VEC + index + 1, :]

    start[...] = target[...].astype(F32) + dot(onehot, vecs[...].astype(BF16))
    layer_norm(start, dec(0), dec(1), s_n)
    arrived(ws, sem.at[0])
    attn_project(s_n, s_n, ws, dec(2), dec(3), s_qe, s_qo, s_k, s_v)
    attn_core(s_qe, s_qo, s_k, s_v, bias_s, s_p, s_i, s_c)
    attn_output(s_c, ws.at[3], dec(4), start, first)
    layer_norm(first, dec(5), dec(6), c_n)
    io.need(memory, cot, b_dec)
    arrived(wc, sem.at[1])
    attn_project(c_n, memory, wc, dec(7), dec(8), c_qe, c_qo, c_k, c_v)
    attn_core(c_qe, c_qo, c_k, c_v, bias_c, c_p, c_i, c_c)
    attn_output(c_c, wc.at[3], dec(9), first, second)
    layer_norm(second, dec(10), dec(11), n3)
    u_t[...] = n3[...].T
    buf[...] = second[...] + dec(12)
    arrived(vi, sem.at[2])
    arrived(vo, sem.at[3])

    def in_p(unit):
        return place_of(d_p, d_other, unit, 0, table, TAB_A)

    def in_q(unit):
        return place_of(d_q, d_other, unit, 8, table, TAB_B)

    feed_both(
        n3, u_t, vi, b_dec, Wide(vo), cot, act, dh, buf, d_in, acc,
        [in_p(k) for k in range(4)], place_of(d_q, d_other, 4, 8, table, SLOT_B), g_bias,
    )
    dec_out[...] = buf[...].astype(BF16)
    io.send(dec_out, g_bias)
    io.send_units(d_other, 0, 4)
    io.send_units(d_other, 12, 16)
    io.send_units(d_q, 4, 8)
    g_second = second
    gain_three = norm_back(second, dec(10), d_in, cot, g_second)
    scratch = (d_even, d_odd, dc_t, q_t, c_t, dq, dk_t, dv_t, dk, dv, du, dm)
    u_t[...] = c_n[...].T
    m_t[...] = memory[...].T
    low[...] = g_second[...].astype(BF16)
    bias_two = attn_back(
        low, u_t, m_t, wc, (c_qe, c_qo, c_k, c_v, c_p, c_i, c_c), scratch, acc,
        [in_p(4 + k) for k in range(4)],
    )
    io.send(d_p)
    io.send_units(d_other, 4, 8)
    g_memory[...] = dm[...]
    io.send(g_memory)
    gain_two = norm_back(first, dec(5), du, g_second, g_first)
    low[...] = g_first[...].astype(BF16)
    u_t[...] = s_n[...].T
    bias_one = attn_back(
        low, u_t, u_t, ws, (s_qe, s_qo, s_k, s_v, s_p, s_i, s_c), scratch, acc,
        [in_q(k) for k in range(4)],
    )
    io.send_units(d_other, 8, 12)
    io.send_units(d_q, 0, 4)
    du[...] = du[...] + dm[...]
    gain_one = norm_back(start, dec(0), du, g_first, g_start)
    io.send(g_start)
    g_vec[...] = lax.dot_general(
        onehot, g_start[...].astype(BF16), (((0,), (0,)), ((), ())), preferred_element_type=F32
    )
    values = gain_one + bias_one + gain_two + bias_two + gain_three + (column_sum(cot),)
    for i, value in enumerate(values):
        g_vec[DEC_VEC + i : DEC_VEC + i + 1, :] = value


def second_kernel(
    io, table, g_memory, e_n2, b_enc, vecs, e_mid, e_n, e_qe, e_qo, e_k, e_v, e_p, e_i, e_c,
    source, g_vec, g_bias_dec, a0, a1, a2, a3, b0, b1, b2, b3,
    d_p, d_q, d_other, g_source,
    we, wi, wo, buf, low, acc, u_t, act, dh, d_in, g_mid, b_grad, all_vec, turned,
    d_even, d_odd, dc_t, q_t, c_t, dq, dk_t, dv_t, dk, dv, du, dm, sem,
):
    io.bring(g_memory, e_n2, b_enc)
    load(table, TAB_A, (a0, a1, a2, a3), ((4, 2, wi, 0, sem.at[0]),))
    load(table, TAB_B, (b0, b1, b2, b3), ((0, 2, wi, 2, sem.at[0]), (2, 4, wo, 0, sem.at[1])))
    io.need(g_memory, e_n2, b_enc)
    u_t[...] = e_n2[...].T
    low[...] = g_memory[...].astype(BF16)
    bias_out = column_sum(low)
    arrived(wi, sem.at[0])
    arrived(wo, sem.at[1])
    io.bring(vecs, e_mid, e_n)
    load(table, TAB_A, (a0, a1, a2, a3), ((0, 4, we, 0, sem.at[2]),))
    io.bring(e_i, e_qe, e_qo, e_c, e_v, e_k, e_p, source, g_vec, g_bias_dec)

    def in_p(unit):
        return place_of(d_p, d_other, unit, 0, table, TAB_A)

    def in_q(unit):
        return place_of(d_q, d_other, unit, 7, table, TAB_B)

    feed_both(
        e_n2, u_t, wi, b_enc, Wide(wo), low, act, dh, None, d_in, acc,
        [in_p(k) for k in range(4)], place_of(d_q, d_other, 0, 7, table, SLOT_B), b_grad,
    )
    io.send_units(d_p, 0, 4)
    io.send_units(d_other, 0, 4)
    io.send_units(d_other, 7, 11)
    io.need(vecs, e_mid, e_n)
    gain_two = norm_back(e_mid, vecs[ENC_VEC + 5 : ENC_VEC + 6, :], d_in, g_memory, g_mid)
    low[...] = g_mid[...].astype(BF16)
    u_t[...] = e_n[...].T
    io.need(e_i, e_qe, e_qo, e_c, e_v, e_k, e_p)
    arrived(we, sem.at[2])
    scratch = (d_even, d_odd, dc_t, q_t, c_t, dq, dk_t, dv_t, dk, dv, du, dm)
    bias_one = attn_back(
        low, u_t, u_t, we, (e_qe, e_qo, e_k, e_v, e_p, e_i, e_c), scratch, acc,
        [in_p(4), in_p(5), in_q(4), in_q(5)],
    )
    io.send(d_q)
    io.send_units(d_p, 4, 6)
    io.send_units(d_other, 4, 6)
    io.send_units(d_other, 11, 13)
    du[...] = du[...] + dm[...]
    io.need(source, g_vec, g_bias_dec)
    buf[...] = source[...].astype(F32)
    gain_one = norm_back(buf, vecs[ENC_VEC : ENC_VEC + 1, :], du, g_mid, g_source)
    io.send(g_source)
    all_vec[...] = g_vec[...]
    for i, value in enumerate(gain_one + bias_one + gain_two + (bias_out,)):
        all_vec[ENC_VEC + i : ENC_VEC + i + 1, :] = value
    turned[:, 0:128] = all_vec[...].T
    for block in range(BLOCKS):
        tile = rows(block // 2, 128)
        turned[rows(block, 16), 128:256] = jnp.broadcast_to(b_grad[:, tile], (16, 128))
        turned[rows(block, 16), 256:384] = jnp.broadcast_to(g_bias_dec[:, tile], (16, 128))
        turned[rows(block, 16), 384:512] = jnp.zeros((16, 128), F32)
    put_blocks(turned, in_p(6))
    io.send_units(d_p, 6, 7)
    io.send_units(d_other, 6, 7)


VM = pl.BlockSpec(memory_space=pltpu.VMEM)
SM = pl.BlockSpec(memory_space=pltpu.SMEM)
HB = pl.BlockSpec(memory_space=pl.ANY)
IN = object()
SPARE = 8


def units_of(count):
    return ((16, count, 16, D), BF16)


def act_shape(dtype=BF16):
    return ((SEQ, D), dtype)


KEPT = [act_shape()] * 5 + [((HEADS, SEQ, SEQ), BF16), act_shape(F32), act_shape()]


def call(body, args, specs, outs, scratch, flops):
    brought = [k for k, spec in enumerate(specs) if spec is IN]

    def kernel(*refs):
        refs = list(refs)
        ins, refs = refs[: len(args)], refs[len(args) :]
        targets, refs = refs[: len(outs)], refs[len(outs) :]
        staged_in, refs = refs[: len(brought)], refs[len(brought) :]
        staged_out, refs = refs[: len(outs)], refs[len(outs) :]
        sem, refs = refs[0], refs[1:]
        pairs_in = []
        for k, ref in zip(brought, staged_in):
            pairs_in.append((ins[k], ref))
            ins[k] = ref
        copies = Copies(pairs_in, list(zip(targets, staged_out)), sem)
        body(copies, *ins, *staged_out, *refs)
        copies.finish()

    buffers = [pltpu.VMEM(args[k].shape, args[k].dtype) for k in brought]
    buffers += [pltpu.VMEM(*out) for out in outs]
    buffers += [pltpu.SemaphoreType.DMA((len(brought) + len(outs) + SPARE,))]
    buffers += [
        pltpu.VMEM(*s) if isinstance(s, tuple) else pltpu.SemaphoreType.DMA((s,)) for s in scratch
    ]
    return pl.pallas_call(
        kernel,
        in_specs=[HB if spec is IN else spec for spec in specs],
        out_specs=[HB] * len(outs),
        out_shape=[jax.ShapeDtypeStruct(s, t) for s, t in outs],
        scratch_shapes=buffers,
        compiler_params=pltpu.CompilerParams(vmem_limit_bytes=63 << 20),
        cost_estimate=pl.CostEstimate(flops=flops, bytes_accessed=flops >> 9, transcendentals=0),
    )(*args)


def plain_call(body, args, outs, scratch):
    return pl.pallas_call(
        body,
        in_specs=[SM] + [VM] * (len(args) - 1),
        out_specs=[VM] * len(outs),
        out_shape=[jax.ShapeDtypeStruct(s, t) for s, t in outs],
        scratch_shapes=[pltpu.VMEM(*s) for s in scratch],
        cost_estimate=pl.CostEstimate(flops=1 << 20, bytes_accessed=1 << 18, transcendentals=0),
    )(*args)


SQUARE = ((4, D, D), BF16)
TALL = ((BLOCKS, 4, 16, D), BF16)
ACC = ((D, D), BF16)
TURN = ((D, SEQ), BF16)
BIAS = ((SEQ, SEQ), F32)
BACK = [act_shape()] * 2 + [TURN] * 3 + [act_shape(), TURN, TURN, act_shape(), act_shape()]
BACK = BACK + [act_shape(F32)] * 2


def pairs(axis, step):
    k = AXES.index(axis)
    found = []

    def flat(place):
        index = 0
        for at, size in zip(place, SIZES):
            index = index * size + at
        return index

    for place in itertools.product(*[range(size) for size in SIZES]):
        if axis == "c":
            other = 1
        elif axis == "z":
            other = step
        else:
            other = 1 if (step == 0) == (place[1] == 0) else 3
        target = list(place)
        target[k] = place[k] ^ other
        found.append((flat(place), flat(target)))
    return found


def swap(values, axis, step=0):
    return lax.ppermute(values, AXES, pairs(axis, step))


def away(core, order):
    hop = 1 if core == 0 else 3
    return (0, hop, 4 - hop, 2)[order]


def tables():
    found = []
    for x, c, y, z in itertools.product(*[range(size) for size in SIZES]):
        row_a, row_b = [], []
        for j in range(2):
            core = c ^ j
            for slot in range(16):
                one, two = away(core, slot % 4), away(core, slot // 4)
                row_a.append((x ^ one) * 8 + core * 4 + (y ^ two))
                row_b.append((x ^ two) * 8 + core * 4 + (y ^ one))
        found.append(row_a + row_b + list(np.argsort(row_a)) + list(np.argsort(row_b)) + [c])
    return np.array(found, np.int32)


def step_all(parts):
    received = [swap(*part) for part in parts]
    return lax.optimization_barrier(tuple(received))


def join(values, received):
    return jnp.concatenate([values, received], axis=0)


def by_z(arrived):
    me = lax.axis_index("z")
    found = []
    for z in range(4):
        distance = me ^ z
        part = arrived[3]
        for k in range(3):
            part = jnp.where(distance == k, arrived[k], part)
        found.append(part)
    narrow = jnp.stack([part[:84].reshape(21, 4, D) for part in found], axis=1).reshape(21 * 16, D)
    enc = [part[96:112] for part in found]
    dec = [part[112:] for part in found]
    return (
        jnp.concatenate([narrow[:112], narrow[144:208], *dec]),
        jnp.concatenate([narrow[112:144], *enc, narrow[208:]]),
    )


def parted(values, received, units, cut):
    values = values.reshape(2, units * 16, D)
    received = received.reshape(2, units * 16, D)
    return [
        jnp.concatenate([values[:, part], received[:, part]]).reshape(-1, D)
        for part in (slice(0, cut * 16), slice(cut * 16, None))
    ]


def gather(table, packed):
    table, *others = lax.optimization_barrier(
        (table, *[swap(packed, "z", distance) for distance in (1, 2, 3)])
    )
    one, two = by_z([packed, *others])
    got = step_all([(one, "x", 0), (two, "y", 0)])
    one, two = join(one, got[0]), join(two, got[1])
    got = step_all([(one, "x", 1), (two, "y", 1)])
    one_enc, one_dec = parted(one, got[0], 15, 7)
    two_enc, two_dec = parted(two, got[1], 14, 6)
    got = step_all([(one_enc, "y", 0), (two_enc, "x", 0)])
    got_dec = swap(one_dec, "y", 0), swap(two_dec, "x", 0)
    one_enc, two_enc = join(one_enc, got[0]), join(two_enc, got[1])
    one_dec, two_dec = join(one_dec, got_dec[0]), join(two_dec, got_dec[1])
    enc = [swap(one_enc, "y", 1), swap(two_enc, "x", 1), swap(one_enc, "c"), swap(two_enc, "c")]
    *enc, one_dec, two_dec = lax.optimization_barrier((*enc, one_dec, two_dec))
    dec = swap(one_dec, "y", 1), swap(two_dec, "x", 1), swap(one_dec, "c"), swap(two_dec, "c")
    return table, pieces_of((one_enc, two_enc), enc, (7, 6)), (one_dec, two_dec), dec


def pieces_of(low, got, units):
    found = []
    for k in range(2):
        for piece in (low[k], got[k], got[2 + k], swap(got[k], "c")):
            found.append(piece.reshape(8, units[k], 16, D))
    return found


def add(left, right):
    return left + right


def fold(values, received):
    half = values.shape[0] // 2
    return add(values[:half], received[:half]), add(values[half:], received[half:])


def beside(left, right):
    return jnp.concatenate([left, right], axis=1)


def z_parts(values, wides):
    me = lax.axis_index("z")
    parts = values.reshape(-1, 4, 4, D)
    found = []
    for distance in range(4):
        want = me ^ distance
        picked = parts[:, 3]
        tall = [parts[wide + 3] for wide in wides]
        for z in range(3):
            picked = jnp.where(want == z, parts[:, z], picked)
            tall = [jnp.where(want == z, parts[w + z], t) for w, t in zip(wides, tall)]
        if wides:
            picked = jnp.concatenate([picked[: wides[0]], *tall, picked[wides[-1] + 4 :]])
        found.append(picked)
    return found


def per_device(
    source, target, source_lengths, target_lengths, lang_ids, out_cotangent,
    enc_attn, enc_vectors, enc_w_in, enc_b_in, enc_w_out,
    dec_self, dec_cross, dec_vectors, dec_w_in, dec_b_in, dec_w_out, lang_table,
):
    spot = (lax.axis_index("z") + 4 * (lax.axis_index("y") % 2)).reshape(1)
    (packed,) = plain_call(
        pack_kernel,
        (
            spot, enc_attn, enc_w_in, enc_w_out, dec_self, dec_cross, dec_w_in, dec_w_out,
            enc_vectors.T, dec_vectors.T, lang_table.T, enc_b_in.reshape(1, 16), dec_b_in.reshape(1, 16),
        ),
        [((128, D), BF16)],
        [((8, 128), F32), ((128, D), F32)],
    )
    me = lax.axis_index(AXES)
    table = lax.dynamic_index_in_dim(jnp.asarray(tables()), me, 0, keepdims=False)
    table, g_enc, low_dec, got_dec = gather(table, packed)
    vecs, b_enc, b_dec, *kept, e_mid, e_n2, memory = call(
        encoder_kernel,
        (table, source_lengths, source[0], *g_enc),
        [SM] * 2 + [IN] + [HB] * 8,
        [((128, D), F32), ((1, FF), F32), ((1, FF), F32)]
        + KEPT
        + [act_shape(F32), act_shape(), act_shape()],
        [((1, D, D), BF16), SQUARE, SQUARE, TALL, BIAS, act_shape(F32), 4],
        1 << 12,
    )
    memory, *got_dec = lax.optimization_barrier((memory, *got_dec))
    g_dec = pieces_of(low_dec, got_dec, (8, 8))
    dec_out, p_dec, q_dec, other, g_start, g_memory, g_vec, g_bias_dec = call(
        first_kernel,
        (
            table, source_lengths, target_lengths, lang_ids, vecs,
            target[0], memory, out_cotangent[0], b_dec, *g_dec,
        ),
        [SM] * 4 + [IN] * 5 + [HB] * 8,
        [act_shape(), units_of(8), units_of(8), units_of(16)]
        + [act_shape(F32), act_shape(F32), ((128, D), F32), ((1, FF), F32)],
        KEPT
        + KEPT
        + [SQUARE, SQUARE, SQUARE, TALL, BIAS, BIAS]
        + [act_shape(F32)] * 4
        + [act_shape()] * 3
        + [act_shape(F32)] * 2
        + [ACC, TURN, TURN, act_shape()]
        + BACK
        + [4],
        15 * 10**9,
    )
    got = swap(other, "c")
    p_enc, q_enc, other, g_source = call(
        second_kernel,
        (
            table, g_memory, e_n2, b_enc, vecs, e_mid, *kept, source[0], g_vec, g_bias_dec, *g_enc,
        ),
        [SM] + [IN] * 16 + [HB] * 8,
        [units_of(7), units_of(6), units_of(13), act_shape(F32)],
        [SQUARE, SQUARE, TALL, act_shape(F32), act_shape(), ACC, TURN, act_shape(), act_shape()]
        + [act_shape(F32), act_shape(F32), ((1, FF), F32), ((128, D), F32), ((D, D), F32)]
        + BACK
        + [3],
        8 * 10**9,
    )
    other, got = lax.optimization_barrier((other, got))
    again = swap(other, "c")
    p_low, p_high = fold(p_dec, got[:, :8])
    q_low, q_high = fold(q_dec, got[:, 8:])
    p_got, q_got = swap(p_high, "y", 1), swap(q_high, "x", 1)
    one_low, one_high = fold(p_enc, again[:, :7])
    two_low, two_high = fold(q_enc, again[:, 7:])
    p_got, q_got, one_got, two_got = lax.optimization_barrier(
        (p_got, q_got, swap(one_high, "y", 1), swap(two_high, "x", 1))
    )
    p_low, p_high = map(beside, fold(p_low, p_got), fold(one_low, one_got))
    q_low, q_high = map(beside, fold(q_low, q_got), fold(two_low, two_got))
    for axes, step in ((("y", "x"), 0), (("x", "y"), 1)):
        p_got, q_got = step_all([(p_high, axes[0], step), (q_high, axes[1], step)])
        p_low, p_high = fold(p_low, p_got)
        q_low, q_high = fold(q_low, q_got)
    p_got, q_got = step_all([(p_high, "x", 0), (q_high, "y", 0)])
    p_parts = z_parts(add(p_low, p_got)[0], ())
    q_parts = z_parts(add(q_low, q_got)[0], (4, 8))
    mine, *others = map(lambda *part: jnp.concatenate(part), p_parts, q_parts)
    got = [swap(part, "z", k + 1) for k, part in enumerate(others)]
    quarter, four = ((4, FF), F32), ((4, 4, D), F32)
    (
        d_attn, d_vec_e, d_w_in, d_b_e, d_w_out, d_self, d_cross, d_vec_d, d_dec_in, d_b_d, d_dec_out, d_lang,
    ) = plain_call(
        unpack_kernel,
        (spot, mine, *got),
        [four, ((4, 8), F32), quarter, ((1, 16), F32), ((16, D), F32), four, four]
        + [((4, 13), F32), quarter, ((1, 16), F32), ((16, D), F32), ((4, LANGS), F32)],
        [((4, D), F32)],
    )
    return (
        dec_out[None],
        g_source[None],
        g_start[None],
        d_attn,
        d_vec_e.T,
        d_w_in,
        d_b_e.reshape(16),
        d_w_out,
        d_self,
        d_cross,
        d_vec_d.T,
        d_dec_in,
        d_b_d.reshape(16),
        d_dec_out,
        d_lang.T,
    )


def solution(mesh):
    fine = Mesh(mesh.devices.reshape(SIZES), AXES)
    flat = AXES
    in_specs = (
        P(flat, None, None),
        P(flat, None, None),
        P(flat, None),
        P(flat, None),
        P(flat, None),
        P(flat, None, None),
        P(None, flat, None),
        P(None, flat),
        P(flat, None),
        P(flat),
        P(flat, None),
        P(None, flat, None),
        P(None, flat, None),
        P(None, flat),
        P(flat, None),
        P(flat),
        P(flat, None),
        P(None, flat),
    )
    out_specs = (
        P(flat, None, None),
        P(flat, None, None),
        P(flat, None, None),
        P(None, flat, None),
        P(None, flat),
        P(flat, None),
        P(flat),
        P(flat, None),
        P(None, flat, None),
        P(None, flat, None),
        P(None, flat),
        P(flat, None),
        P(flat),
        P(flat, None),
        P(None, flat),
    )
    return jax.shard_map(
        per_device, mesh=fine, in_specs=in_specs, out_specs=out_specs, check_vma=False
    )
```
